32 devices in a mesh: fsdp: 4 (over y, x), tp: 2 (over core), ad: 4 (over z).
Axes of the slice: x: 2, y: 2, z: 4, core: 2. Of those that a mesh axis runs over, the one named last changes fastest.
Arguments:
- input_rows: bfloat16 [4096, 8192], P(('fsdp', 'ad')), may hold values from -6 to 6
- value_weight_frozen: bfloat16 [8192, 1024], P('fsdp', 'tp'), may hold values from -0.0625 to 0.0625
- adapter_down_weight: bfloat16 [32, 256, 8192], P('ad', None, 'tp'), may hold values from -0.0625 to 0.0625
- adapter_up_weight: bfloat16 [32, 256, 1024], P('ad', None, 'tp'), may hold values from -0.375 to 0.375
- layer_output_gradient: bfloat16 [4096, 1024], P(('fsdp', 'ad'), 'tp'), may hold values from -0.5 to 0.5
- domain: int32 [4096, 1], P(('fsdp', 'ad')), may hold values from 0 to 31; in each aligned block of 256 rows (0 to 255, 256 to 511, ...) at most 12 rows name the same one
Outputs:
- y_out: bfloat16 [4096, 1024], P(('fsdp', 'ad'), 'tp')
- grad_a: float32 [32, 256, 8192], P('ad', 'fsdp', 'tp')
- grad_b: float32 [32, 256, 1024], P('ad', 'fsdp', 'tp')
The draws below stay inside these ranges and needn't reach their ends.
Inputs may be any that keep to these rules, and one draw needn't show every extreme that they name: In each aligned block of 256 rows (the tokens of one fsdp and ad index) no domain is named by more than 12 tokens, a bound that some block reaches.
All inputs are finite; a program needn't handle non-finite values.
Results may differ from the reference program's by a relative error of at most 0.004.
Values may be sent and summed in bfloat16 or wider, within the bound.
No kernel may reach another device: no remote copies, remote signals or barrier semaphores. Data moves between devices by JAX's collectives and lax.ppermute only.
A program may use at most 128 MiB of HBM per device.

```python
import math
import jax
import jax.numpy as jnp
import numpy as np
from jax import lax

MODEL_WIDTH = 8192
VALUE_WIDTH = 1024
ADAPTER_RANK = 256
DOMAIN_COUNT = 32
TOK_GRP = 256
CAPD = 12
FSDP_ROWS = 1024
TOKENS = 4096
N_FSDP = 4
N_AD = 4


def levels(stream_key, shape, cuts, smallest, top_value):
    loudness, own = 1.0, jax.random.fold_in(stream_key, 6)
    for dim, blocks in cuts:
        steps = jnp.exp(jax.random.uniform(jax.random.fold_in(own, dim), (blocks,), jnp.float32, smallest / len(cuts), top_value / len(cuts)))
        loudness = loudness * jnp.repeat(steps, shape[dim] // blocks).reshape([-1 if axis == dim else 1 for axis in range(len(shape))])
    return loudness


def shared_out(rng, own, number, rows, count, top, bound, skew):
    order = jax.random.permutation(rng, count)
    packed, usual = load_shares(count, rows * top, bound, skew, True), load_shares(count, rows * top, bound, skew, False)
    places = jnp.arange(count)

    def named(lengths, turn):
        used = int((lengths > 0).sum())
        fixed = max(1, used // 4)
        moved = fixed + (places - fixed + turn * (used - fixed)) % max(1, count - fixed)
        return jnp.zeros((count,), jnp.int32).at[order[jnp.where(places < fixed, places, moved)]].set(jnp.asarray(lengths, jnp.int32))

    lengths = jnp.where(number % 4 == 0, named(packed, number // 4), named(usual, number - number // 4 - 1))
    mixed = jax.random.permutation(jax.random.fold_in(own, 3), count)
    giver, receiver = mixed[0:count // 2 * 2:2], mixed[1:count // 2 * 2:2]
    room = jnp.minimum(lengths[giver] - 1, bound - lengths[receiver]) // 2
    room = jnp.where((giver == order[0]) | (receiver == order[0]) | (lengths[receiver] == 0), 0, jnp.maximum(room, 0))
    moved = jax.random.randint(jax.random.fold_in(own, 4), (count // 2,), 0, 1 << 20) % (room + 1)
    lengths = lengths.at[giver].add(-moved).at[receiver].add(moved)
    labels = jnp.searchsorted(jnp.cumsum(lengths), jnp.arange(rows * top), side="right").astype(jnp.int32)
    grid = labels.reshape(top, rows).T
    grid = grid[jax.random.permutation(jax.random.fold_in(own, 1), rows)]
    turn = jax.random.randint(jax.random.fold_in(own, 2), (rows, 1), 0, top)
    return jnp.take_along_axis(grid, (jnp.arange(top)[None, :] + turn) % top, axis=1)


def load_shares(count, total, reach, skew, full):
    loads = [(1 << 20) // math.isqrt(standing ** skew) + 1 for standing in range(1, count + 1)]
    largest = reach if full else min(reach, max(-(-total // count), total * loads[0] // sum(loads)))
    least = 1 if total - largest >= count - 1 else 0
    counts, surplus = [largest] + [least] * (count - 1), total - largest - least * (count - 1)
    while surplus > 0:
        candidates = [i for i in range(1, count) if counts[i] < largest] or [i for i in range(1, count) if counts[i] < reach]
        whole, left = sum([loads[i] for i in candidates]), surplus
        for i in candidates:
            more = min(reach - counts[i], max(1, left * loads[i] // whole), surplus)
            counts[i] = counts[i] + more
            surplus = surplus - more
    return np.array(counts)


def bell_draw(key, dims, width, most, cuts=(), kind=jnp.bfloat16):
    result = width * jax.random.normal(key, dims, jnp.float32)
    if cuts:
        result = result * levels(key, dims, cuts, -0.22, 0.18)
    return jnp.clip(result, -most, most).astype(kind)


def setup_inputs(seed: int = 0) -> dict:
    seeds = jax.random.split(jax.random.key(seed), 7)
    input_rows = bell_draw(seeds[0], (TOKENS, MODEL_WIDTH), 1.0, 6.0, ((0, 16),))
    value_weight_frozen = bell_draw(seeds[1], (MODEL_WIDTH, VALUE_WIDTH), MODEL_WIDTH ** -0.5, 0.0625, ((0, 4), (1, 2)))
    adapter_down_weight = bell_draw(seeds[2], (DOMAIN_COUNT, ADAPTER_RANK, MODEL_WIDTH), MODEL_WIDTH ** -0.5, 0.0625, ((0, 4), (2, 2)))
    adapter_up_weight = bell_draw(seeds[3], (DOMAIN_COUNT, ADAPTER_RANK, VALUE_WIDTH), ADAPTER_RANK ** -0.5, 0.375, ((0, 4), (2, 2)))
    layer_output_gradient = bell_draw(seeds[4], (TOKENS, VALUE_WIDTH), 0.0625, 0.5, ((0, 16), (1, 2)))
    domain_keys = jax.random.split(jax.random.fold_in(seeds[5], 1), TOKENS // TOK_GRP)
    domain_turns = jax.random.permutation(jax.random.fold_in(seeds[5], 3), TOKENS // TOK_GRP)
    domain = jax.vmap(lambda own, number: shared_out(jax.random.fold_in(seeds[5], 2), own, number, TOK_GRP, DOMAIN_COUNT, 1, CAPD, 2))(domain_keys, domain_turns).reshape((TOKENS, 1))
    return dict(input_rows=input_rows, value_weight_frozen=value_weight_frozen, adapter_down_weight=adapter_down_weight, adapter_up_weight=adapter_up_weight, layer_output_gradient=layer_output_gradient, domain=domain)


adapter_scale = 0.5


def reference(input_rows, value_weight_frozen, adapter_down_weight, adapter_up_weight, layer_output_gradient, domain):
    slot_count = N_AD * CAPD
    down_weight_full = adapter_down_weight.astype(jnp.float32)
    up_weight_full = adapter_up_weight.astype(jnp.float32)
    x_blocks = input_rows.reshape(N_FSDP, FSDP_ROWS, MODEL_WIDTH)
    dy_blocks = layer_output_gradient.reshape(N_FSDP, FSDP_ROWS, VALUE_WIDTH)
    dom_blocks = domain[:, 0].reshape(N_FSDP, FSDP_ROWS)

    def step(carry, item):
        x_part, dy_part, dom_part = item
        onehot = (dom_part[:, None] == jnp.arange(DOMAIN_COUNT, dtype=jnp.int32)[None, :]).astype(jnp.int32)
        before = jnp.cumsum(onehot, axis=0) - onehot
        position = jnp.sum(before * onehot, axis=1).astype(jnp.int32)
        place = (dom_part * slot_count + position).astype(jnp.int32)
        x_buf = jnp.zeros((DOMAIN_COUNT * slot_count, MODEL_WIDTH), jnp.float32).at[place].set(x_part.astype(jnp.float32))
        x_buf = x_buf.reshape(DOMAIN_COUNT, slot_count, MODEL_WIDTH)
        output_gradient_buffer = jnp.zeros((DOMAIN_COUNT * slot_count, VALUE_WIDTH), jnp.float32).at[place].set(dy_part.astype(jnp.float32))
        output_gradient_buffer = output_gradient_buffer.reshape(DOMAIN_COUNT, slot_count, VALUE_WIDTH)
        hidden_state = jnp.einsum('dsx,drx->dsr', x_buf, down_weight_full).astype(jnp.bfloat16)
        hidden_state = lax.optimization_barrier(hidden_state).astype(jnp.float32)
        input_gradient = (adapter_scale * jnp.einsum('cmn,cln->cml', output_gradient_buffer, up_weight_full)).astype(jnp.bfloat16)
        input_gradient = lax.optimization_barrier(input_gradient).astype(jnp.float32)
        adapter_update = (adapter_scale * jnp.einsum('txl,tlz->txz', hidden_state, up_weight_full)).astype(jnp.bfloat16)
        part_a = jnp.einsum('dsr,dsx->drx', input_gradient, x_buf)
        up_weight_partial = adapter_scale * jnp.einsum('noi,noh->nih', hidden_state, output_gradient_buffer)
        base = jnp.dot(x_part, value_weight_frozen, preferred_element_type=jnp.float32)
        adapted = adapter_update.reshape(DOMAIN_COUNT * slot_count, VALUE_WIDTH)[place].astype(jnp.float32)
        output = (base + adapted).astype(jnp.bfloat16)
        return (carry[0] + part_a, carry[1] + up_weight_partial), output

    start = (jnp.zeros((DOMAIN_COUNT, ADAPTER_RANK, MODEL_WIDTH), jnp.float32), jnp.zeros((DOMAIN_COUNT, ADAPTER_RANK, VALUE_WIDTH), jnp.float32))
    (grad_a, grad_b), outputs = lax.scan(step, start, (x_blocks, dy_blocks, dom_blocks))
    return outputs.reshape(TOKENS, VALUE_WIDTH), grad_a, grad_b
```

```python
import jax
import jax.numpy as jnp
from jax import lax
from jax.sharding import PartitionSpec as P

CAPD = 12
GROUP = 4
CHUNKS = 2

adapter_scale = 0.5


def slot_places(dom_ids, dom_total):
    row_count = dom_ids.shape[0]
    onehot = (dom_ids[:, None] == jnp.arange(dom_total, dtype=jnp.int32)[None, :]).astype(
        jnp.float32
    )
    row_iota = jnp.arange(row_count, dtype=jnp.int32)
    earlier = (row_iota[:, None] > row_iota[None, :]).astype(jnp.float32)
    prior = jnp.dot(earlier, onehot, preferred_element_type=jnp.float32)
    position = jnp.sum(prior * onehot, axis=1).astype(jnp.int32)
    return dom_ids * CAPD + position


def general_body(
    input_rows,
    value_weight_frozen,
    adapter_down_weight,
    adapter_up_weight,
    layer_output_gradient,
    domain,
):
    row_count = input_rows.shape[0]
    domain_local = adapter_down_weight.shape[0]
    width_local = adapter_down_weight.shape[2]
    value_width_local = adapter_up_weight.shape[2]
    ad_count = lax.axis_size("ad")
    slot_total = ad_count * domain_local * CAPD
    place = slot_places(domain[:, 0], ad_count * domain_local)
    row_iota = jnp.arange(row_count, dtype=jnp.int32)
    matches = place[None, :] == jnp.arange(slot_total, dtype=jnp.int32)[:, None]
    filled = jnp.any(matches, axis=1)
    source_row = jnp.sum(jnp.where(matches, row_iota[None, :], 0), axis=1)
    base = jnp.dot(
        input_rows,
        lax.all_gather(value_weight_frozen, "fsdp", axis=0, tiled=True),
        preferred_element_type=jnp.float32,
    )
    feature_cols = lax.dynamic_slice_in_dim(
        input_rows, lax.axis_index("tp") * width_local, width_local, 1
    )
    zero_value = jnp.zeros((), jnp.bfloat16)
    send_x = jnp.where(filled[:, None], feature_cols[source_row], zero_value)
    send_dy = jnp.where(filled[:, None], layer_output_gradient[source_row], zero_value)
    send_x = send_x.reshape(ad_count, domain_local * CAPD, width_local)
    send_dy = send_dy.reshape(ad_count, domain_local * CAPD, value_width_local)
    got_x = lax.all_to_all(send_x, "ad", split_axis=0, concat_axis=0, tiled=True)
    got_dy = lax.all_to_all(send_dy, "ad", split_axis=0, concat_axis=0, tiled=True)
    rows = got_x.reshape(ad_count, domain_local, CAPD, width_local)
    grads = got_dy.reshape(ad_count, domain_local, CAPD, value_width_local)
    f32 = dict(preferred_element_type=jnp.float32)
    hidden, back = lax.psum(
        (
            jnp.einsum("vqfj,qwj->vqfw", rows, adapter_down_weight, **f32),
            jnp.einsum("amgy,mzy->amgz", grads, adapter_up_weight, **f32),
        ),
        "tp",
    )
    hidden = hidden.astype(jnp.bfloat16)
    back = (adapter_scale * back).astype(jnp.bfloat16)
    delta = adapter_scale * jnp.einsum("lokh,ohi->loki", hidden, adapter_up_weight, **f32)
    delta = delta.astype(jnp.bfloat16).reshape(ad_count, domain_local * CAPD, value_width_local)
    part_a = jnp.einsum("sdcr,sdcx->drx", back, rows, **f32)
    part_b = adapter_scale * jnp.einsum("sdcr,sdce->dre", hidden, grads, **f32)
    returned = lax.all_to_all(delta, "ad", split_axis=0, concat_axis=0, tiled=True)
    returned = returned.reshape(slot_total, value_width_local)
    y_out = (base + returned[place].astype(jnp.float32)).astype(jnp.bfloat16)
    return (
        y_out,
        lax.psum_scatter(part_a, "fsdp", scatter_dimension=1, tiled=True),
        lax.psum_scatter(part_b, "fsdp", scatter_dimension=1, tiled=True),
    )


def column_body(
    input_rows,
    value_weight_frozen,
    adapter_down_weight,
    adapter_up_weight,
    layer_output_gradient,
    domain,
):
    f32 = dict(preferred_element_type=jnp.float32)
    bf16 = jnp.bfloat16
    fsdp, ad = lax.axis_size("fsdp"), lax.axis_size("ad")
    f, t, a = lax.axis_index("fsdp"), lax.axis_index("tp"), lax.axis_index("ad")
    fy, fx = f // 2, f % 2
    rows, width = input_rows.shape
    dloc, rank, half = adapter_down_weight.shape
    vloc = adapter_up_weight.shape[2]
    rloc = rank // fsdp
    kf_width = width // fsdp
    kt = kf_width // 2
    cw = kt // CHUNKS
    slots = dloc * CAPD
    ngroup = dloc // GROUP
    gslots = GROUP * CAPD

    def over_f(v, k):
        return lax.ppermute(v, "fsdp", [(i, i ^ k) for i in range(fsdp)])

    def over_a(v, k):
        return lax.ppermute(v, "ad", [(i, (i + k) % ad) for i in range(ad)])

    def swap(v):
        return lax.ppermute(v, "tp", [(0, 1), (1, 0)])

    def cut(v, start, size, axis):
        return lax.dynamic_slice_in_dim(v, start, size, axis)

    own_dom = lax.broadcasted_iota(jnp.int32, (gslots, GROUP, 1), 0) // CAPD
    own_dom = own_dom == lax.broadcasted_iota(jnp.int32, (gslots, GROUP, 1), 1)

    def spread(v):
        n = v.shape[-1]
        wide = jnp.where(own_dom, v[..., None, :], jnp.zeros((), v.dtype))
        return wide.reshape(*v.shape[:-1], GROUP * n)

    def pick(v):
        n = v.shape[-1] // GROUP
        total = jnp.where(own_dom[:, 0], v[..., :n], 0.0)
        for e in range(1, GROUP):
            total = total + jnp.where(own_dom[:, e], v[..., e * n : (e + 1) * n], 0.0)
        return total

    x_in = []
    for c in range(CHUNKS):
        piece = []
        for k in range(fsdp):
            block = cut(input_rows, (f ^ k) * kf_width + t * kt + c * cw, cw, 1)
            piece.append(over_f(block, k) if k else block)
        x_in.append(piece)
    place = slot_places(domain[:, 0], ad * dloc)
    places = [over_f(place, k) if k else place for k in range(fsdp)]

    slot_iota = lax.broadcasted_iota(jnp.int32, (slots, rows), 0)

    def onehot(kf, ka):
        return (places[kf][None, :] == slot_iota + ((a + ka) % ad) * slots).astype(bf16)

    own_hot = [onehot(0, ka) for ka in range(ad)]
    dy = []
    for ka in range(ad):
        block = jnp.dot(own_hot[ka], layer_output_gradient, **f32).astype(bf16)
        dy.append(over_a(block, ka) if ka else block)
    dy = jnp.stack(dy).reshape(ad, ngroup, gslots, vloc)
    up = adapter_up_weight.reshape(ngroup, GROUP * rank, vloc)
    back = pick(jnp.einsum("agkv,gjv->agkj", dy, up, **f32))
    back = (adapter_scale * (back + swap(back))).astype(bf16)
    backs = jnp.stack([over_f(back, k) if k else back for k in range(fsdp)], axis=1)
    dys = jnp.stack([over_f(dy, k) if k else dy for k in range(fsdp)])

    hots = jnp.stack(
        [jnp.stack([onehot(kf, ka) for kf in range(fsdp)]) for ka in range(ad)]
    )
    x_full = [jnp.stack(piece) for piece in x_in]
    x_routed = []
    for c in range(CHUNKS):
        piece = []
        for ka in range(ad):
            block = jnp.einsum("fin,fnw->fiw", hots[ka], x_full[c], **f32).astype(bf16)
            piece.append(over_a(block, ka) if ka else block)
        x_routed.append(jnp.stack(piece).reshape(ad, fsdp, ngroup, gslots, cw))

    holder = t == fy
    col0 = fx * kf_width
    down_mine = cut(adapter_down_weight, col0 + t * kt, kt, 2)
    down_other = cut(adapter_down_weight, col0 + (1 - t) * kt, kt, 2)
    pairs = [(i * 2 + i // 2, i * 2 + 1 - i // 2) for i in range(fsdp)]
    down_got = lax.ppermute(down_other, ("fsdp", "tp"), pairs)
    down = jnp.where(holder, down_mine, down_got).reshape(ngroup, GROUP * rank, kt)

    w_mine = cut(value_weight_frozen, t * kt, kt, 0)
    w_got = swap(cut(value_weight_frozen, (1 - t) * kt, kt, 0))
    x_cols = jnp.concatenate(x_full, axis=2)
    base_other = jnp.einsum("fnw,wv->fnv", x_cols, w_got, **f32)
    base = jnp.einsum("fnw,wv->fnv", x_cols, w_mine, **f32) + swap(base_other)
    base_sum = base[0]
    for k in range(1, fsdp):
        base_sum = base_sum + over_f(base[k], k)

    grad_a = jnp.zeros((dloc, rloc, half), jnp.float32)
    rounds = [(p, q) for p in range(2) for q in range(2)]
    masked = []
    for p, q in rounds:
        owner = (t ^ q) * 2 + (fx ^ p)
        masked.append(spread(cut(backs, owner * rloc, rloc, 4)))
    for c in range(CHUNKS):
        for (p, q), mb in zip(rounds, masked):
            block = jnp.einsum("abgkj,abgkw->gjw", mb, x_routed[c], **f32)
            block = block.astype(bf16).reshape(dloc, rloc, cw)
            perm = [
                ((y * 2 + x) * 2 + s, ((s ^ q) * 2 + (x ^ p)) * 2 + y)
                for y in range(2)
                for x in range(2)
                for s in range(2)
            ]
            got = lax.ppermute(block, ("fsdp", "tp"), perm)
            start = (fx ^ p) * kf_width + (fy ^ q) * kt + c * cw
            grad_a = lax.dynamic_update_slice_in_dim(grad_a, got.astype(jnp.float32), start, 2)

    hid = None
    for c in range(CHUNKS):
        part = jnp.einsum(
            "abgkw,gjw->abgkj", x_routed[c], down[:, :, c * cw : (c + 1) * cw], **f32
        )
        hid = pick(part) if hid is None else hid + pick(part)
    rhalf = rank // 2
    hid = cut(hid, t * rhalf, rhalf, 4) + swap(cut(hid, (1 - t) * rhalf, rhalf, 4))
    hid_sum = hid[:, 0]
    for k in range(1, fsdp):
        hid_sum = hid_sum + over_f(hid[:, k], k)
    hid_own = hid_sum.astype(bf16)
    hid_got = swap(hid_own)
    hidden = jnp.where(
        t == 0,
        jnp.concatenate([hid_own, hid_got], axis=3),
        jnp.concatenate([hid_got, hid_own], axis=3),
    )

    delta = adapter_scale * jnp.einsum("agkj,gjv->agkv", spread(hidden), up, **f32)
    delta = delta.astype(bf16).reshape(ad, slots, vloc)
    back_rows = [over_a(delta[ka], ad - ka) if ka else delta[ka] for ka in range(ad)]
    added = jnp.einsum("ain,aiv->nv", jnp.stack(own_hot), jnp.stack(back_rows), **f32)
    y_out = (base_sum + added).astype(bf16)

    hid_cols = []
    for k in range(fsdp):
        block = cut(hidden, (f ^ k) * rloc, rloc, 3)
        hid_cols.append(over_f(block, k) if k else block)
    hid_cols = spread(jnp.stack(hid_cols))
    grad_b = adapter_scale * jnp.einsum("fagkj,fagkv->gjv", hid_cols, dys, **f32)
    return y_out, grad_a, grad_b.reshape(dloc, rloc, vloc)


def solution(mesh):
    placed = (
        P(("fsdp", "ad"), None),
        P("fsdp", "tp"),
        P("ad", None, "tp"),
        P("ad", None, "tp"),
        P(("fsdp", "ad"), "tp"),
        P(("fsdp", "ad"), None),
    )
    square = mesh.shape["fsdp"] == 4 and mesh.shape["tp"] == 2
    return jax.shard_map(
        column_body if square else general_body,
        mesh=mesh,
        in_specs=placed,
        out_specs=(P(("fsdp", "ad"), "tp"), P("ad", "fsdp", "tp"), P("ad", "fsdp", "tp")),
        check_vma=False,
    )
```

```python
import jax
import jax.numpy as jnp
from jax import lax
from jax.experimental import pallas as pl
from jax.experimental.pallas import tpu as pltpu
from jax.sharding import PartitionSpec as P

CAPD = 12
GROUP = 4
CHUNKS = 2

adapter_scale = 0.5


def slot_places(dom_ids, dom_total):
    row_count = dom_ids.shape[0]
    onehot = (dom_ids[:, None] == jnp.arange(dom_total, dtype=jnp.int32)[None, :]).astype(
        jnp.float32
    )
    row_iota = jnp.arange(row_count, dtype=jnp.int32)
    earlier = (row_iota[:, None] > row_iota[None, :]).astype(jnp.float32)
    prior = jnp.dot(earlier, onehot, preferred_element_type=jnp.float32)
    position = jnp.sum(prior * onehot, axis=1).astype(jnp.int32)
    return dom_ids * CAPD + position


def general_body(
    input_rows,
    value_weight_frozen,
    adapter_down_weight,
    adapter_up_weight,
    layer_output_gradient,
    domain,
):
    row_count = input_rows.shape[0]
    domain_local = adapter_down_weight.shape[0]
    width_local = adapter_down_weight.shape[2]
    value_width_local = adapter_up_weight.shape[2]
    ad_count = lax.axis_size("ad")
    slot_total = ad_count * domain_local * CAPD
    place = slot_places(domain[:, 0], ad_count * domain_local)
    row_iota = jnp.arange(row_count, dtype=jnp.int32)
    matches = place[None, :] == jnp.arange(slot_total, dtype=jnp.int32)[:, None]
    filled = jnp.any(matches, axis=1)
    source_row = jnp.sum(jnp.where(matches, row_iota[None, :], 0), axis=1)
    base = jnp.dot(
        input_rows,
        lax.all_gather(value_weight_frozen, "fsdp", axis=0, tiled=True),
        preferred_element_type=jnp.float32,
    )
    feature_cols = lax.dynamic_slice_in_dim(
        input_rows, lax.axis_index("tp") * width_local, width_local, 1
    )
    zero_value = jnp.zeros((), jnp.bfloat16)
    send_x = jnp.where(filled[:, None], feature_cols[source_row], zero_value)
    send_dy = jnp.where(filled[:, None], layer_output_gradient[source_row], zero_value)
    send_x = send_x.reshape(ad_count, domain_local * CAPD, width_local)
    send_dy = send_dy.reshape(ad_count, domain_local * CAPD, value_width_local)
    got_x = lax.all_to_all(send_x, "ad", split_axis=0, concat_axis=0, tiled=True)
    got_dy = lax.all_to_all(send_dy, "ad", split_axis=0, concat_axis=0, tiled=True)
    rows = got_x.reshape(ad_count, domain_local, CAPD, width_local)
    grads = got_dy.reshape(ad_count, domain_local, CAPD, value_width_local)
    f32 = dict(preferred_element_type=jnp.float32)
    hidden, back = lax.psum(
        (
            jnp.einsum("vqfj,qwj->vqfw", rows, adapter_down_weight, **f32),
            jnp.einsum("amgy,mzy->amgz", grads, adapter_up_weight, **f32),
        ),
        "tp",
    )
    hidden = hidden.astype(jnp.bfloat16)
    back = (adapter_scale * back).astype(jnp.bfloat16)
    delta = adapter_scale * jnp.einsum("lokh,ohi->loki", hidden, adapter_up_weight, **f32)
    delta = delta.astype(jnp.bfloat16).reshape(ad_count, domain_local * CAPD, value_width_local)
    part_a = jnp.einsum("sdcr,sdcx->drx", back, rows, **f32)
    part_b = adapter_scale * jnp.einsum("sdcr,sdce->dre", hidden, grads, **f32)
    returned = lax.all_to_all(delta, "ad", split_axis=0, concat_axis=0, tiled=True)
    returned = returned.reshape(slot_total, value_width_local)
    y_out = (base + returned[place].astype(jnp.float32)).astype(jnp.bfloat16)
    return (
        y_out,
        lax.psum_scatter(part_a, "fsdp", scatter_dimension=1, tiled=True),
        lax.psum_scatter(part_b, "fsdp", scatter_dimension=1, tiled=True),
    )


def base_kernel(order, *refs):
    out = refs[-1]
    w_refs, x_refs = refs[-3:-1], refs[:-3]
    chunks = len(x_refs) // (out.shape[0] // 2)
    cw = x_refs[0].shape[1]
    for k in range(out.shape[0] // 2):
        for side in range(2):
            total = None
            for c in range(chunks):
                term = jnp.dot(
                    x_refs[k * chunks + c][...],
                    w_refs[side][c * cw : (c + 1) * cw, :],
                    preferred_element_type=jnp.float32,
                )
                total = term if total is None else total + term
            out[order[2 * k + side]] = total


def column_body(
    input_rows,
    value_weight_frozen,
    adapter_down_weight,
    adapter_up_weight,
    layer_output_gradient,
    domain,
):
    f32 = dict(preferred_element_type=jnp.float32)
    bf16 = jnp.bfloat16
    fsdp, ad = lax.axis_size("fsdp"), lax.axis_size("ad")
    f, t, a = lax.axis_index("fsdp"), lax.axis_index("tp"), lax.axis_index("ad")
    fy, fx = f // 2, f % 2
    rows, width = input_rows.shape
    dloc, rank, half = adapter_down_weight.shape
    vloc = adapter_up_weight.shape[2]
    rloc = rank // fsdp
    kf_width = width // fsdp
    kt = kf_width // 2
    cw = kt // CHUNKS
    slots = dloc * CAPD
    ngroup = dloc // GROUP
    gslots = GROUP * CAPD

    def over_f(v, k):
        return lax.ppermute(v, "fsdp", [(i, i ^ k) for i in range(fsdp)])

    def over_a(v, k):
        return lax.ppermute(v, "ad", [(i, (i + k) % ad) for i in range(ad)])

    def swap(v):
        return lax.ppermute(v, "tp", [(0, 1), (1, 0)])

    def cut(v, start, size, axis):
        return lax.dynamic_slice_in_dim(v, start, size, axis)

    def own_lanes(n):
        slot = lax.broadcasted_iota(jnp.int32, (gslots, GROUP * n), 0) // CAPD
        return slot == lax.broadcasted_iota(jnp.int32, (gslots, GROUP * n), 1) // n

    def spread(v):
        wide = jnp.concatenate([v] * GROUP, axis=-1)
        return jnp.where(own_lanes(v.shape[-1]), wide, jnp.zeros((), v.dtype))

    def pick(v):
        n = v.shape[-1] // GROUP
        slot = lax.broadcasted_iota(jnp.int32, (gslots, n), 0) // CAPD
        total = v[..., :n]
        for e in range(1, GROUP):
            total = jnp.where(slot == e, v[..., e * n : (e + 1) * n], total)
        return total

    x_in = []
    for c in range(CHUNKS):
        piece = []
        for k in range(fsdp):
            block = cut(input_rows, (f ^ k) * kf_width + t * kt + c * cw, cw, 1)
            if c == 0:
                dom_row = jnp.pad(domain.T.astype(bf16), ((0, 15), (0, cw - rows)))
                block = jnp.concatenate([block, dom_row], axis=0)
            piece.append(over_f(block, k) if k else block)
        x_in.append(piece)
    doms = [v[rows, :rows].astype(jnp.int32) for v in x_in[0]]
    x_in[0] = [v[:rows] for v in x_in[0]]
    places = [slot_places(v, ad * dloc) for v in [domain[:, 0]] + doms[1:]]

    slot_iota = lax.broadcasted_iota(jnp.int32, (slots, rows), 0)

    def onehot(kf, ka):
        return (places[kf][None, :] == slot_iota + ((a + ka) % ad) * slots).astype(bf16)

    own_hot = [onehot(0, ka) for ka in range(ad)]
    dy = []
    for ka in range(ad):
        block = jnp.dot(own_hot[ka], layer_output_gradient, **f32).astype(bf16)
        dy.append(over_a(block, ka) if ka else block)

    hots = jnp.stack(
        [jnp.stack([onehot(kf, ka) for kf in range(fsdp)]) for ka in range(ad)]
    )
    x_routed = []
    for c in range(CHUNKS):
        piece = []
        for ka in range(ad):
            block = jnp.einsum("fin,fnw->fiw", hots[ka], jnp.stack(x_in[c]), **f32)
            block = block.astype(bf16)
            if c == 0 and ka == ad - 1:
                block, dn_held, w_held = lax.optimization_barrier(
                    (block, adapter_down_weight, value_weight_frozen)
                )
            piece.append(over_a(block, ka) if ka else block)
        x_routed.append(jnp.stack(piece).reshape(ad, fsdp, ngroup, gslots, cw))

    dy = jnp.stack(dy).reshape(ad, ngroup, gslots, vloc)
    up = adapter_up_weight.reshape(ngroup, GROUP * rank, vloc)
    back = pick(jnp.einsum("agkv,gjv->agkj", dy, up, **f32))
    back = (adapter_scale * (back + swap(back))).astype(bf16)
    back_all = lax.all_gather(back, "fsdp")
    dy_all = lax.all_gather(dy, "fsdp")

    holder = t == fy
    col0 = fx * kf_width
    down_mine = cut(dn_held, col0 + t * kt, kt, 2)
    down_other = cut(dn_held, col0 + (1 - t) * kt, kt, 2)
    pairs = [(i * 2 + i // 2, i * 2 + 1 - i // 2) for i in range(fsdp)]
    down_got = lax.ppermute(down_other, ("fsdp", "tp"), pairs)
    down = jnp.where(holder, down_mine, down_got).reshape(ngroup, GROUP * rank, kt)

    w_mine = cut(w_held, t * kt, kt, 0)
    w_got = swap(cut(w_held, (1 - t) * kt, kt, 0))
    order = jnp.stack([(f ^ k) * 2 + (t ^ s) for k in range(fsdp) for s in range(2)])
    vmem = pl.BlockSpec(memory_space=pltpu.VMEM)
    base = pl.pallas_call(
        base_kernel,
        out_shape=jax.ShapeDtypeStruct((2 * fsdp, rows, vloc), jnp.float32),
        in_specs=[pl.BlockSpec(memory_space=pltpu.SMEM)] + [vmem] * (fsdp * CHUNKS + 2),
        out_specs=vmem,
        compiler_params=pltpu.CompilerParams(vmem_limit_bytes=32 << 20),
        cost_estimate=pl.CostEstimate(
            flops=4 * fsdp * rows * kt * vloc, bytes_accessed=10 << 20, transcendentals=0
        ),
    )(order, *[x_in[c][k] for k in range(fsdp) for c in range(CHUNKS)], w_mine, w_got)
    base = lax.psum_scatter(base, ("fsdp", "tp"), scatter_dimension=0)

    backs = jnp.stack([cut(back_all, f ^ k, 1, 0)[0] for k in range(fsdp)], axis=1)
    parts = jnp.split(backs, fsdp, axis=-1)
    parts = [jnp.where(fx == 1, parts[i ^ 1], parts[i]) for i in range(fsdp)]
    parts = [jnp.where(t == 1, parts[i ^ 2], parts[i]) for i in range(fsdp)]
    masked = spread(jnp.concatenate(parts, axis=-1))

    grad_a = jnp.zeros((dloc, rloc, half), jnp.float32)
    rhalf = rank // 2
    hid = None
    for c in range(CHUNKS):
        part = jnp.einsum(
            "abgkw,gjw->abgkj", x_routed[c], down[:, :, c * cw : (c + 1) * cw], **f32
        )
        hid = pick(part) if hid is None else hid + pick(part)
        if c == CHUNKS - 1:
            hid = cut(hid, t * rhalf, rhalf, 4) + swap(cut(hid, (1 - t) * rhalf, rhalf, 4))
        hid, masked = lax.optimization_barrier((hid, masked))

        sums = jnp.einsum("abgkj,abgkw->gjw", masked, x_routed[c], **f32)
        sums = sums.astype(bf16).reshape(dloc, fsdp, rloc, cw)
        for r in range(fsdp):
            p, q = r % 2, r // 2
            perm = [
                ((y * 2 + x) * 2 + s, ((s ^ q) * 2 + (x ^ p)) * 2 + y)
                for y in range(2)
                for x in range(2)
                for s in range(2)
            ]
            got = lax.ppermute(sums[:, r], ("fsdp", "tp"), perm)
            start = (fx ^ p) * kf_width + (fy ^ q) * kt + c * cw
            grad_a = lax.dynamic_update_slice_in_dim(grad_a, got.astype(jnp.float32), start, 2)

    hid_sum = hid[:, 0]
    for k in range(1, fsdp):
        hid_sum = hid_sum + over_f(hid[:, k], k)
    hid_own = hid_sum.astype(bf16)
    hid_got = swap(hid_own)
    hidden = jnp.where(
        t == 0,
        jnp.concatenate([hid_own, hid_got], axis=3),
        jnp.concatenate([hid_got, hid_own], axis=3),
    )

    delta = adapter_scale * jnp.einsum("agkj,gjv->agkv", spread(hidden), up, **f32)
    delta = delta.astype(bf16).reshape(ad, slots, vloc)
    back_rows = [over_a(delta[ka], ad - ka) if ka else delta[ka] for ka in range(ad)]
    added = jnp.einsum("ain,aiv->nv", jnp.stack(own_hot), jnp.stack(back_rows), **f32)
    y_out = (base + added).astype(bf16)

    hid_cols = []
    for k in range(fsdp):
        block = cut(hidden, (f ^ k) * rloc, rloc, 3)
        hid_cols.append(over_f(block, k) if k else block)
    hid_cols = spread(jnp.stack(hid_cols))
    dys = jnp.stack([cut(dy_all, f ^ k, 1, 0)[0] for k in range(fsdp)])
    grad_b = adapter_scale * jnp.einsum("fagkj,fagkv->gjv", hid_cols, dys, **f32)
    return y_out, grad_a, grad_b.reshape(dloc, rloc, vloc)


def solution(mesh):
    placed = (
        P(("fsdp", "ad"), None),
        P("fsdp", "tp"),
        P("ad", None, "tp"),
        P("ad", None, "tp"),
        P(("fsdp", "ad"), "tp"),
        P(("fsdp", "ad"), None),
    )
    square = mesh.shape["fsdp"] == 4 and mesh.shape["tp"] == 2
    return jax.shard_map(
        column_body if square else general_body,
        mesh=mesh,
        in_specs=placed,
        out_specs=(P(("fsdp", "ad"), "tp"), P("ad", "fsdp", "tp"), P("ad", "fsdp", "tp")),
        check_vma=False,
    )
```

```python
import functools

import jax
import jax.numpy as jnp
from jax import lax
from jax.experimental import pallas as pl
from jax.experimental.pallas import tpu as pltpu
from jax.sharding import PartitionSpec as P

CAPD = 12
GROUP = 4
CHUNKS = 1

adapter_scale = 0.5


def slot_places(dom_ids, dom_total):
    row_count = dom_ids.shape[0]
    onehot = (dom_ids[:, None] == jnp.arange(dom_total, dtype=jnp.int32)[None, :]).astype(
        jnp.float32
    )
    row_iota = jnp.arange(row_count, dtype=jnp.int32)
    earlier = (row_iota[:, None] > row_iota[None, :]).astype(jnp.float32)
    prior = jnp.dot(earlier, onehot, preferred_element_type=jnp.float32)
    position = jnp.sum(prior * onehot, axis=1).astype(jnp.int32)
    return dom_ids * CAPD + position


def general_body(
    input_rows,
    value_weight_frozen,
    adapter_down_weight,
    adapter_up_weight,
    layer_output_gradient,
    domain,
):
    row_count = input_rows.shape[0]
    domain_local = adapter_down_weight.shape[0]
    width_local = adapter_down_weight.shape[2]
    value_width_local = adapter_up_weight.shape[2]
    ad_count = lax.axis_size("ad")
    slot_total = ad_count * domain_local * CAPD
    place = slot_places(domain[:, 0], ad_count * domain_local)
    row_iota = jnp.arange(row_count, dtype=jnp.int32)
    matches = place[None, :] == jnp.arange(slot_total, dtype=jnp.int32)[:, None]
    filled = jnp.any(matches, axis=1)
    source_row = jnp.sum(jnp.where(matches, row_iota[None, :], 0), axis=1)
    base = jnp.dot(
        input_rows,
        lax.all_gather(value_weight_frozen, "fsdp", axis=0, tiled=True),
        preferred_element_type=jnp.float32,
    )
    feature_cols = lax.dynamic_slice_in_dim(
        input_rows, lax.axis_index("tp") * width_local, width_local, 1
    )
    zero_value = jnp.zeros((), jnp.bfloat16)
    send_x = jnp.where(filled[:, None], feature_cols[source_row], zero_value)
    send_dy = jnp.where(filled[:, None], layer_output_gradient[source_row], zero_value)
    send_x = send_x.reshape(ad_count, domain_local * CAPD, width_local)
    send_dy = send_dy.reshape(ad_count, domain_local * CAPD, value_width_local)
    got_x = lax.all_to_all(send_x, "ad", split_axis=0, concat_axis=0, tiled=True)
    got_dy = lax.all_to_all(send_dy, "ad", split_axis=0, concat_axis=0, tiled=True)
    rows = got_x.reshape(ad_count, domain_local, CAPD, width_local)
    grads = got_dy.reshape(ad_count, domain_local, CAPD, value_width_local)
    f32 = dict(preferred_element_type=jnp.float32)
    hidden, back = lax.psum(
        (
            jnp.einsum("vqfj,qwj->vqfw", rows, adapter_down_weight, **f32),
            jnp.einsum("amgy,mzy->amgz", grads, adapter_up_weight, **f32),
        ),
        "tp",
    )
    hidden = hidden.astype(jnp.bfloat16)
    back = (adapter_scale * back).astype(jnp.bfloat16)
    delta = adapter_scale * jnp.einsum("lokh,ohi->loki", hidden, adapter_up_weight, **f32)
    delta = delta.astype(jnp.bfloat16).reshape(ad_count, domain_local * CAPD, value_width_local)
    part_a = jnp.einsum("sdcr,sdcx->drx", back, rows, **f32)
    part_b = adapter_scale * jnp.einsum("sdcr,sdce->dre", hidden, grads, **f32)
    returned = lax.all_to_all(delta, "ad", split_axis=0, concat_axis=0, tiled=True)
    returned = returned.reshape(slot_total, value_width_local)
    y_out = (base + returned[place].astype(jnp.float32)).astype(jnp.bfloat16)
    return (
        y_out,
        lax.psum_scatter(part_a, "fsdp", scatter_dimension=1, tiled=True),
        lax.psum_scatter(part_b, "fsdp", scatter_dimension=1, tiled=True),
    )


BF16, F32 = jnp.bfloat16, jnp.float32
VMEM = pl.BlockSpec(memory_space=pltpu.VMEM)
SMEM = pl.BlockSpec(memory_space=pltpu.SMEM)
ANY = pl.BlockSpec(memory_space=pl.ANY)


def dot(lhs, rhs, dims):
    return lax.dot_general(lhs, rhs, (dims, ((), ())), preferred_element_type=F32)


def call(kernel, out_shape, args, in_specs=None, **kwargs):
    outs = [jax.ShapeDtypeStruct(shape, dtype) for shape, dtype in out_shape]
    kwargs.setdefault("out_specs", [VMEM] * len(outs))
    return pl.pallas_call(
        kernel,
        out_shape=outs,
        in_specs=in_specs or [VMEM] * len(args),
        compiler_params=pltpu.CompilerParams(vmem_limit_bytes=48 << 20),
        cost_estimate=pl.CostEstimate(flops=1, bytes_accessed=1, transcendentals=0),
        **kwargs,
    )(*args)


def slot_domain(count, lanes, gslots):
    slot = lax.broadcasted_iota(jnp.int32, (count, lanes), 0)
    return lax.rem(slot, gslots) // CAPD


def widen(v, gslots):
    domain = slot_domain(*v.shape, gslots)
    parts = [jnp.where(domain == e, v.astype(F32), 0.0).astype(v.dtype) for e in range(GROUP)]
    return jnp.concatenate(parts, axis=1)


def narrow(v, gslots):
    n = v.shape[1] // GROUP
    domain = slot_domain(v.shape[0], n, gslots)
    total = v[:, :n]
    for e in range(1, GROUP):
        total = jnp.where(domain == e, v[:, e * n : (e + 1) * n], total)
    return total


def group_rows(refs, g, gslots):
    rows = pl.ds(g * gslots, gslots)
    parts = []
    for r in refs:
        if len(r.shape) == 2:
            parts.append(r[rows, :])
        else:
            parts.extend(r[i, rows, :] for i in range(r.shape[0]))
    return jnp.concatenate(parts, axis=0)


def pack_kernel(at, down, weight, down_out, w_out, sems):
    kt, rows = down_out.shape[2], w_out.shape[0]
    copies = []
    for d in range(down_out.shape[0]):
        columns = pl.ds(pl.multiple_of(at[0] * kt, kt), kt)
        copies.append((down.at[d, :, columns], down_out.at[d]))
    copies.append((weight.at[pl.ds(pl.multiple_of(at[1] * rows, rows), rows), :], w_out))
    copies = [pltpu.make_async_copy(*c, sems.at[i]) for i, c in enumerate(copies)]
    for c in copies:
        c.start()
    for c in copies:
        c.wait()


def one_hot(dom, first, slots, ad, dom_total):
    rows = dom.shape[1]
    names = lax.broadcasted_iota(jnp.int32, (dom_total, rows), 0)
    is_dom = (names == dom).astype(F32)
    before = lax.broadcasted_iota(jnp.int32, (rows, rows), 0) < lax.broadcasted_iota(
        jnp.int32, (rows, rows), 1
    )
    prior = dot(is_dom.astype(BF16), before.astype(F32).astype(BF16), ((1,), (0,)))
    position = jnp.sum(prior * is_dom, axis=0, keepdims=True).astype(jnp.int32)
    slot = lax.broadcasted_iota(jnp.int32, (ad * slots, rows), 0)
    slot = lax.rem(slot + first * slots, ad * slots)
    return (slot == dom * CAPD + position).astype(F32).astype(BF16)


def own_kernel(ad, slots, dom_total, at, dom, x, dy, hot_ref, *outs):
    hot = one_hot(dom[...], at[0], slots, ad, dom_total)
    hot_ref[...] = hot
    width = x.shape[1]
    moved = dot(hot, x[...], ((1,), (0,))).astype(BF16)
    moved_dy = dot(hot, dy[...], ((1,), (0,))).astype(BF16)
    for ka in range(ad):
        outs[ka][:, :width] = moved[ka * slots : (ka + 1) * slots]
        outs[ka][:, width:] = moved_dy[ka * slots : (ka + 1) * slots]


def others_kernel(fsdp, ad, slots, dom_total, at, *refs):
    x_refs, outs = refs[: fsdp - 1], refs[fsdp - 1 :]
    for kf in range(fsdp - 1):
        rows = x_refs[kf].shape[0] - 16
        dom = x_refs[kf][rows:, :rows].astype(F32).astype(jnp.int32)[:1]
        hot = one_hot(dom, at[0], slots, ad, dom_total)
        moved = dot(hot, x_refs[kf][:rows, :], ((1,), (0,))).astype(BF16)
        for c in range(CHUNKS):
            for ka in range(ad):
                cw = outs[c * ad + ka].shape[2]
                part = moved[ka * slots : (ka + 1) * slots, c * cw : (c + 1) * cw]
                outs[c * ad + ka][kf] = part


def back_kernel(ad, gslots, *refs):
    dy_refs, up, out = refs[:ad], refs[ad], refs[ad + 1]
    for g in range(up.shape[0] // GROUP):
        rows = pl.ds(g * gslots, gslots)
        dy = jnp.concatenate([r[rows, :] for r in dy_refs], axis=0)
        weights = up[g * GROUP : (g + 1) * GROUP].reshape(-1, up.shape[2])
        part = narrow(dot(dy, weights, ((1,), (1,))), gslots)
        for ka in range(ad):
            out[ka, rows, :] = part[ka * gslots : (ka + 1) * gslots]


def both_kernel(ad, mine, got, *refs):
    dy_refs, out = refs[:ad], refs[ad]
    width = dy_refs[0].shape[1]
    for ka in range(ad):
        out[ka, :, :width] = dy_refs[ka][...]
        out[ka, :, width:] = (adapter_scale * (mine[ka] + got[ka])).astype(BF16)


def hidden_kernel(fsdp, ad, gslots, start, last, at, *refs):
    own_refs, x_refs, down, down_got = refs[:ad], refs[ad : 2 * ad], refs[2 * ad], refs[2 * ad + 1]
    outs = refs[2 * ad + 2 : -2]
    earlier = None
    if start:
        earlier, outs = outs[0], outs[1:]
    held, sem = refs[-2:]
    cw = held.shape[2]

    @pl.when(at[0] == 1)
    def _():
        columns = pl.ds(pl.multiple_of(at[1], 128), cw)
        copy = pltpu.make_async_copy(down.at[:, :, columns], held, sem)
        copy.start()
        copy.wait()

    @pl.when(at[0] != 1)
    def _():
        copy = pltpu.make_async_copy(down_got.at[:, :, pl.ds(start, cw)], held, sem)
        copy.start()
        copy.wait()

    for g in range(held.shape[0] // GROUP):
        weights = held[g * GROUP : (g + 1) * GROUP].reshape(-1, cw)
        rows = pl.ds(g * gslots, gslots)
        for ka in range(ad):
            x = group_rows((own_refs[ka], x_refs[ka]), g, gslots)
            part = narrow(dot(x, weights, ((1,), (1,))), gslots)
            for kf in range(fsdp):
                new = part[kf * gslots : (kf + 1) * gslots]
                if earlier is not None:
                    new = new + earlier[kf, ka, rows, :]
                if not last:
                    outs[0][kf, ka, rows, :] = new
                else:
                    n = new.shape[1] // 2
                    second = at[2] == 1
                    outs[0][kf, ka, rows, :] = jnp.where(second, new[:, n:], new[:, :n])
                    outs[1][kf, ka, rows, :] = jnp.where(second, new[:, :n], new[:, n:])


def down_grad_kernel(fsdp, ad, gslots, at, *refs):
    own_refs, x_refs, back_refs = refs[:ad], refs[ad : 2 * ad], refs[2 * ad : 2 * ad + fsdp]
    outs, total = refs[2 * ad + fsdp : -1], refs[-1]
    rloc = outs[0].shape[1]
    rank = back_refs[0].shape[2]
    for g in range(outs[0].shape[0] // GROUP):
        rows = pl.ds(g * gslots, gslots)
        x = group_rows([r for pair in zip(own_refs, x_refs) for r in pair], g, gslots)
        back = [back_refs[kf][ka, rows, :] for ka in range(ad) for kf in range(fsdp)]
        back = widen(jnp.concatenate(back, axis=0), gslots)
        total[...] = dot(back, x, ((0,), (0,)))
        for r in range(fsdp):
            for e in range(GROUP):
                first = pl.multiple_of(e * rank + at[r] * rloc, rloc)
                outs[r][g * GROUP + e] = total[pl.ds(first, rloc), :].astype(BF16)


def place_kernel(fsdp, at, *refs):
    for r in range(fsdp):

        @pl.when(pl.program_id(0) == r)
        def _():
            refs[-1][...] = refs[r][...].astype(F32)


def delta_kernel(fsdp, ad, gslots, at, own, got, up, *outs):
    for g in range(up.shape[0] // GROUP):
        rows = pl.ds(g * gslots, gslots)
        mine = jnp.concatenate([own[ka, rows, :] for ka in range(ad)], axis=0)
        other = jnp.concatenate([got[ka, rows, :] for ka in range(ad)], axis=0)
        second = at[0] == 1
        low = jnp.where(second, other.astype(F32), mine.astype(F32))
        high = jnp.where(second, mine.astype(F32), other.astype(F32))
        hidden = jnp.concatenate([low, high], axis=1)
        weights = up[g * GROUP : (g + 1) * GROUP].reshape(-1, up.shape[2])
        delta = dot(widen(hidden.astype(BF16), gslots), weights, ((1,), (0,)))
        delta = (adapter_scale * delta).astype(BF16)
        rloc = hidden.shape[1] // fsdp
        for ka in range(ad):
            outs[ka][rows, :] = delta[ka * gslots : (ka + 1) * gslots]
        for kf in range(fsdp):
            part = hidden[:, :rloc]
            for i in range(1, fsdp):
                part = jnp.where(at[1 + kf] == i, hidden[:, i * rloc : (i + 1) * rloc], part)
            part = part.astype(BF16)
            for ka in range(ad):
                outs[ad + kf][ka, rows, :] = part[ka * gslots : (ka + 1) * gslots]


def up_grad_kernel(fsdp, ad, gslots, *refs):
    hid_refs, dy_refs, out = refs[:fsdp], refs[fsdp:-1], refs[-1]
    rloc = hid_refs[0].shape[2]
    for g in range(out.shape[0] // GROUP):
        hid = group_rows(hid_refs, g, gslots)
        dy = group_rows(dy_refs, g, gslots)
        domain = slot_domain(hid.shape[0], rloc, gslots)
        wide = [jnp.where(domain == e, hid.astype(F32), 0.0) for e in range(GROUP)]
        wide = jnp.concatenate(wide, axis=1).astype(BF16)
        total = adapter_scale * dot(wide, dy, ((0,), (0,)))
        for e in range(GROUP):
            out[g * GROUP + e] = total[e * rloc : (e + 1) * rloc]


def output_kernel(fsdp, ad, *refs):
    base, hot, rows, out = refs[:fsdp], refs[fsdp], refs[fsdp + 1 : -1], refs[-1]
    total = base[0][...]
    for k in range(1, fsdp):
        total = total + base[k][...]
    delta = jnp.concatenate([r[...] for r in rows], axis=0)
    out[...] = (total + dot(hot[...], delta, ((0,), (0,)))).astype(BF16)


def base_kernel(fsdp, rows, at, *refs):
    mine, other, weight, w_got, x_refs = refs[-2], refs[-1], refs[-4], refs[-3], refs[:-4]
    kt = w_got.shape[0]
    for k in range(fsdp):
        x = x_refs[k][:rows, :]
        own = weight[pl.ds(pl.multiple_of(at[0] * kt, kt), kt), :]
        mine[k] = dot(x, own, ((1,), (0,)))
        other[k] = dot(x, w_got[...], ((1,), (0,)))


def column_body(
    input_rows,
    value_weight_frozen,
    adapter_down_weight,
    adapter_up_weight,
    layer_output_gradient,
    domain,
):
    fsdp, ad = lax.axis_size("fsdp"), lax.axis_size("ad")
    f, t, a = lax.axis_index("fsdp"), lax.axis_index("tp"), lax.axis_index("ad")
    fy, fx = f // 2, f % 2
    rows, width = input_rows.shape
    dloc, rank, half = adapter_down_weight.shape
    vloc = adapter_up_weight.shape[2]
    rloc = rank // fsdp
    kf_width = width // fsdp
    kt = kf_width // 2
    slots = dloc * CAPD
    gslots = GROUP * CAPD
    cw = kt // CHUNKS

    def over_f(v, k):
        return lax.ppermute(v, "fsdp", [(i, i ^ k) for i in range(fsdp)]) if k else v

    def over_a(v, k):
        return lax.ppermute(v, "ad", [(i, (i + k) % ad) for i in range(ad)]) if k else v

    def swap(v):
        return lax.ppermute(v, "tp", [(0, 1), (1, 0)])

    def numbers(*values):
        return jnp.stack([jnp.asarray(v, jnp.int32) for v in values])

    def after(v, *others):
        return lax.optimization_barrier((v, others))[0]

    x_in = []
    for k in range(fsdp):
        block = lax.dynamic_slice_in_dim(input_rows, (f ^ k) * kf_width + t * kt, kt, 1)
        if k:
            dom_row = jnp.pad(domain.T.astype(BF16), ((0, 15), (0, kt - rows)))
            block = jnp.concatenate([block, dom_row], axis=0)
        x_in.append(block)
    x_in = lax.optimization_barrier(x_in)
    x_in = [over_f(v, k) for k, v in enumerate(x_in)]

    hot, *sends = call(
        functools.partial(own_kernel, ad, slots, ad * dloc),
        [((ad * slots, rows), BF16)] + [((slots, kt + vloc), BF16)] * ad,
        [numbers(a), domain.T, x_in[0], layer_output_gradient],
        [SMEM] + [VMEM] * 3,
    )
    sends[-1] = after(sends[-1], x_in[1])
    own = [over_a(v, ka) for ka, v in enumerate(sends)]

    down_other, w_other = call(
        pack_kernel,
        [((dloc, rank, kt), BF16), ((kt, vloc), BF16)],
        [
            numbers(fx * 2 + 1 - t, 1 - t),
            after(adapter_down_weight, *sends[:-1]),
            value_weight_frozen,
        ],
        [SMEM, ANY, ANY],
        out_specs=[ANY, ANY],
        scratch_shapes=[pltpu.SemaphoreType.DMA((dloc + 1,))],
    )

    sends = call(
        functools.partial(others_kernel, fsdp, ad, slots, ad * dloc),
        [((fsdp - 1, slots, cw), BF16)] * (CHUNKS * ad),
        [numbers(a), *lax.optimization_barrier((x_in[1:], own[1:]))[0]],
        [SMEM] + [VMEM] * (fsdp - 1),
    )
    x_routed = [[over_a(v, ka) for ka, v in enumerate(sends[:ad])]]

    own = after(own, *sends)

    dy_specs = [pl.BlockSpec((slots, vloc), lambda i: (0, kt // vloc))] * ad
    (back,) = call(
        functools.partial(back_kernel, ad, gslots),
        [((ad, slots, rank), F32)],
        [*own, adapter_up_weight],
        dy_specs + [pl.BlockSpec((dloc, rank, vloc), lambda i: (0, 0, 0))],
        grid=(1,),
    )
    pairs = [(i * 2 + i // 2, i * 2 + 1 - i // 2) for i in range(fsdp)]
    w_got = swap(after(w_other, back))
    back_spec = pl.BlockSpec((ad, slots, rank), lambda i: (0, 0, 0))
    (both,) = call(
        functools.partial(both_kernel, ad),
        [((ad, slots, vloc + rank), BF16)],
        [back, swap(back), *own],
        [back_spec] * 2 + dy_specs,
        grid=(1,),
    )
    w_got = after(w_got, both)
    both = [over_f(both, k) for k in range(fsdp)]
    down_got = lax.ppermute(after(down_other, w_got), ("fsdp", "tp"), pairs)
    for c in range(1, CHUNKS):
        chunk = [after(v, *x_routed[c - 1], *both) for v in sends[c * ad : (c + 1) * ad]]
        x_routed.append([over_a(v, ka) for ka, v in enumerate(chunk)])

    mine, other = call(
        functools.partial(base_kernel, fsdp, rows),
        [((fsdp, rows, vloc), F32)] * 2,
        [numbers(t), *x_in, value_weight_frozen, w_got],
        [SMEM] + [VMEM] * (fsdp + 2),
    )
    base = mine + swap(after(other, down_got))
    base = [over_f(base[k], k) for k in range(fsdp)]

    def chunk_specs(c):
        specs = [pl.BlockSpec((slots, cw), lambda i: (0, c))] * ad
        return specs + [pl.BlockSpec((fsdp - 1, slots, cw), lambda i: (0, 0, 0))] * ad

    def hidden(c, earlier, routed):
        last = c == CHUNKS - 1
        return call(
            functools.partial(hidden_kernel, fsdp, ad, gslots, c * cw, last),
            [((fsdp, ad, slots, rank // 2 if last else rank), F32)] * (2 if last else 1),
            [
                numbers(t == fy, fx * kf_width + t * kt + c * cw, t),
                *own,
                *routed,
                adapter_down_weight,
                down_got,
                *earlier,
            ],
            [SMEM] + chunk_specs(c) + [ANY, ANY] + [VMEM] * len(earlier),
            grid=(1,),
            scratch_shapes=[pltpu.VMEM((dloc, rank, cw), BF16), pltpu.SemaphoreType.DMA],
        )

    grad_a = None
    hid = []
    for c in range(CHUNKS):
        last = c == CHUNKS - 1
        if last:
            hid = hidden(c, hid, after(x_routed[c], *both, *base))
            hid = hid[0] + swap(hid[1])
            hid, both = lax.optimization_barrier((hid, both))
        sums = call(
            functools.partial(down_grad_kernel, fsdp, ad, gslots),
            [((dloc, rloc, cw), BF16)] * fsdp,
            [
                numbers(*[(t ^ (r // 2)) * 2 + (fx ^ (r % 2)) for r in range(fsdp)]),
                *own,
                *x_routed[c],
                *both,
            ],
            [SMEM]
            + chunk_specs(c)
            + [pl.BlockSpec((ad, slots, rank), lambda i: (0, 0, vloc // rank))] * fsdp,
            grid=(1,),
            scratch_shapes=[pltpu.VMEM((GROUP * rank, cw), F32)],
        )
        got = []
        for r in range(fsdp):
            p, q = r % 2, r // 2
            perm = [
                ((y * 2 + x) * 2 + s, ((s ^ q) * 2 + (x ^ p)) * 2 + y)
                for y in range(2)
                for x in range(2)
                for s in range(2)
            ]
            got.append(lax.ppermute(sums[r], ("fsdp", "tp"), perm))
        if not last:
            hid = hidden(c, hid, after(x_routed[c], *sums))
            x_routed[c + 1] = after(x_routed[c + 1], *got[:2])
        at = [
            ((fx ^ (r % 2)) * kf_width + (fy ^ (r // 2)) * kt + c * cw) // cw
            for r in range(fsdp)
        ]
        args = got if grad_a is None else [*got, grad_a]
        grad_a = pl.pallas_call(
            functools.partial(place_kernel, fsdp),
            out_shape=jax.ShapeDtypeStruct((dloc, rloc, half), F32),
            grid_spec=pltpu.PrefetchScalarGridSpec(
                num_scalar_prefetch=1,
                grid=(fsdp,),
                in_specs=[VMEM] * fsdp + [ANY] * (len(args) - fsdp),
                out_specs=pl.BlockSpec((dloc, rloc, cw), lambda i, at: (0, 0, at[i])),
            ),
            input_output_aliases={} if grad_a is None else {fsdp + 1: 0},
            cost_estimate=pl.CostEstimate(flops=1, bytes_accessed=1, transcendentals=0),
        )(numbers(*at), *args)

    hid = [over_f(hid[k], k) for k in range(fsdp)]
    hid_own = (hid[0] + hid[1] + hid[2] + hid[3]).astype(BF16)
    outs = call(
        functools.partial(delta_kernel, fsdp, ad, gslots),
        [((slots, vloc), BF16)] * ad + [((ad, slots, rloc), BF16)] * fsdp,
        [numbers(t, *[f ^ k for k in range(fsdp)]), hid_own, swap(hid_own), adapter_up_weight],
        [SMEM] + [VMEM] * 3,
    )
    returned = [over_a(v, (ad - ka) % ad) for ka, v in enumerate(outs[:ad])]
    hid_cols = [over_f(v, k) for k, v in enumerate(outs[ad:])]

    (y_out,) = call(
        functools.partial(output_kernel, fsdp, ad),
        [((rows, vloc), BF16)],
        [*base, hot, *returned],
    )
    (grad_b,) = call(
        functools.partial(up_grad_kernel, fsdp, ad, gslots),
        [((dloc, rloc, vloc), F32)],
        [*hid_cols, *both],
        [pl.BlockSpec((ad, slots, rloc), lambda i: (0, 0, 0))] * fsdp
        + [pl.BlockSpec((ad, slots, vloc), lambda i: (0, 0, 0))] * fsdp,
        grid=(1,),
    )
    return y_out, grad_a, grad_b


def solution(mesh):
    placed = (
        P(("fsdp", "ad"), None),
        P("fsdp", "tp"),
        P("ad", None, "tp"),
        P("ad", None, "tp"),
        P(("fsdp", "ad"), "tp"),
        P(("fsdp", "ad"), None),
    )
    square = mesh.shape["fsdp"] == 4 and mesh.shape["tp"] == 2
    return jax.shard_map(
        column_body if square else general_body,
        mesh=mesh,
        in_specs=placed,
        out_specs=(P(("fsdp", "ad"), "tp"), P("ad", "fsdp", "tp"), P("ad", "fsdp", "tp")),
        check_vma=False,
    )
```

```python
import functools

import jax
import jax.numpy as jnp
from jax import lax
from jax.experimental import pallas as pl
from jax.experimental.pallas import tpu as pltpu
from jax.sharding import PartitionSpec as P

CAPD = 12
GROUP = 4
CHUNKS = 2

adapter_scale = 0.5


def slot_places(dom_ids, dom_total):
    row_count = dom_ids.shape[0]
    onehot = (dom_ids[:, None] == jnp.arange(dom_total, dtype=jnp.int32)[None, :]).astype(
        jnp.float32
    )
    row_iota = jnp.arange(row_count, dtype=jnp.int32)
    earlier = (row_iota[:, None] > row_iota[None, :]).astype(jnp.float32)
    prior = jnp.dot(earlier, onehot, preferred_element_type=jnp.float32)
    position = jnp.sum(prior * onehot, axis=1).astype(jnp.int32)
    return dom_ids * CAPD + position


def general_body(
    input_rows,
    value_weight_frozen,
    adapter_down_weight,
    adapter_up_weight,
    layer_output_gradient,
    domain,
):
    row_count = input_rows.shape[0]
    domain_local = adapter_down_weight.shape[0]
    width_local = adapter_down_weight.shape[2]
    value_width_local = adapter_up_weight.shape[2]
    ad_count = lax.axis_size("ad")
    slot_total = ad_count * domain_local * CAPD
    place = slot_places(domain[:, 0], ad_count * domain_local)
    row_iota = jnp.arange(row_count, dtype=jnp.int32)
    matches = place[None, :] == jnp.arange(slot_total, dtype=jnp.int32)[:, None]
    filled = jnp.any(matches, axis=1)
    source_row = jnp.sum(jnp.where(matches, row_iota[None, :], 0), axis=1)
    base = jnp.dot(
        input_rows,
        lax.all_gather(value_weight_frozen, "fsdp", axis=0, tiled=True),
        preferred_element_type=jnp.float32,
    )
    feature_cols = lax.dynamic_slice_in_dim(
        input_rows, lax.axis_index("tp") * width_local, width_local, 1
    )
    zero_value = jnp.zeros((), jnp.bfloat16)
    send_x = jnp.where(filled[:, None], feature_cols[source_row], zero_value)
    send_dy = jnp.where(filled[:, None], layer_output_gradient[source_row], zero_value)
    send_x = send_x.reshape(ad_count, domain_local * CAPD, width_local)
    send_dy = send_dy.reshape(ad_count, domain_local * CAPD, value_width_local)
    got_x = lax.all_to_all(send_x, "ad", split_axis=0, concat_axis=0, tiled=True)
    got_dy = lax.all_to_all(send_dy, "ad", split_axis=0, concat_axis=0, tiled=True)
    rows = got_x.reshape(ad_count, domain_local, CAPD, width_local)
    grads = got_dy.reshape(ad_count, domain_local, CAPD, value_width_local)
    f32 = dict(preferred_element_type=jnp.float32)
    hidden, back = lax.psum(
        (
            jnp.einsum("vqfj,qwj->vqfw", rows, adapter_down_weight, **f32),
            jnp.einsum("amgy,mzy->amgz", grads, adapter_up_weight, **f32),
        ),
        "tp",
    )
    hidden = hidden.astype(jnp.bfloat16)
    back = (adapter_scale * back).astype(jnp.bfloat16)
    delta = adapter_scale * jnp.einsum("lokh,ohi->loki", hidden, adapter_up_weight, **f32)
    delta = delta.astype(jnp.bfloat16).reshape(ad_count, domain_local * CAPD, value_width_local)
    part_a = jnp.einsum("sdcr,sdcx->drx", back, rows, **f32)
    part_b = adapter_scale * jnp.einsum("sdcr,sdce->dre", hidden, grads, **f32)
    returned = lax.all_to_all(delta, "ad", split_axis=0, concat_axis=0, tiled=True)
    returned = returned.reshape(slot_total, value_width_local)
    y_out = (base + returned[place].astype(jnp.float32)).astype(jnp.bfloat16)
    return (
        y_out,
        lax.psum_scatter(part_a, "fsdp", scatter_dimension=1, tiled=True),
        lax.psum_scatter(part_b, "fsdp", scatter_dimension=1, tiled=True),
    )


BF16, F32 = jnp.bfloat16, jnp.float32
VMEM = pl.BlockSpec(memory_space=pltpu.VMEM)
SMEM = pl.BlockSpec(memory_space=pltpu.SMEM)
ANY = pl.BlockSpec(memory_space=pl.ANY)


def dot(lhs, rhs, dims):
    return lax.dot_general(lhs, rhs, (dims, ((), ())), preferred_element_type=F32)


def call(kernel, out_shape, fetched, plain=(), at=None, scratch=()):
    nf, n_out = len(fetched), len(out_shape)
    shapes = [v.shape[:-1] + (v.shape[-1] if w is None else w[1],) for v, w in fetched]

    def body(*refs):
        refs = list(refs)
        head = [refs.pop(0)] if at is not None else []
        sources, refs = refs[:nf], refs[nf:]
        rest, buffers = refs[: len(plain) + n_out], refs[len(plain) + n_out :]
        buffers, sems, extra = buffers[:nf], buffers[nf], buffers[nf + 1 :]
        copies = []
        for i, (source, (_, columns)) in enumerate(zip(sources, fetched)):
            if columns is not None:
                lead = (slice(None),) * (len(source.shape) - 1)
                source = source.at[lead + (pl.ds(*columns),)]
            copies.append(pltpu.make_async_copy(source, buffers[i], sems.at[i]))
        for c in copies:
            c.start()
        for c in copies:
            c.wait()
        kernel(*head, *buffers, *rest, *extra)

    return pl.pallas_call(
        body,
        out_shape=[jax.ShapeDtypeStruct(shape, dtype) for shape, dtype in out_shape],
        in_specs=[SMEM] * (at is not None) + [ANY] * nf + [VMEM] * len(plain),
        out_specs=[VMEM] * n_out,
        scratch_shapes=[pltpu.VMEM(shape, v.dtype) for shape, (v, _) in zip(shapes, fetched)]
        + [pltpu.SemaphoreType.DMA((max(nf, 1),))]
        + list(scratch),
        compiler_params=pltpu.CompilerParams(vmem_limit_bytes=48 << 20),
        cost_estimate=pl.CostEstimate(flops=1, bytes_accessed=1, transcendentals=0),
    )(*([at] if at is not None else []), *[v for v, _ in fetched], *plain)


def slot_domain(count, lanes, gslots):
    slot = lax.broadcasted_iota(jnp.int32, (count, lanes), 0)
    return lax.rem(slot, gslots) // CAPD


def widen(v, gslots):
    domain = slot_domain(*v.shape, gslots)
    parts = [jnp.where(domain == e, v.astype(F32), 0.0).astype(v.dtype) for e in range(GROUP)]
    return jnp.concatenate(parts, axis=1)


def narrow(v, gslots):
    n = v.shape[1] // GROUP
    domain = slot_domain(v.shape[0], n, gslots)
    total = v[:, :n]
    for e in range(1, GROUP):
        total = jnp.where(domain == e, v[:, e * n : (e + 1) * n], total)
    return total


def group_rows(refs, g, gslots):
    rows = pl.ds(g * gslots, gslots)
    parts = []
    for r in refs:
        if len(r.shape) == 2:
            parts.append(r[rows, :])
        else:
            parts.extend(r[i, rows, :] for i in range(r.shape[0]))
    return jnp.concatenate(parts, axis=0)


def one_hot(dom, first, slots, ad, dom_total):
    rows = dom.shape[1]
    names = lax.broadcasted_iota(jnp.int32, (dom_total, rows), 0)
    is_dom = (names == dom).astype(F32)
    before = lax.broadcasted_iota(jnp.int32, (rows, rows), 0) < lax.broadcasted_iota(
        jnp.int32, (rows, rows), 1
    )
    prior = dot(is_dom.astype(BF16), before.astype(F32).astype(BF16), ((1,), (0,)))
    position = jnp.sum(prior * is_dom, axis=0, keepdims=True).astype(jnp.int32)
    slot = lax.broadcasted_iota(jnp.int32, (ad * slots, rows), 0)
    slot = lax.rem(slot + first * slots, ad * slots)
    return (slot == dom * CAPD + position).astype(F32).astype(BF16)


def own_kernel(ad, slots, dom_total, at, dom, x, dy, hot_ref, *outs):
    hot = one_hot(dom[...], at[0], slots, ad, dom_total)
    hot_ref[...] = hot
    moved_dy = dot(hot, dy[...], ((1,), (0,))).astype(BF16)
    moved = dot(hot, x[...], ((1,), (0,))).astype(BF16)
    for ka in range(ad):
        outs[ka][...] = moved_dy[ka * slots : (ka + 1) * slots]
        outs[ad + ka][...] = moved[ka * slots : (ka + 1) * slots]


def others_kernel(fsdp, ad, slots, dom_total, at, *refs):
    x_refs, outs, plain = refs[: fsdp - 1], refs[fsdp - 1 : -1], refs[-1]
    for kf in range(fsdp - 1):
        rows = x_refs[kf].shape[0] - 16
        plain[kf] = x_refs[kf][:rows, :]
        dom = x_refs[kf][rows:, :rows].astype(F32).astype(jnp.int32)[:1]
        hot = one_hot(dom, at[0], slots, ad, dom_total)
        moved = dot(hot, x_refs[kf][:rows, :], ((1,), (0,))).astype(BF16)
        for c in range(CHUNKS):
            for ka in range(ad):
                cw = outs[c * ad + ka].shape[2]
                part = moved[ka * slots : (ka + 1) * slots, c * cw : (c + 1) * cw]
                outs[c * ad + ka][kf] = part


def back_kernel(ad, gslots, *refs):
    dy_refs, up, out = refs[:ad], refs[ad], refs[ad + 1]
    for g in range(up.shape[0] // GROUP):
        rows = pl.ds(g * gslots, gslots)
        dy = jnp.concatenate([r[rows, :] for r in dy_refs], axis=0)
        weights = up[g * GROUP : (g + 1) * GROUP].reshape(-1, up.shape[2])
        part = narrow(dot(dy, weights, ((1,), (1,))), gslots)
        for ka in range(ad):
            out[ka, rows, :] = part[ka * gslots : (ka + 1) * gslots]


def both_kernel(ad, mine, got, *refs):
    dy_refs, out = refs[:ad], refs[ad]
    width = dy_refs[0].shape[1]
    for ka in range(ad):
        out[ka, :, :width] = dy_refs[ka][...]
        out[ka, :, width:] = (adapter_scale * (mine[ka] + got[ka])).astype(BF16)


def hidden_kernel(fsdp, ad, gslots, first, last, at, *refs):
    own_refs, x_refs, held = refs[:ad], refs[ad : 2 * ad], refs[2 * ad]
    outs = refs[2 * ad + 1 :]
    earlier = None
    if not first:
        earlier, outs = outs[0], outs[1:]
    cw = held.shape[2]
    for g in range(held.shape[0] // GROUP):
        weights = held[g * GROUP : (g + 1) * GROUP].reshape(-1, cw)
        rows = pl.ds(g * gslots, gslots)
        for ka in range(ad):
            x = group_rows((own_refs[ka], x_refs[ka]), g, gslots)
            part = narrow(dot(x, weights, ((1,), (1,))), gslots)
            for kf in range(fsdp):
                new = part[kf * gslots : (kf + 1) * gslots]
                if earlier is not None:
                    new = new + earlier[kf, ka, rows, :]
                if not last:
                    outs[0][kf, ka, rows, :] = new
                else:
                    n = new.shape[1] // 2
                    second = at[0] == 1
                    outs[0][kf, ka, rows, :] = jnp.where(second, new[:, n:], new[:, :n])
                    outs[1][kf, ka, rows, :] = jnp.where(second, new[:, :n], new[:, n:])


def down_grad_kernel(fsdp, ad, gslots, at, *refs):
    own_refs, x_refs, back_refs = refs[:ad], refs[ad : 2 * ad], refs[2 * ad : 2 * ad + fsdp]
    outs, total = refs[2 * ad + fsdp : -1], refs[-1]
    rloc = outs[0].shape[1]
    rank = back_refs[0].shape[2]
    for g in range(outs[0].shape[0] // GROUP):
        rows = pl.ds(g * gslots, gslots)
        x = group_rows([r for pair in zip(own_refs, x_refs) for r in pair], g, gslots)
        back = [back_refs[kf][ka, rows, :] for ka in range(ad) for kf in range(fsdp)]
        back = widen(jnp.concatenate(back, axis=0), gslots)
        total[...] = dot(back, x, ((0,), (0,)))
        for r in range(fsdp):
            for e in range(GROUP):
                first = pl.multiple_of(e * rank + at[r] * rloc, rloc)
                outs[r][g * GROUP + e] = total[pl.ds(first, rloc), :].astype(BF16)


def place_kernel(fsdp, at, *refs):
    for r in range(fsdp):

        @pl.when(pl.program_id(0) == r)
        def _():
            refs[-1][...] = refs[r][...].astype(F32)


def delta_kernel(fsdp, ad, gslots, at, own, got, up, *outs):
    for g in range(up.shape[0] // GROUP):
        rows = pl.ds(g * gslots, gslots)
        mine = jnp.concatenate([own[ka, rows, :] for ka in range(ad)], axis=0)
        other = jnp.concatenate([got[ka, rows, :] for ka in range(ad)], axis=0)
        second = at[0] == 1
        low = jnp.where(second, other.astype(F32), mine.astype(F32))
        high = jnp.where(second, mine.astype(F32), other.astype(F32))
        hidden = jnp.concatenate([low, high], axis=1)
        weights = up[g * GROUP : (g + 1) * GROUP].reshape(-1, up.shape[2])
        delta = dot(widen(hidden.astype(BF16), gslots), weights, ((1,), (0,)))
        delta = (adapter_scale * delta).astype(BF16)
        rloc = hidden.shape[1] // fsdp
        for ka in range(ad):
            outs[ka][rows, :] = delta[ka * gslots : (ka + 1) * gslots]
        for kf in range(fsdp):
            part = hidden[:, :rloc]
            for i in range(1, fsdp):
                part = jnp.where(at[1 + kf] == i, hidden[:, i * rloc : (i + 1) * rloc], part)
            part = part.astype(BF16)
            for ka in range(ad):
                outs[ad + kf][ka, rows, :] = part[ka * gslots : (ka + 1) * gslots]


def up_grad_kernel(fsdp, ad, gslots, *refs):
    hid_refs, dy_refs, out = refs[:fsdp], refs[fsdp:-1], refs[-1]
    rloc = hid_refs[0].shape[2]
    for g in range(out.shape[0] // GROUP):
        hid = group_rows(hid_refs, g, gslots)
        dy = group_rows(dy_refs, g, gslots)
        domain = slot_domain(hid.shape[0], rloc, gslots)
        wide = [jnp.where(domain == e, hid.astype(F32), 0.0) for e in range(GROUP)]
        wide = jnp.concatenate(wide, axis=1).astype(BF16)
        total = adapter_scale * dot(wide, dy, ((0,), (0,)))
        for e in range(GROUP):
            out[g * GROUP + e] = total[e * rloc : (e + 1) * rloc]


def output_kernel(fsdp, ad, *refs):
    base, hot, rows, out = refs[:fsdp], refs[fsdp], refs[fsdp + 1 : -1], refs[-1]
    total = base[0][...]
    for k in range(1, fsdp):
        total = total + base[k][...]
    delta = jnp.concatenate([r[...] for r in rows], axis=0)
    out[...] = (total + dot(hot[...], delta, ((0,), (0,)))).astype(BF16)


def base_kernel(fsdp, at, own, mine, got, weight, *outs):
    kt = mine.shape[2]
    outs[0][...] = dot(own[...], weight[...], ((1,), (0,)))
    w_mine = weight[pl.ds(pl.multiple_of(at[0] * kt, kt), kt), :]
    w_got = weight[pl.ds(pl.multiple_of((1 - at[0]) * kt, kt), kt), :]
    for k in range(1, fsdp):
        total = dot(mine[k - 1], w_mine, ((1,), (0,)))
        outs[k][...] = total + dot(got[k - 1], w_got, ((1,), (0,)))


def column_body(
    input_rows,
    value_weight_frozen,
    adapter_down_weight,
    adapter_up_weight,
    layer_output_gradient,
    domain,
):
    fsdp, ad = lax.axis_size("fsdp"), lax.axis_size("ad")
    f, t, a = lax.axis_index("fsdp"), lax.axis_index("tp"), lax.axis_index("ad")
    fy, fx = f // 2, f % 2
    rows, width = input_rows.shape
    dloc, rank, half = adapter_down_weight.shape
    vloc = adapter_up_weight.shape[2]
    rloc = rank // fsdp
    kf_width = width // fsdp
    kt = kf_width // 2
    slots = dloc * CAPD
    gslots = GROUP * CAPD
    cw = kt // CHUNKS

    def over_f(v, k):
        return lax.ppermute(v, "fsdp", [(i, i ^ k) for i in range(fsdp)]) if k else v

    def over_a(v, k):
        return lax.ppermute(v, "ad", [(i, (i + k) % ad) for i in range(ad)]) if k else v

    def swap(v):
        return lax.ppermute(v, "tp", [(0, 1), (1, 0)])

    def numbers(*values):
        return jnp.stack([jnp.asarray(v, jnp.int32) for v in values])

    def after(v, *others):
        return lax.optimization_barrier((v, others))[0]

    x_in = []
    for k in range(fsdp):
        block = lax.dynamic_slice_in_dim(input_rows, (f ^ k) * kf_width + t * kt, kt, 1)
        if k:
            dom_row = jnp.pad(domain.T.astype(BF16), ((0, 15), (0, kt - rows)))
            block = jnp.concatenate([block, dom_row], axis=0)
        x_in.append(block)
    x_in = lax.optimization_barrier(x_in)
    x_in[1], x_in[2] = over_f(x_in[1], 1), over_f(x_in[2], 2)
    x_in[3] = over_f(x_in[3], 3)

    hot, *sends = call(
        functools.partial(own_kernel, ad, slots, ad * dloc),
        [((ad * slots, rows), BF16)]
        + [((slots, vloc), BF16)] * ad
        + [((slots, kt), BF16)] * ad,
        [(v, None) for v in (domain.T, x_in[0], layer_output_gradient)],
        at=numbers(a),
    )
    dy = [over_a(v, ka) for ka, v in enumerate(sends[:ad])]
    own = [over_a(after(v, *dy), ka) for ka, v in enumerate(sends[ad:-1])]
    own.append(over_a(after(sends[-1], *dy, x_in[1]), ad - 1))

    (back,) = call(
        functools.partial(back_kernel, ad, gslots),
        [((ad, slots, rank), F32)],
        [(v, None) for v in after(dy, x_in[1], x_in[2])] + [(adapter_up_weight, None)],
    )
    (both,) = call(
        functools.partial(both_kernel, ad),
        [((ad, slots, vloc + rank), BF16)],
        [(back, None), (swap(back), None)] + [(v, None) for v in dy],
    )

    ready = after(x_in[1:], *own, both)
    *sends, x_plain = call(
        functools.partial(others_kernel, fsdp, ad, slots, ad * dloc),
        [((fsdp - 1, slots, cw), BF16)] * (CHUNKS * ad) + [((fsdp - 1, rows, kt), BF16)],
        [(v, None) for v in ready],
        at=numbers(a),
    )
    x_routed = [[over_a(v, ka) for ka, v in enumerate(sends[:ad])]]

    x_chip = lax.dynamic_slice_in_dim(input_rows, f * kf_width, kf_width, 1)
    base = call(
        functools.partial(base_kernel, fsdp),
        [((rows, vloc), F32)] * fsdp,
        [(v, None) for v in (x_chip, x_plain, swap(x_plain), value_weight_frozen)],
        at=numbers(t),
    )
    base_plain = base[0]

    both = [after(both, x_plain)] * fsdp
    both[1], both[2] = over_f(both[1], 1), over_f(both[2], 2)
    both[3] = over_f(after(both[3], base_plain), 3)
    held = after(adapter_down_weight, x_plain)
    down_other = lax.dynamic_slice_in_dim(held, (fx * 2 + 1 - t) * kt, kt, 2)
    pairs = [(i * 2 + i // 2, i * 2 + 1 - i // 2) for i in range(fsdp)]
    down_got = lax.ppermute(after(down_other, x_routed[0], both), ("fsdp", "tp"), pairs)

    for c in range(1, CHUNKS):
        chunk = [after(v, *x_routed[c - 1], *both) for v in sends[c * ad : (c + 1) * ad]]
        x_routed.append([over_a(v, ka) for ka, v in enumerate(chunk)])


    down_mine = lax.dynamic_slice_in_dim(adapter_down_weight, (fx * 2 + t) * kt, kt, 2)
    down = jnp.where(t == fy, down_mine, down_got)

    def chunk_of(c, routed):
        return [(v, (c * cw, cw)) for v in own] + [(v, None) for v in routed]

    def hidden(c, earlier, routed):
        last = c == CHUNKS - 1
        return call(
            functools.partial(hidden_kernel, fsdp, ad, gslots, c == 0, last),
            [((fsdp, ad, slots, rank // 2 if last else rank), F32)] * (2 if last else 1),
            [*chunk_of(c, routed), (down, (c * cw, cw)), *[(v, None) for v in earlier]],
            at=numbers(t),
        )

    grad_a = None
    hid = []
    for c in range(CHUNKS):
        last = c == CHUNKS - 1
        if last:
            hid = hidden(c, hid, x_routed[c])
            hid = hid[0] + swap(hid[1])
            hid = [over_f(hid[k], k) for k in range(fsdp)]
            hid, both = lax.optimization_barrier((hid, both))
        sums = call(
            functools.partial(down_grad_kernel, fsdp, ad, gslots),
            [((dloc, rloc, cw), BF16)] * fsdp,
            [*chunk_of(c, x_routed[c]), *[(v, (vloc, rank)) for v in both]],
            at=numbers(*[(t ^ (r // 2)) * 2 + (fx ^ (r % 2)) for r in range(fsdp)]),
            scratch=[pltpu.VMEM((GROUP * rank, cw), F32)],
        )
        got = []
        if not last:
            hid = hidden(c, hid, after(x_routed[c], *sums))
            sums = [*sums[:2], *after(sums[2:], hid)]
        for r in range(fsdp):
            p, q = r % 2, r // 2
            perm = [
                ((y * 2 + x) * 2 + s, ((s ^ q) * 2 + (x ^ p)) * 2 + y)
                for y in range(2)
                for x in range(2)
                for s in range(2)
            ]
            got.append(lax.ppermute(sums[r], ("fsdp", "tp"), perm))
        if not last:
            x_routed[c + 1] = after(x_routed[c + 1], *got)
            base = [over_f(after(v, *got), k) for k, v in enumerate(base)]
        at = [
            ((fx ^ (r % 2)) * kf_width + (fy ^ (r // 2)) * kt + c * cw) // cw
            for r in range(fsdp)
        ]
        if c == 0:
            grad_a = pl.pallas_call(
                functools.partial(place_kernel, fsdp),
                out_shape=jax.ShapeDtypeStruct((dloc, rloc, half), F32),
                grid_spec=pltpu.PrefetchScalarGridSpec(
                    num_scalar_prefetch=1,
                    grid=(fsdp,),
                    in_specs=[VMEM] * fsdp,
                    out_specs=pl.BlockSpec((dloc, rloc, cw), lambda i, at: (0, 0, at[i])),
                ),
                cost_estimate=pl.CostEstimate(flops=1, bytes_accessed=1, transcendentals=0),
            )(numbers(*at), *got)
        else:
            for v, column in zip(got, at):
                grad_a = lax.dynamic_update_slice_in_dim(
                    grad_a, v.astype(F32), column * cw, 2
                )

    hid_own = (hid[0] + hid[1] + hid[2] + hid[3]).astype(BF16)
    outs = call(
        functools.partial(delta_kernel, fsdp, ad, gslots),
        [((slots, vloc), BF16)] * ad + [((ad, slots, rloc), BF16)] * fsdp,
        [(v, None) for v in (hid_own, swap(hid_own), adapter_up_weight)],
        at=numbers(t, *[f ^ k for k in range(fsdp)]),
    )
    returned = [over_a(v, (ad - ka) % ad) for ka, v in enumerate(outs[:ad])]
    hid_cols = [over_f(v, k) for k, v in enumerate(outs[ad:])]

    (y_out,) = call(
        functools.partial(output_kernel, fsdp, ad),
        [((rows, vloc), BF16)],
        [(v, None) for v in (*base, hot, *returned)],
    )
    (grad_b,) = call(
        functools.partial(up_grad_kernel, fsdp, ad, gslots),
        [((dloc, rloc, vloc), F32)],
        [(v, None) for v in hid_cols] + [(v, (0, vloc)) for v in both],
    )
    return y_out, grad_a, grad_b


def solution(mesh):
    placed = (
        P(("fsdp", "ad"), None),
        P("fsdp", "tp"),
        P("ad", None, "tp"),
        P("ad", None, "tp"),
        P(("fsdp", "ad"), "tp"),
        P(("fsdp", "ad"), None),
    )
    square = mesh.shape["fsdp"] == 4 and mesh.shape["tp"] == 2
    return jax.shard_map(
        column_body if square else general_body,
        mesh=mesh,
        in_specs=placed,
        out_specs=(P(("fsdp", "ad"), "tp"), P("ad", "fsdp", "tp"), P("ad", "fsdp", "tp")),
        check_vma=False,
    )
```

```python
import functools

import jax
import jax.numpy as jnp
from jax import lax
from jax.experimental import pallas as pl
from jax.experimental.pallas import tpu as pltpu
from jax.sharding import PartitionSpec as P

CAPD = 12
GROUP = 4
CHUNKS = 2

adapter_scale = 0.5


def slot_places(dom_ids, dom_total):
    row_count = dom_ids.shape[0]
    onehot = (dom_ids[:, None] == jnp.arange(dom_total, dtype=jnp.int32)[None, :]).astype(
        jnp.float32
    )
    row_iota = jnp.arange(row_count, dtype=jnp.int32)
    earlier = (row_iota[:, None] > row_iota[None, :]).astype(jnp.float32)
    prior = jnp.dot(earlier, onehot, preferred_element_type=jnp.float32)
    position = jnp.sum(prior * onehot, axis=1).astype(jnp.int32)
    return dom_ids * CAPD + position


def general_body(
    input_rows,
    value_weight_frozen,
    adapter_down_weight,
    adapter_up_weight,
    layer_output_gradient,
    domain,
):
    row_count = input_rows.shape[0]
    domain_local = adapter_down_weight.shape[0]
    width_local = adapter_down_weight.shape[2]
    value_width_local = adapter_up_weight.shape[2]
    ad_count = lax.axis_size("ad")
    slot_total = ad_count * domain_local * CAPD
    place = slot_places(domain[:, 0], ad_count * domain_local)
    row_iota = jnp.arange(row_count, dtype=jnp.int32)
    matches = place[None, :] == jnp.arange(slot_total, dtype=jnp.int32)[:, None]
    filled = jnp.any(matches, axis=1)
    source_row = jnp.sum(jnp.where(matches, row_iota[None, :], 0), axis=1)
    base = jnp.dot(
        input_rows,
        lax.all_gather(value_weight_frozen, "fsdp", axis=0, tiled=True),
        preferred_element_type=jnp.float32,
    )
    feature_cols = lax.dynamic_slice_in_dim(
        input_rows, lax.axis_index("tp") * width_local, width_local, 1
    )
    zero_value = jnp.zeros((), jnp.bfloat16)
    send_x = jnp.where(filled[:, None], feature_cols[source_row], zero_value)
    send_dy = jnp.where(filled[:, None], layer_output_gradient[source_row], zero_value)
    send_x = send_x.reshape(ad_count, domain_local * CAPD, width_local)
    send_dy = send_dy.reshape(ad_count, domain_local * CAPD, value_width_local)
    got_x = lax.all_to_all(send_x, "ad", split_axis=0, concat_axis=0, tiled=True)
    got_dy = lax.all_to_all(send_dy, "ad", split_axis=0, concat_axis=0, tiled=True)
    rows = got_x.reshape(ad_count, domain_local, CAPD, width_local)
    grads = got_dy.reshape(ad_count, domain_local, CAPD, value_width_local)
    f32 = dict(preferred_element_type=jnp.float32)
    hidden, back = lax.psum(
        (
            jnp.einsum("vqfj,qwj->vqfw", rows, adapter_down_weight, **f32),
            jnp.einsum("amgy,mzy->amgz", grads, adapter_up_weight, **f32),
        ),
        "tp",
    )
    hidden = hidden.astype(jnp.bfloat16)
    back = (adapter_scale * back).astype(jnp.bfloat16)
    delta = adapter_scale * jnp.einsum("lokh,ohi->loki", hidden, adapter_up_weight, **f32)
    delta = delta.astype(jnp.bfloat16).reshape(ad_count, domain_local * CAPD, value_width_local)
    part_a = jnp.einsum("sdcr,sdcx->drx", back, rows, **f32)
    part_b = adapter_scale * jnp.einsum("sdcr,sdce->dre", hidden, grads, **f32)
    returned = lax.all_to_all(delta, "ad", split_axis=0, concat_axis=0, tiled=True)
    returned = returned.reshape(slot_total, value_width_local)
    y_out = (base + returned[place].astype(jnp.float32)).astype(jnp.bfloat16)
    return (
        y_out,
        lax.psum_scatter(part_a, "fsdp", scatter_dimension=1, tiled=True),
        lax.psum_scatter(part_b, "fsdp", scatter_dimension=1, tiled=True),
    )


BF16, F32 = jnp.bfloat16, jnp.float32
VMEM_BYTES = 58 << 20
VMEM = pl.BlockSpec(memory_space=pltpu.VMEM)
SMEM = pl.BlockSpec(memory_space=pltpu.SMEM)
ANY = pl.BlockSpec(memory_space=pl.ANY)


def dot(lhs, rhs, dims):
    return lax.dot_general(lhs, rhs, (dims, ((), ())), preferred_element_type=F32)


def call(kernel, out_shape, fetched, at=None, scratch=(), either=None, flops=1):
    nf, n_out = len(fetched), len(out_shape)
    shapes = [v.shape[:-1] + (v.shape[-1] if w is None else w[1],) for v, w in fetched]
    sources = [v for v, _ in fetched] + ([] if either is None else list(either[:2]))
    buffers = [pltpu.VMEM(shape, v.dtype) for shape, (v, _) in zip(shapes, fetched)]
    if either is not None:
        lead, width = either[0].shape[:-1], either[2][1]
        buffers.append(pltpu.VMEM(lead + (width,), either[0].dtype))
        buffers.append(pltpu.SemaphoreType.DMA((lead[0],)))

    def body(*refs):
        refs = list(refs)
        head = [refs.pop(0)] if at is not None else []
        froms, refs = refs[: len(sources)], refs[len(sources) :]
        outs, refs = refs[:n_out], refs[n_out:]
        sems, held, extra = refs[0], refs[1 : 1 + len(buffers)], refs[1 + len(buffers) :]
        copies = []
        for i, (source, (_, columns)) in enumerate(zip(froms, fetched)):
            if columns is not None:
                first = (slice(None),) * (len(source.shape) - 1)
                source = source.at[first + (pl.ds(*columns),)]
            copies.append(pltpu.make_async_copy(source, held[i], sems.at[i]))
        for c in copies:
            c.start()
        if either is not None:
            one, other = froms[nf:]
            buffer, more = held[nf], held.pop()
            start = pl.multiple_of(head[0][1], 128)
            parts = [
                pltpu.make_async_copy(one.at[d, :, pl.ds(start, width)], buffer.at[d], more.at[d])
                for d in range(lead[0])
            ]
            others = [
                pltpu.make_async_copy(
                    other.at[d, :, pl.ds(*either[2])], buffer.at[d], more.at[d]
                )
                for d in range(lead[0])
            ]

            @pl.when(head[0][0] == 1)
            def _():
                for c in parts:
                    c.start()

            @pl.when(head[0][0] != 1)
            def _():
                for c in others:
                    c.start()

            copies.extend(others)
        for c in copies:
            c.wait()
        kernel(*head, *held[:nf], *outs, *held[nf:], *extra)

    return pl.pallas_call(
        body,
        out_shape=[jax.ShapeDtypeStruct(shape, dtype) for shape, dtype in out_shape],
        in_specs=[SMEM] * (at is not None) + [ANY] * len(sources),
        out_specs=[VMEM] * n_out,
        scratch_shapes=[pltpu.SemaphoreType.DMA((nf,)), *buffers, *scratch],
        compiler_params=pltpu.CompilerParams(vmem_limit_bytes=VMEM_BYTES),
        cost_estimate=pl.CostEstimate(flops=flops, bytes_accessed=1, transcendentals=0),
    )(*([at] if at is not None else []), *sources)


def slot_domain(count, lanes, gslots):
    slot = lax.broadcasted_iota(jnp.int32, (count, lanes), 0)
    return lax.rem(slot, gslots) // CAPD


def widen(v, gslots):
    domain = slot_domain(*v.shape, gslots)
    parts = [jnp.where(domain == e, v.astype(F32), 0.0).astype(v.dtype) for e in range(GROUP)]
    return jnp.concatenate(parts, axis=1)


def narrow(v, gslots):
    n = v.shape[1] // GROUP
    domain = slot_domain(v.shape[0], n, gslots)
    total = v[:, :n]
    for e in range(1, GROUP):
        total = jnp.where(domain == e, v[:, e * n : (e + 1) * n], total)
    return total


def group_rows(refs, g, gslots):
    rows = pl.ds(g * gslots, gslots)
    parts = []
    for r in refs:
        if len(r.shape) == 2:
            parts.append(r[rows, :])
        else:
            parts.extend(r[i, rows, :] for i in range(r.shape[0]))
    return jnp.concatenate(parts, axis=0)


def one_hot(dom, first, slots, ad, dom_total):
    rows = dom.shape[1]
    names = lax.broadcasted_iota(jnp.int32, (dom_total, rows), 0)
    is_dom = (names == dom).astype(F32)
    before = lax.broadcasted_iota(jnp.int32, (rows, rows), 0) < lax.broadcasted_iota(
        jnp.int32, (rows, rows), 1
    )
    prior = dot(is_dom.astype(BF16), before.astype(F32).astype(BF16), ((1,), (0,)))
    position = jnp.sum(prior * is_dom, axis=0, keepdims=True).astype(jnp.int32)
    slot = lax.broadcasted_iota(jnp.int32, (ad * slots, rows), 0)
    slot = lax.rem(slot + first * slots, ad * slots)
    return (slot == dom * CAPD + position).astype(F32).astype(BF16)


def own_kernel(ad, slots, dom_total, at, dom, x, dy, hot_ref, *outs):
    hot = one_hot(dom[...], at[0], slots, ad, dom_total)
    hot_ref[...] = hot
    width = x.shape[1]
    moved = dot(hot, x[...], ((1,), (0,))).astype(BF16)
    moved_dy = dot(hot, dy[...], ((1,), (0,))).astype(BF16)
    for ka in range(ad):
        outs[ka][:, :width] = moved[ka * slots : (ka + 1) * slots]
        outs[ka][:, width:] = moved_dy[ka * slots : (ka + 1) * slots]


def others_kernel(fsdp, ad, slots, dom_total, at, *refs):
    x_refs, outs, plain = refs[: fsdp - 1], refs[fsdp - 1 : -1], refs[-1]
    for kf in range(fsdp - 1):
        rows = x_refs[kf].shape[0] - 16
        plain[kf] = x_refs[kf][:rows, :]
        dom = x_refs[kf][rows:, :rows].astype(F32).astype(jnp.int32)[:1]
        hot = one_hot(dom, at[0], slots, ad, dom_total)
        moved = dot(hot, x_refs[kf][:rows, :], ((1,), (0,))).astype(BF16)
        for c in range(CHUNKS):
            for ka in range(ad):
                cw = outs[c * ad + ka].shape[2]
                part = moved[ka * slots : (ka + 1) * slots, c * cw : (c + 1) * cw]
                outs[c * ad + ka][kf] = part


def back_kernel(ad, gslots, *refs):
    dy_refs, up, out = refs[:ad], refs[ad], refs[ad + 1]
    for g in range(up.shape[0] // GROUP):
        rows = pl.ds(g * gslots, gslots)
        dy = jnp.concatenate([r[rows, :] for r in dy_refs], axis=0)
        weights = up[g * GROUP : (g + 1) * GROUP].reshape(-1, up.shape[2])
        part = narrow(dot(dy, weights, ((1,), (1,))), gslots)
        for ka in range(ad):
            out[ka, rows, :] = part[ka * gslots : (ka + 1) * gslots]


def both_kernel(ad, mine, got, *refs):
    dy_refs, out = refs[:ad], refs[ad]
    width = dy_refs[0].shape[1]
    for ka in range(ad):
        out[ka, :, :width] = dy_refs[ka][...]
        out[ka, :, width:] = (adapter_scale * (mine[ka] + got[ka])).astype(BF16)


def hidden_kernel(fsdp, ad, gslots, first, last, at, *refs):
    own_refs, x_refs, outs, held = refs[:ad], refs[ad : 2 * ad], refs[2 * ad : -1], refs[-1]
    earlier = None
    if not first:
        earlier, outs = outs[0], outs[1:]
    cw = held.shape[2]
    for g in range(held.shape[0] // GROUP):
        weights = held[g * GROUP : (g + 1) * GROUP].reshape(-1, cw)
        rows = pl.ds(g * gslots, gslots)
        for ka in range(ad):
            x = group_rows((own_refs[ka], x_refs[ka]), g, gslots)
            part = narrow(dot(x, weights, ((1,), (1,))), gslots)
            for kf in range(fsdp):
                new = part[kf * gslots : (kf + 1) * gslots]
                if earlier is not None:
                    new = new + earlier[kf, ka, rows, :]
                if not last:
                    outs[0][kf, ka, rows, :] = new
                else:
                    n = new.shape[1] // 2
                    second = at[2] == 1
                    outs[0][kf, ka, rows, :] = jnp.where(second, new[:, n:], new[:, :n])
                    outs[1][kf, ka, rows, :] = jnp.where(second, new[:, :n], new[:, n:])


def down_grad_kernel(fsdp, ad, gslots, at, *refs):
    own_refs, x_refs, back_refs = refs[:ad], refs[ad : 2 * ad], refs[2 * ad : 2 * ad + fsdp]
    outs, total = refs[2 * ad + fsdp : -1], refs[-1]
    rloc = outs[0].shape[1]
    rank = back_refs[0].shape[2]
    for g in range(outs[0].shape[0] // GROUP):
        rows = pl.ds(g * gslots, gslots)
        x = group_rows([r for pair in zip(own_refs, x_refs) for r in pair], g, gslots)
        back = [back_refs[kf][ka, rows, :] for ka in range(ad) for kf in range(fsdp)]
        back = widen(jnp.concatenate(back, axis=0), gslots)
        total[...] = dot(back, x, ((0,), (0,)))
        for r in range(fsdp):
            for e in range(GROUP):
                first = pl.multiple_of(e * rank + at[r] * rloc, rloc)
                outs[r][g * GROUP + e] = total[pl.ds(first, rloc), :].astype(BF16)


def place_kernel(fsdp, at, *refs):
    for r in range(fsdp):

        @pl.when(pl.program_id(0) == r)
        def _():
            refs[-1][...] = refs[r][...].astype(F32)


def delta_kernel(fsdp, ad, gslots, at, own, got, up, *outs):
    for g in range(up.shape[0] // GROUP):
        rows = pl.ds(g * gslots, gslots)
        mine = jnp.concatenate([own[ka, rows, :] for ka in range(ad)], axis=0)
        other = jnp.concatenate([got[ka, rows, :] for ka in range(ad)], axis=0)
        second = at[0] == 1
        low = jnp.where(second, other.astype(F32), mine.astype(F32))
        high = jnp.where(second, mine.astype(F32), other.astype(F32))
        hidden = jnp.concatenate([low, high], axis=1)
        weights = up[g * GROUP : (g + 1) * GROUP].reshape(-1, up.shape[2])
        delta = dot(widen(hidden.astype(BF16), gslots), weights, ((1,), (0,)))
        delta = (adapter_scale * delta).astype(BF16)
        rloc = hidden.shape[1] // fsdp
        for ka in range(ad):
            outs[ka][rows, :] = delta[ka * gslots : (ka + 1) * gslots]
        for kf in range(fsdp):
            part = hidden[:, :rloc]
            for i in range(1, fsdp):
                part = jnp.where(at[1 + kf] == i, hidden[:, i * rloc : (i + 1) * rloc], part)
            part = part.astype(BF16)
            for ka in range(ad):
                outs[ad + kf][ka, rows, :] = part[ka * gslots : (ka + 1) * gslots]


def up_grad_kernel(fsdp, ad, gslots, *refs):
    hid_refs, dy_refs, out = refs[:fsdp], refs[fsdp:-1], refs[-1]
    rloc = hid_refs[0].shape[2]
    for g in range(out.shape[0] // GROUP):
        hid = group_rows(hid_refs, g, gslots)
        dy = group_rows(dy_refs, g, gslots)
        domain = slot_domain(hid.shape[0], rloc, gslots)
        wide = [jnp.where(domain == e, hid.astype(F32), 0.0) for e in range(GROUP)]
        wide = jnp.concatenate(wide, axis=1).astype(BF16)
        total = adapter_scale * dot(wide, dy, ((0,), (0,)))
        for e in range(GROUP):
            out[g * GROUP + e] = total[e * rloc : (e + 1) * rloc]


def output_kernel(fsdp, ad, *refs):
    base, hot, rows, out = refs[:fsdp], refs[fsdp], refs[fsdp + 1 : -1], refs[-1]
    total = base[0][...]
    for k in range(1, fsdp):
        total = total + base[k][...]
    delta = jnp.concatenate([r[...] for r in rows], axis=0)
    out[...] = (total + dot(hot[...], delta, ((0,), (0,)))).astype(BF16)


def base_kernel(fsdp, at, own, mine, got, weight, *outs):
    kt = mine.shape[2]
    outs[0][...] = dot(own[...], weight[...], ((1,), (0,)))
    w_mine = weight[pl.ds(pl.multiple_of(at[0] * kt, kt), kt), :]
    w_got = weight[pl.ds(pl.multiple_of((1 - at[0]) * kt, kt), kt), :]
    for k in range(1, fsdp):
        total = dot(mine[k - 1], w_mine, ((1,), (0,)))
        outs[k][...] = total + dot(got[k - 1], w_got, ((1,), (0,)))


def column_body(
    input_rows,
    value_weight_frozen,
    adapter_down_weight,
    adapter_up_weight,
    layer_output_gradient,
    domain,
):
    fsdp, ad = lax.axis_size("fsdp"), lax.axis_size("ad")
    f, t, a = lax.axis_index("fsdp"), lax.axis_index("tp"), lax.axis_index("ad")
    fy, fx = f // 2, f % 2
    rows, width = input_rows.shape
    dloc, rank, half = adapter_down_weight.shape
    vloc = adapter_up_weight.shape[2]
    rloc = rank // fsdp
    kf_width = width // fsdp
    kt = kf_width // 2
    slots = dloc * CAPD
    gslots = GROUP * CAPD
    cw = kt // CHUNKS

    def over_f(v, k):
        return lax.ppermute(v, "fsdp", [(i, i ^ k) for i in range(fsdp)]) if k else v

    def over_a(v, k):
        return lax.ppermute(v, "ad", [(i, (i + k) % ad) for i in range(ad)]) if k else v

    def swap(v):
        return lax.ppermute(v, "tp", [(0, 1), (1, 0)])

    def numbers(*values):
        return jnp.stack([jnp.asarray(v, jnp.int32) for v in values])

    def after(v, *others):
        return lax.optimization_barrier((v, others))[0]

    x_in = []
    for k in range(fsdp):
        block = lax.dynamic_slice_in_dim(input_rows, (f ^ k) * kf_width + t * kt, kt, 1)
        if k:
            dom_row = jnp.pad(domain.T.astype(BF16), ((0, 15), (0, kt - rows)))
            block = jnp.concatenate([block, dom_row], axis=0)
        x_in.append(block)
    x_in = lax.optimization_barrier(x_in)
    x_in[1], x_in[2] = over_f(x_in[1], 1), over_f(x_in[2], 2)
    x_in[3] = over_f(x_in[3], 3)

    hot, *sends = call(
        functools.partial(own_kernel, ad, slots, ad * dloc),
        [((ad * slots, rows), BF16)] + [((slots, kt + vloc), BF16)] * ad,
        [(v, None) for v in (domain.T, x_in[0], layer_output_gradient)],
        at=numbers(a),
    )
    held = after(adapter_down_weight, *sends)
    sends[-1] = after(sends[-1], x_in[1])
    own = [over_a(v, ka) for ka, v in enumerate(sends)]

    down_other = lax.dynamic_slice_in_dim(held, (fx * 2 + 1 - t) * kt, kt, 2)
    pairs = [(i * 2 + i // 2, i * 2 + 1 - i // 2) for i in range(fsdp)]

    ready, own, down_other = lax.optimization_barrier((x_in[1:], own, down_other))
    *sends, x_plain = call(
        functools.partial(others_kernel, fsdp, ad, slots, ad * dloc),
        [((fsdp - 1, slots, cw), BF16)] * (CHUNKS * ad) + [((fsdp - 1, rows, kt), BF16)],
        [(v, None) for v in ready],
        at=numbers(a),
    )
    x_routed = [[over_a(v, ka) for ka, v in enumerate(sends[:ad])]]

    dy = [(v, (kt, vloc)) for v in after(own, x_plain)]
    (back,) = call(
        functools.partial(back_kernel, ad, gslots),
        [((ad, slots, rank), F32)],
        [*dy, (adapter_up_weight, None)],
    )
    (both,) = call(
        functools.partial(both_kernel, ad),
        [((ad, slots, vloc + rank), BF16)],
        [(back, None), (swap(back), None), *dy],
    )

    down_got = lax.ppermute(after(down_other, both), ("fsdp", "tp"), pairs)

    x_chip = lax.dynamic_slice_in_dim(input_rows, f * kf_width, kf_width, 1)
    x_other = after(swap(x_plain), both, down_got)
    base = call(
        functools.partial(base_kernel, fsdp),
        [((rows, vloc), F32)] * fsdp,
        [(v, None) for v in (x_chip, x_plain, x_other, value_weight_frozen)],
        at=numbers(t),
        flops=20 * fsdp * rows * kt * vloc,
    )
    base_plain = base[0]

    both = [both] * fsdp
    both[1], both[2] = over_f(both[1], 1), over_f(both[2], 2)
    both[3] = over_f(both[3], 3)
    base = [over_f(v, k) for k, v in enumerate(base)]
    for c in range(1, CHUNKS):
        chunk = [after(v, *x_routed[c - 1], *both, base_plain) for v in sends[c * ad : (c + 1) * ad]]
        x_routed.append([over_a(v, ka) for ka, v in enumerate(chunk)])

    def chunk_of(c, routed):
        return [(v, (c * cw, cw)) for v in own] + [(v, None) for v in routed]

    def hidden(c, earlier, routed):
        last = c == CHUNKS - 1
        return call(
            functools.partial(hidden_kernel, fsdp, ad, gslots, c == 0, last),
            [((fsdp, ad, slots, rank // 2 if last else rank), F32)] * (2 if last else 1),
            [*chunk_of(c, routed), *[(v, None) for v in earlier]],
            at=numbers(t == fy, fx * kf_width + t * kt + c * cw, t),
            either=(adapter_down_weight, down_got, (c * cw, cw)),
        )

    grad_a = None
    hid = []
    for c in range(CHUNKS):
        last = c == CHUNKS - 1
        if last:
            hid = hidden(c, hid, x_routed[c])
            hid = hid[0] + swap(hid[1])
            hid, both = lax.optimization_barrier((hid, both))
            hid = [over_f(hid[k], k) for k in range(fsdp)]
        sums = call(
            functools.partial(down_grad_kernel, fsdp, ad, gslots),
            [((dloc, rloc, cw), BF16)] * fsdp,
            [*chunk_of(c, x_routed[c]), *[(v, (vloc, rank)) for v in both]],
            at=numbers(*[(t ^ (r // 2)) * 2 + (fx ^ (r % 2)) for r in range(fsdp)]),
            scratch=[pltpu.VMEM((GROUP * rank, cw), F32)],
        )
        got = []
        if not last:
            hid = hidden(c, hid, after(x_routed[c], x_routed[c + 1][2], *sums))
            sums = [*sums[:2], *after(sums[2:], hid)]
        for r in range(fsdp):
            p, q = r % 2, r // 2
            perm = [
                ((y * 2 + x) * 2 + s, ((s ^ q) * 2 + (x ^ p)) * 2 + y)
                for y in range(2)
                for x in range(2)
                for s in range(2)
            ]
            got.append(lax.ppermute(sums[r], ("fsdp", "tp"), perm))
        at = [
            ((fx ^ (r % 2)) * kf_width + (fy ^ (r // 2)) * kt + c * cw) // cw
            for r in range(fsdp)
        ]
        if c == 0:
            grad_a = pl.pallas_call(
                functools.partial(place_kernel, fsdp),
                out_shape=jax.ShapeDtypeStruct((dloc, rloc, half), F32),
                grid_spec=pltpu.PrefetchScalarGridSpec(
                    num_scalar_prefetch=1,
                    grid=(fsdp,),
                    in_specs=[VMEM] * fsdp,
                    out_specs=pl.BlockSpec((dloc, rloc, cw), lambda i, at: (0, 0, at[i])),
                ),
                cost_estimate=pl.CostEstimate(flops=1, bytes_accessed=1, transcendentals=0),
            )(numbers(*at), *after(got, x_routed[1][1]))
            x_routed[c + 1] = after(x_routed[c + 1], grad_a, *base)
        else:
            for v, column in zip(got, at):
                grad_a = lax.dynamic_update_slice_in_dim(
                    grad_a, v.astype(F32), column * cw, 2
                )

    hid_own = (hid[0] + hid[1] + hid[2] + hid[3]).astype(BF16)
    outs = call(
        functools.partial(delta_kernel, fsdp, ad, gslots),
        [((slots, vloc), BF16)] * ad + [((ad, slots, rloc), BF16)] * fsdp,
        [(v, None) for v in (hid_own, swap(hid_own), adapter_up_weight)],
        at=numbers(t, *[f ^ k for k in range(fsdp)]),
    )
    returned = [over_a(v, (ad - ka) % ad) for ka, v in enumerate(outs[:ad])]
    hid_cols = [over_f(after(v, got[0], got[1]), k) for k, v in enumerate(outs[ad:])]

    (y_out,) = call(
        functools.partial(output_kernel, fsdp, ad),
        [((rows, vloc), BF16)],
        [(v, None) for v in (*base, hot, *returned)],
    )
    (grad_b,) = call(
        functools.partial(up_grad_kernel, fsdp, ad, gslots),
        [((dloc, rloc, vloc), F32)],
        [(v, None) for v in hid_cols] + [(v, (0, vloc)) for v in both],
    )
    return y_out, grad_a, grad_b


def solution(mesh):
    placed = (
        P(("fsdp", "ad"), None),
        P("fsdp", "tp"),
        P("ad", None, "tp"),
        P("ad", None, "tp"),
        P(("fsdp", "ad"), "tp"),
        P(("fsdp", "ad"), None),
    )
    square = mesh.shape["fsdp"] == 4 and mesh.shape["tp"] == 2
    return jax.shard_map(
        column_body if square else general_body,
        mesh=mesh,
        in_specs=placed,
        out_specs=(P(("fsdp", "ad"), "tp"), P("ad", "fsdp", "tp"), P("ad", "fsdp", "tp")),
        check_vma=False,
    )
```

```python
import functools

import jax
import jax.numpy as jnp
from jax import lax
from jax.experimental import pallas as pl
from jax.experimental.pallas import tpu as pltpu
from jax.sharding import PartitionSpec as P

CAPD = 12
GROUP = 4
CHUNKS = 2

adapter_scale = 0.5


def slot_places(dom_ids, dom_total):
    row_count = dom_ids.shape[0]
    onehot = (dom_ids[:, None] == jnp.arange(dom_total, dtype=jnp.int32)[None, :]).astype(
        jnp.float32
    )
    row_iota = jnp.arange(row_count, dtype=jnp.int32)
    earlier = (row_iota[:, None] > row_iota[None, :]).astype(jnp.float32)
    prior = jnp.dot(earlier, onehot, preferred_element_type=jnp.float32)
    position = jnp.sum(prior * onehot, axis=1).astype(jnp.int32)
    return dom_ids * CAPD + position


def general_body(
    input_rows,
    value_weight_frozen,
    adapter_down_weight,
    adapter_up_weight,
    layer_output_gradient,
    domain,
):
    row_count = input_rows.shape[0]
    domain_local = adapter_down_weight.shape[0]
    width_local = adapter_down_weight.shape[2]
    value_width_local = adapter_up_weight.shape[2]
    ad_count = lax.axis_size("ad")
    slot_total = ad_count * domain_local * CAPD
    place = slot_places(domain[:, 0], ad_count * domain_local)
    row_iota = jnp.arange(row_count, dtype=jnp.int32)
    matches = place[None, :] == jnp.arange(slot_total, dtype=jnp.int32)[:, None]
    filled = jnp.any(matches, axis=1)
    source_row = jnp.sum(jnp.where(matches, row_iota[None, :], 0), axis=1)
    base = jnp.dot(
        input_rows,
        lax.all_gather(value_weight_frozen, "fsdp", axis=0, tiled=True),
        preferred_element_type=jnp.float32,
    )
    feature_cols = lax.dynamic_slice_in_dim(
        input_rows, lax.axis_index("tp") * width_local, width_local, 1
    )
    zero_value = jnp.zeros((), jnp.bfloat16)
    send_x = jnp.where(filled[:, None], feature_cols[source_row], zero_value)
    send_dy = jnp.where(filled[:, None], layer_output_gradient[source_row], zero_value)
    send_x = send_x.reshape(ad_count, domain_local * CAPD, width_local)
    send_dy = send_dy.reshape(ad_count, domain_local * CAPD, value_width_local)
    got_x = lax.all_to_all(send_x, "ad", split_axis=0, concat_axis=0, tiled=True)
    got_dy = lax.all_to_all(send_dy, "ad", split_axis=0, concat_axis=0, tiled=True)
    rows = got_x.reshape(ad_count, domain_local, CAPD, width_local)
    grads = got_dy.reshape(ad_count, domain_local, CAPD, value_width_local)
    f32 = dict(preferred_element_type=jnp.float32)
    hidden, back = lax.psum(
        (
            jnp.einsum("vqfj,qwj->vqfw", rows, adapter_down_weight, **f32),
            jnp.einsum("amgy,mzy->amgz", grads, adapter_up_weight, **f32),
        ),
        "tp",
    )
    hidden = hidden.astype(jnp.bfloat16)
    back = (adapter_scale * back).astype(jnp.bfloat16)
    delta = adapter_scale * jnp.einsum("lokh,ohi->loki", hidden, adapter_up_weight, **f32)
    delta = delta.astype(jnp.bfloat16).reshape(ad_count, domain_local * CAPD, value_width_local)
    part_a = jnp.einsum("sdcr,sdcx->drx", back, rows, **f32)
    part_b = adapter_scale * jnp.einsum("sdcr,sdce->dre", hidden, grads, **f32)
    returned = lax.all_to_all(delta, "ad", split_axis=0, concat_axis=0, tiled=True)
    returned = returned.reshape(slot_total, value_width_local)
    y_out = (base + returned[place].astype(jnp.float32)).astype(jnp.bfloat16)
    return (
        y_out,
        lax.psum_scatter(part_a, "fsdp", scatter_dimension=1, tiled=True),
        lax.psum_scatter(part_b, "fsdp", scatter_dimension=1, tiled=True),
    )


BF16, F32 = jnp.bfloat16, jnp.float32
VMEM_BYTES = 58 << 20
VMEM = pl.BlockSpec(memory_space=pltpu.VMEM)
SMEM = pl.BlockSpec(memory_space=pltpu.SMEM)
ANY = pl.BlockSpec(memory_space=pl.ANY)


def dot(lhs, rhs, dims):
    return lax.dot_general(lhs, rhs, (dims, ((), ())), preferred_element_type=F32)


def call(kernel, out_shape, fetched, at=None, scratch=(), either=None, flops=1):
    nf, n_out = len(fetched), len(out_shape)
    shapes = [v.shape[:-1] + (v.shape[-1] if w is None else w[1],) for v, w in fetched]
    sources = [v for v, _ in fetched] + ([] if either is None else list(either[:2]))
    buffers = [pltpu.VMEM(shape, v.dtype) for shape, (v, _) in zip(shapes, fetched)]
    if either is not None:
        lead, width = either[0].shape[:-1], either[2][1]
        buffers.append(pltpu.VMEM(lead + (width,), either[0].dtype))
        buffers.append(pltpu.SemaphoreType.DMA((lead[0],)))

    def body(*refs):
        refs = list(refs)
        head = [refs.pop(0)] if at is not None else []
        froms, refs = refs[: len(sources)], refs[len(sources) :]
        outs, refs = refs[:n_out], refs[n_out:]
        sems, held, extra = refs[0], refs[1 : 1 + len(buffers)], refs[1 + len(buffers) :]
        copies = []
        for i, (source, (_, columns)) in enumerate(zip(froms, fetched)):
            if columns is not None:
                first = (slice(None),) * (len(source.shape) - 1)
                source = source.at[first + (pl.ds(*columns),)]
            copies.append(pltpu.make_async_copy(source, held[i], sems.at[i]))
        for c in copies:
            c.start()
        if either is not None:
            one, other = froms[nf:]
            buffer, more = held[nf], held.pop()
            start = pl.multiple_of(head[0][1], 128)
            parts = [
                pltpu.make_async_copy(one.at[d, :, pl.ds(start, width)], buffer.at[d], more.at[d])
                for d in range(lead[0])
            ]
            others = [
                pltpu.make_async_copy(
                    other.at[d, :, pl.ds(*either[2])], buffer.at[d], more.at[d]
                )
                for d in range(lead[0])
            ]

            @pl.when(head[0][0] == 1)
            def _():
                for c in parts:
                    c.start()

            @pl.when(head[0][0] != 1)
            def _():
                for c in others:
                    c.start()

            copies.extend(others)
        for c in copies:
            c.wait()
        kernel(*head, *held[:nf], *outs, *held[nf:], *extra)

    return pl.pallas_call(
        body,
        out_shape=[jax.ShapeDtypeStruct(shape, dtype) for shape, dtype in out_shape],
        in_specs=[SMEM] * (at is not None) + [ANY] * len(sources),
        out_specs=[VMEM] * n_out,
        scratch_shapes=[pltpu.SemaphoreType.DMA((nf,)), *buffers, *scratch],
        compiler_params=pltpu.CompilerParams(vmem_limit_bytes=VMEM_BYTES),
        cost_estimate=pl.CostEstimate(flops=flops, bytes_accessed=1, transcendentals=0),
    )(*([at] if at is not None else []), *sources)


def slot_domain(count, lanes, gslots):
    slot = lax.broadcasted_iota(jnp.int32, (count, lanes), 0)
    return lax.rem(slot, gslots) // CAPD


def widen(v, gslots):
    domain = slot_domain(*v.shape, gslots)
    parts = [jnp.where(domain == e, v.astype(F32), 0.0).astype(v.dtype) for e in range(GROUP)]
    return jnp.concatenate(parts, axis=1)


def narrow(v, gslots):
    n = v.shape[1] // GROUP
    domain = slot_domain(v.shape[0], n, gslots)
    total = v[:, :n]
    for e in range(1, GROUP):
        total = jnp.where(domain == e, v[:, e * n : (e + 1) * n], total)
    return total


def group_rows(refs, g, gslots):
    rows = pl.ds(g * gslots, gslots)
    parts = []
    for r in refs:
        if len(r.shape) == 2:
            parts.append(r[rows, :])
        else:
            parts.extend(r[i, rows, :] for i in range(r.shape[0]))
    return jnp.concatenate(parts, axis=0)


def one_hot(dom, first, slots, ad, dom_total):
    rows = dom.shape[1]
    names = lax.broadcasted_iota(jnp.int32, (dom_total, rows), 0)
    is_dom = (names == dom).astype(F32)
    before = lax.broadcasted_iota(jnp.int32, (rows, rows), 0) < lax.broadcasted_iota(
        jnp.int32, (rows, rows), 1
    )
    prior = dot(is_dom.astype(BF16), before.astype(F32).astype(BF16), ((1,), (0,)))
    position = jnp.sum(prior * is_dom, axis=0, keepdims=True).astype(jnp.int32)
    slot = lax.broadcasted_iota(jnp.int32, (ad * slots, rows), 0)
    slot = lax.rem(slot + first * slots, ad * slots)
    return (slot == dom * CAPD + position).astype(F32).astype(BF16)


def own_kernel(ad, slots, dom_total, at, dom, x, dy, hot_ref, *outs):
    hot = one_hot(dom[...], at[0], slots, ad, dom_total)
    hot_ref[...] = hot
    width = x.shape[1]
    moved = dot(hot, x[...], ((1,), (0,))).astype(BF16)
    moved_dy = dot(hot, dy[...], ((1,), (0,))).astype(BF16)
    for ka in range(ad):
        outs[ka][:, :width] = moved[ka * slots : (ka + 1) * slots]
        outs[ka][:, width:] = moved_dy[ka * slots : (ka + 1) * slots]


def others_kernel(fsdp, ad, slots, dom_total, at, *refs):
    x_refs, outs = refs[: fsdp - 1], refs[fsdp - 1 :]
    for kf in range(fsdp - 1):
        rows = x_refs[kf].shape[0] - 16
        dom = x_refs[kf][rows:, :rows].astype(F32).astype(jnp.int32)[:1]
        hot = one_hot(dom, at[0], slots, ad, dom_total)
        moved = dot(hot, x_refs[kf][:rows, :], ((1,), (0,))).astype(BF16)
        for c in range(CHUNKS):
            for ka in range(ad):
                cw = outs[c * ad + ka].shape[2]
                part = moved[ka * slots : (ka + 1) * slots, c * cw : (c + 1) * cw]
                outs[c * ad + ka][kf] = part


def back_kernel(ad, gslots, *refs):
    dy_refs, up, out = refs[:ad], refs[ad], refs[ad + 1]
    for g in range(up.shape[0] // GROUP):
        rows = pl.ds(g * gslots, gslots)
        dy = jnp.concatenate([r[rows, :] for r in dy_refs], axis=0)
        weights = up[g * GROUP : (g + 1) * GROUP].reshape(-1, up.shape[2])
        part = narrow(dot(dy, weights, ((1,), (1,))), gslots)
        for ka in range(ad):
            out[ka, rows, :] = part[ka * gslots : (ka + 1) * gslots]


def both_kernel(ad, mine, got, *refs):
    dy_refs, out = refs[:ad], refs[ad]
    width = dy_refs[0].shape[1]
    for ka in range(ad):
        out[ka, :, :width] = dy_refs[ka][...]
        out[ka, :, width:] = (adapter_scale * (mine[ka] + got[ka])).astype(BF16)


def hidden_kernel(fsdp, ad, gslots, first, last, at, *refs):
    own_refs, x_refs, outs, held = refs[:ad], refs[ad : 2 * ad], refs[2 * ad : -1], refs[-1]
    earlier = None
    if not first:
        earlier, outs = outs[0], outs[1:]
    cw = held.shape[2]
    for g in range(held.shape[0] // GROUP):
        weights = held[g * GROUP : (g + 1) * GROUP].reshape(-1, cw)
        rows = pl.ds(g * gslots, gslots)
        for ka in range(ad):
            x = group_rows((own_refs[ka], x_refs[ka]), g, gslots)
            part = narrow(dot(x, weights, ((1,), (1,))), gslots)
            for kf in range(fsdp):
                new = part[kf * gslots : (kf + 1) * gslots]
                if earlier is not None:
                    new = new + earlier[kf, ka, rows, :]
                if not last:
                    outs[0][kf, ka, rows, :] = new
                else:
                    n = new.shape[1] // 2
                    second = at[2] == 1
                    outs[0][kf, ka, rows, :] = jnp.where(second, new[:, n:], new[:, :n])
                    outs[1][kf, ka, rows, :] = jnp.where(second, new[:, :n], new[:, n:])


def down_grad_kernel(fsdp, ad, gslots, at, *refs):
    own_refs, x_refs, back_refs = refs[:ad], refs[ad : 2 * ad], refs[2 * ad : 2 * ad + fsdp]
    outs, total = refs[2 * ad + fsdp : -1], refs[-1]
    rloc = outs[0].shape[1]
    rank = back_refs[0].shape[2]
    for g in range(outs[0].shape[0] // GROUP):
        rows = pl.ds(g * gslots, gslots)
        x = group_rows([r for pair in zip(own_refs, x_refs) for r in pair], g, gslots)
        back = [back_refs[kf][ka, rows, :] for ka in range(ad) for kf in range(fsdp)]
        back = widen(jnp.concatenate(back, axis=0), gslots)
        total[...] = dot(back, x, ((0,), (0,)))
        for r in range(fsdp):
            for e in range(GROUP):
                first = pl.multiple_of(e * rank + at[r] * rloc, rloc)
                outs[r][g * GROUP + e] = total[pl.ds(first, rloc), :].astype(BF16)


def place_kernel(fsdp, at, *refs):
    for r in range(fsdp):

        @pl.when(pl.program_id(0) == r)
        def _():
            refs[-1][...] = refs[r][...].astype(F32)


def delta_kernel(fsdp, ad, gslots, at, own, got, up, *outs):
    for g in range(up.shape[0] // GROUP):
        rows = pl.ds(g * gslots, gslots)
        mine = jnp.concatenate([own[ka, rows, :] for ka in range(ad)], axis=0)
        other = jnp.concatenate([got[ka, rows, :] for ka in range(ad)], axis=0)
        second = at[0] == 1
        low = jnp.where(second, other.astype(F32), mine.astype(F32))
        high = jnp.where(second, mine.astype(F32), other.astype(F32))
        hidden = jnp.concatenate([low, high], axis=1)
        weights = up[g * GROUP : (g + 1) * GROUP].reshape(-1, up.shape[2])
        delta = dot(widen(hidden.astype(BF16), gslots), weights, ((1,), (0,)))
        delta = (adapter_scale * delta).astype(BF16)
        rloc = hidden.shape[1] // fsdp
        for ka in range(ad):
            outs[ka][rows, :] = delta[ka * gslots : (ka + 1) * gslots]
        for kf in range(fsdp):
            part = hidden[:, :rloc]
            for i in range(1, fsdp):
                part = jnp.where(at[1 + kf] == i, hidden[:, i * rloc : (i + 1) * rloc], part)
            part = part.astype(BF16)
            for ka in range(ad):
                outs[ad + kf][ka, rows, :] = part[ka * gslots : (ka + 1) * gslots]


def up_grad_kernel(fsdp, ad, gslots, *refs):
    hid_refs, dy_refs, out = refs[:fsdp], refs[fsdp:-1], refs[-1]
    rloc = hid_refs[0].shape[2]
    for g in range(out.shape[0] // GROUP):
        hid = group_rows(hid_refs, g, gslots)
        dy = group_rows(dy_refs, g, gslots)
        domain = slot_domain(hid.shape[0], rloc, gslots)
        wide = [jnp.where(domain == e, hid.astype(F32), 0.0) for e in range(GROUP)]
        wide = jnp.concatenate(wide, axis=1).astype(BF16)
        total = adapter_scale * dot(wide, dy, ((0,), (0,)))
        for e in range(GROUP):
            out[g * GROUP + e] = total[e * rloc : (e + 1) * rloc]


def output_kernel(fsdp, ad, *refs):
    base, hot, rows, out = refs[:fsdp], refs[fsdp], refs[fsdp + 1 : -1], refs[-1]
    total = base[0][...]
    for k in range(1, fsdp):
        total = total + base[k][...]
    delta = jnp.concatenate([r[...] for r in rows], axis=0)
    out[...] = (total + dot(hot[...], delta, ((0,), (0,)))).astype(BF16)


def base_kernel(fsdp, at, own, *refs):
    mine, got = refs[: fsdp - 1], refs[fsdp - 1 : 2 * fsdp - 2]
    weight, outs = refs[2 * fsdp - 2], refs[2 * fsdp - 1 :]
    rows, kt = own.shape[0], mine[0].shape[1]
    outs[0][...] = dot(own[...], weight[...], ((1,), (0,)))
    w_mine = weight[pl.ds(pl.multiple_of(at[0] * kt, kt), kt), :]
    w_got = weight[pl.ds(pl.multiple_of((1 - at[0]) * kt, kt), kt), :]
    for k in range(1, fsdp):
        total = dot(mine[k - 1][:rows, :], w_mine, ((1,), (0,)))
        outs[k][...] = total + dot(got[k - 1][:rows, :], w_got, ((1,), (0,)))


def column_body(
    input_rows,
    value_weight_frozen,
    adapter_down_weight,
    adapter_up_weight,
    layer_output_gradient,
    domain,
):
    fsdp, ad = lax.axis_size("fsdp"), lax.axis_size("ad")
    f, t, a = lax.axis_index("fsdp"), lax.axis_index("tp"), lax.axis_index("ad")
    fy, fx = f // 2, f % 2
    rows, width = input_rows.shape
    dloc, rank, half = adapter_down_weight.shape
    vloc = adapter_up_weight.shape[2]
    rloc = rank // fsdp
    kf_width = width // fsdp
    kt = kf_width // 2
    slots = dloc * CAPD
    gslots = GROUP * CAPD
    cw = kt // CHUNKS

    def over_f(v, k):
        return lax.ppermute(v, "fsdp", [(i, i ^ k) for i in range(fsdp)]) if k else v

    def over_a(v, k):
        return lax.ppermute(v, "ad", [(i, (i + k) % ad) for i in range(ad)]) if k else v

    def swap(v):
        return lax.ppermute(v, "tp", [(0, 1), (1, 0)])

    def numbers(*values):
        return jnp.stack([jnp.asarray(v, jnp.int32) for v in values])

    def after(v, *others):
        return lax.optimization_barrier((v, others))[0]

    x_in = []
    for k in range(fsdp):
        block = lax.dynamic_slice_in_dim(input_rows, (f ^ k) * kf_width + t * kt, kt, 1)
        if k:
            dom_row = jnp.pad(domain.T.astype(BF16), ((0, 15), (0, kt - rows)))
            block = jnp.concatenate([block, dom_row], axis=0)
        x_in.append(block)
    x_in = lax.optimization_barrier(x_in)
    x_in[1], x_in[2] = over_f(x_in[1], 1), over_f(x_in[2], 2)
    x_in[3] = over_f(x_in[3], 3)

    hot, *sends = call(
        functools.partial(own_kernel, ad, slots, ad * dloc),
        [((ad * slots, rows), BF16)] + [((slots, kt + vloc), BF16)] * ad,
        [(v, None) for v in (domain.T, x_in[0], layer_output_gradient)],
        at=numbers(a),
    )
    held = after((adapter_down_weight, input_rows), *sends)
    sends[-1] = after(sends[-1], x_in[1])
    own = [over_a(v, ka) for ka, v in enumerate(sends)]

    down_other = lax.dynamic_slice_in_dim(held[0], (fx * 2 + 1 - t) * kt, kt, 2)
    pairs = [(i * 2 + i // 2, i * 2 + 1 - i // 2) for i in range(fsdp)]

    x_other = [swap(v) for v in x_in[1:]]
    x_chip = lax.dynamic_slice_in_dim(held[1], f * kf_width, kf_width, 1)
    x_in, x_other, own, down_other, x_chip = lax.optimization_barrier(
        (x_in, x_other, own, down_other, x_chip)
    )
    base = call(
        functools.partial(base_kernel, fsdp),
        [((rows, vloc), F32)] * fsdp,
        [(v, None) for v in (x_chip, *x_in[1:], *x_other, value_weight_frozen)],
        at=numbers(t),
    )
    ready = after(x_in[1:], base[0])
    base = [over_f(v, k) for k, v in enumerate(base)]

    sends = call(
        functools.partial(others_kernel, fsdp, ad, slots, ad * dloc),
        [((fsdp - 1, slots, cw), BF16)] * (CHUNKS * ad),
        [(v, None) for v in ready],
        at=numbers(a),
    )
    x_routed = [[over_a(v, ka) for ka, v in enumerate(sends[:ad])]]

    dy = [(v, (kt, vloc)) for v in after(own, *sends)]
    (back,) = call(
        functools.partial(back_kernel, ad, gslots),
        [((ad, slots, rank), F32)],
        [*dy, (adapter_up_weight, None)],
    )
    back, back_got = after((back, swap(back)), base[1], base[2], x_routed[0][2])
    (both,) = call(
        functools.partial(both_kernel, ad),
        [((ad, slots, vloc + rank), BF16)],
        [(back, None), (back_got, None), *dy],
    )
    down_got = lax.ppermute(after(down_other, both), ("fsdp", "tp"), pairs)
    both = [over_f(both, k) for k in range(fsdp)]
    for c in range(1, CHUNKS):
        chunk = [
            after(v, *x_routed[c - 1], *both, base[3]) for v in sends[c * ad : (c + 1) * ad]
        ]
        x_routed.append([over_a(v, ka) for ka, v in enumerate(chunk)])

    def chunk_of(c, routed):
        return [(v, (c * cw, cw)) for v in own] + [(v, None) for v in routed]

    def hidden(c, earlier, routed):
        last = c == CHUNKS - 1
        return call(
            functools.partial(hidden_kernel, fsdp, ad, gslots, c == 0, last),
            [((fsdp, ad, slots, rank // 2 if last else rank), F32)] * (2 if last else 1),
            [*chunk_of(c, routed), *[(v, None) for v in earlier]],
            at=numbers(t == fy, fx * kf_width + t * kt + c * cw, t),
            either=(adapter_down_weight, down_got, (c * cw, cw)),
        )

    grad_a = None
    hid = []
    for c in range(CHUNKS):
        last = c == CHUNKS - 1
        if last:
            hid = hidden(c, hid, x_routed[c])
            hid, both = lax.optimization_barrier((hid, both))
            hid = hid[0] + swap(hid[1])
        sums = call(
            functools.partial(down_grad_kernel, fsdp, ad, gslots),
            [((dloc, rloc, cw), BF16)] * fsdp,
            [*chunk_of(c, x_routed[c]), *[(v, (vloc, rank)) for v in both]],
            at=numbers(*[(t ^ (r // 2)) * 2 + (fx ^ (r % 2)) for r in range(fsdp)]),
            scratch=[pltpu.VMEM((GROUP * rank, cw), F32)],
            flops=20 * dloc * rank * cw * 192,
        )
        got = []
        if last:
            hid, sums = lax.optimization_barrier((hid, sums))
            hid = [over_f(hid[k], k) for k in range(fsdp)]
        else:
            hid = hidden(c, hid, after(x_routed[c], x_routed[c + 1][2], *sums))
            sums = [*sums[:3], after(sums[3], hid)]
        for r in range(fsdp):
            p, q = r % 2, r // 2
            perm = [
                ((y * 2 + x) * 2 + s, ((s ^ q) * 2 + (x ^ p)) * 2 + y)
                for y in range(2)
                for x in range(2)
                for s in range(2)
            ]
            got.append(lax.ppermute(sums[r], ("fsdp", "tp"), perm))
        at = [
            ((fx ^ (r % 2)) * kf_width + (fy ^ (r // 2)) * kt + c * cw) // cw
            for r in range(fsdp)
        ]
        if c == 0:
            grad_a = pl.pallas_call(
                functools.partial(place_kernel, fsdp),
                out_shape=jax.ShapeDtypeStruct((dloc, rloc, half), F32),
                grid_spec=pltpu.PrefetchScalarGridSpec(
                    num_scalar_prefetch=1,
                    grid=(fsdp,),
                    in_specs=[VMEM] * fsdp,
                    out_specs=pl.BlockSpec((dloc, rloc, cw), lambda i, at: (0, 0, at[i])),
                ),
                cost_estimate=pl.CostEstimate(flops=1, bytes_accessed=1, transcendentals=0),
            )(numbers(*at), *after(got, x_routed[1][1]))
            x_routed[c + 1] = after(x_routed[c + 1], grad_a)
        else:
            for v, column in zip(got, at):
                grad_a = lax.dynamic_update_slice_in_dim(
                    grad_a, v.astype(F32), column * cw, 2
                )

    hid_own = (hid[0] + hid[1] + hid[2] + hid[3]).astype(BF16)
    outs = call(
        functools.partial(delta_kernel, fsdp, ad, gslots),
        [((slots, vloc), BF16)] * ad + [((ad, slots, rloc), BF16)] * fsdp,
        [(v, None) for v in (hid_own, swap(hid_own), adapter_up_weight)],
        at=numbers(t, *[f ^ k for k in range(fsdp)]),
    )
    returned = [over_a(after(v, got[0]), (ad - ka) % ad) for ka, v in enumerate(outs[:ad])]
    hid_cols = [over_f(v, k) for k, v in enumerate(outs[ad:])]

    (y_out,) = call(
        functools.partial(output_kernel, fsdp, ad),
        [((rows, vloc), BF16)],
        [(v, None) for v in (*base, hot, *returned)],
    )
    (grad_b,) = call(
        functools.partial(up_grad_kernel, fsdp, ad, gslots),
        [((dloc, rloc, vloc), F32)],
        [(v, None) for v in hid_cols] + [(v, (0, vloc)) for v in both],
    )
    return y_out, grad_a, grad_b


def solution(mesh):
    placed = (
        P(("fsdp", "ad"), None),
        P("fsdp", "tp"),
        P("ad", None, "tp"),
        P("ad", None, "tp"),
        P(("fsdp", "ad"), "tp"),
        P(("fsdp", "ad"), None),
    )
    square = mesh.shape["fsdp"] == 4 and mesh.shape["tp"] == 2
    return jax.shard_map(
        column_body if square else general_body,
        mesh=mesh,
        in_specs=placed,
        out_specs=(P(("fsdp", "ad"), "tp"), P("ad", "fsdp", "tp"), P("ad", "fsdp", "tp")),
        check_vma=False,
    )
```

```python
import functools

import jax
import jax.numpy as jnp
from jax import lax
from jax.experimental import pallas as pl
from jax.experimental.pallas import tpu as pltpu
from jax.sharding import PartitionSpec as P

CAPD = 12
GROUP = 4
CHUNKS = 1

adapter_scale = 0.5


def slot_places(dom_ids, dom_total):
    row_count = dom_ids.shape[0]
    onehot = (dom_ids[:, None] == jnp.arange(dom_total, dtype=jnp.int32)[None, :]).astype(
        jnp.float32
    )
    row_iota = jnp.arange(row_count, dtype=jnp.int32)
    earlier = (row_iota[:, None] > row_iota[None, :]).astype(jnp.float32)
    prior = jnp.dot(earlier, onehot, preferred_element_type=jnp.float32)
    position = jnp.sum(prior * onehot, axis=1).astype(jnp.int32)
    return dom_ids * CAPD + position


def general_body(
    input_rows,
    value_weight_frozen,
    adapter_down_weight,
    adapter_up_weight,
    layer_output_gradient,
    domain,
):
    row_count = input_rows.shape[0]
    domain_local = adapter_down_weight.shape[0]
    width_local = adapter_down_weight.shape[2]
    value_width_local = adapter_up_weight.shape[2]
    ad_count = lax.axis_size("ad")
    slot_total = ad_count * domain_local * CAPD
    place = slot_places(domain[:, 0], ad_count * domain_local)
    row_iota = jnp.arange(row_count, dtype=jnp.int32)
    matches = place[None, :] == jnp.arange(slot_total, dtype=jnp.int32)[:, None]
    filled = jnp.any(matches, axis=1)
    source_row = jnp.sum(jnp.where(matches, row_iota[None, :], 0), axis=1)
    base = jnp.dot(
        input_rows,
        lax.all_gather(value_weight_frozen, "fsdp", axis=0, tiled=True),
        preferred_element_type=jnp.float32,
    )
    feature_cols = lax.dynamic_slice_in_dim(
        input_rows, lax.axis_index("tp") * width_local, width_local, 1
    )
    zero_value = jnp.zeros((), jnp.bfloat16)
    send_x = jnp.where(filled[:, None], feature_cols[source_row], zero_value)
    send_dy = jnp.where(filled[:, None], layer_output_gradient[source_row], zero_value)
    send_x = send_x.reshape(ad_count, domain_local * CAPD, width_local)
    send_dy = send_dy.reshape(ad_count, domain_local * CAPD, value_width_local)
    got_x = lax.all_to_all(send_x, "ad", split_axis=0, concat_axis=0, tiled=True)
    got_dy = lax.all_to_all(send_dy, "ad", split_axis=0, concat_axis=0, tiled=True)
    rows = got_x.reshape(ad_count, domain_local, CAPD, width_local)
    grads = got_dy.reshape(ad_count, domain_local, CAPD, value_width_local)
    f32 = dict(preferred_element_type=jnp.float32)
    hidden, back = lax.psum(
        (
            jnp.einsum("vqfj,qwj->vqfw", rows, adapter_down_weight, **f32),
            jnp.einsum("amgy,mzy->amgz", grads, adapter_up_weight, **f32),
        ),
        "tp",
    )
    hidden = hidden.astype(jnp.bfloat16)
    back = (adapter_scale * back).astype(jnp.bfloat16)
    delta = adapter_scale * jnp.einsum("lokh,ohi->loki", hidden, adapter_up_weight, **f32)
    delta = delta.astype(jnp.bfloat16).reshape(ad_count, domain_local * CAPD, value_width_local)
    part_a = jnp.einsum("sdcr,sdcx->drx", back, rows, **f32)
    part_b = adapter_scale * jnp.einsum("sdcr,sdce->dre", hidden, grads, **f32)
    returned = lax.all_to_all(delta, "ad", split_axis=0, concat_axis=0, tiled=True)
    returned = returned.reshape(slot_total, value_width_local)
    y_out = (base + returned[place].astype(jnp.float32)).astype(jnp.bfloat16)
    return (
        y_out,
        lax.psum_scatter(part_a, "fsdp", scatter_dimension=1, tiled=True),
        lax.psum_scatter(part_b, "fsdp", scatter_dimension=1, tiled=True),
    )


BF16, F32 = jnp.bfloat16, jnp.float32
VMEM_BYTES = 58 << 20
VMEM = pl.BlockSpec(memory_space=pltpu.VMEM)
SMEM = pl.BlockSpec(memory_space=pltpu.SMEM)
ANY = pl.BlockSpec(memory_space=pl.ANY)


def dot(lhs, rhs, dims):
    return lax.dot_general(lhs, rhs, (dims, ((), ())), preferred_element_type=F32)


def call(kernel, out_shape, fetched, at=None, scratch=(), either=None, flops=1):
    nf, n_out = len(fetched), len(out_shape)
    shapes = [v.shape[:-1] + (v.shape[-1] if w is None else w[1],) for v, w in fetched]
    sources = [v for v, _ in fetched] + ([] if either is None else list(either[:2]))
    buffers = [pltpu.VMEM(shape, v.dtype) for shape, (v, _) in zip(shapes, fetched)]
    if either is not None:
        lead, width = either[0].shape[:-1], either[2][1]
        buffers.append(pltpu.VMEM(lead + (width,), either[0].dtype))
        buffers.append(pltpu.SemaphoreType.DMA((lead[0],)))

    def body(*refs):
        refs = list(refs)
        head = [refs.pop(0)] if at is not None else []
        froms, refs = refs[: len(sources)], refs[len(sources) :]
        outs, refs = refs[:n_out], refs[n_out:]
        sems, held, extra = refs[0], refs[1 : 1 + len(buffers)], refs[1 + len(buffers) :]
        copies = []
        for i, (source, (_, columns)) in enumerate(zip(froms, fetched)):
            if columns is not None:
                first = (slice(None),) * (len(source.shape) - 1)
                source = source.at[first + (pl.ds(*columns),)]
            copies.append(pltpu.make_async_copy(source, held[i], sems.at[i]))
        for c in copies:
            c.start()
        if either is not None:
            one, other = froms[nf:]
            buffer, more = held[nf], held.pop()
            start = pl.multiple_of(head[0][1], 128)
            parts = [
                pltpu.make_async_copy(one.at[d, :, pl.ds(start, width)], buffer.at[d], more.at[d])
                for d in range(lead[0])
            ]
            others = [
                pltpu.make_async_copy(
                    other.at[d, :, pl.ds(*either[2])], buffer.at[d], more.at[d]
                )
                for d in range(lead[0])
            ]

            @pl.when(head[0][0] == 1)
            def _():
                for c in parts:
                    c.start()

            @pl.when(head[0][0] != 1)
            def _():
                for c in others:
                    c.start()

            copies.extend(others)
        for c in copies:
            c.wait()
        kernel(*head, *held[:nf], *outs, *held[nf:], *extra)

    return pl.pallas_call(
        body,
        out_shape=[jax.ShapeDtypeStruct(shape, dtype) for shape, dtype in out_shape],
        in_specs=[SMEM] * (at is not None) + [ANY] * len(sources),
        out_specs=[VMEM] * n_out,
        scratch_shapes=[pltpu.SemaphoreType.DMA((nf,)), *buffers, *scratch],
        compiler_params=pltpu.CompilerParams(vmem_limit_bytes=VMEM_BYTES),
        cost_estimate=pl.CostEstimate(flops=flops, bytes_accessed=1, transcendentals=0),
    )(*([at] if at is not None else []), *sources)


def slot_domain(count, lanes, gslots):
    slot = lax.broadcasted_iota(jnp.int32, (count, lanes), 0)
    return lax.rem(slot, gslots) // CAPD


def widen(v, gslots):
    domain = slot_domain(*v.shape, gslots)
    parts = [jnp.where(domain == e, v.astype(F32), 0.0).astype(v.dtype) for e in range(GROUP)]
    return jnp.concatenate(parts, axis=1)


def narrow(v, gslots):
    n = v.shape[1] // GROUP
    domain = slot_domain(v.shape[0], n, gslots)
    total = v[:, :n]
    for e in range(1, GROUP):
        total = jnp.where(domain == e, v[:, e * n : (e + 1) * n], total)
    return total


def group_rows(refs, g, gslots):
    rows = pl.ds(g * gslots, gslots)
    parts = []
    for r in refs:
        if len(r.shape) == 2:
            parts.append(r[rows, :])
        else:
            parts.extend(r[i, rows, :] for i in range(r.shape[0]))
    return jnp.concatenate(parts, axis=0)


def one_hot(dom, first, slots, ad, dom_total):
    rows = dom.shape[1]
    names = lax.broadcasted_iota(jnp.int32, (dom_total, rows), 0)
    is_dom = (names == dom).astype(F32)
    before = lax.broadcasted_iota(jnp.int32, (rows, rows), 0) < lax.broadcasted_iota(
        jnp.int32, (rows, rows), 1
    )
    prior = dot(is_dom.astype(BF16), before.astype(F32).astype(BF16), ((1,), (0,)))
    position = jnp.sum(prior * is_dom, axis=0, keepdims=True).astype(jnp.int32)
    slot = lax.broadcasted_iota(jnp.int32, (ad * slots, rows), 0)
    slot = lax.rem(slot + first * slots, ad * slots)
    return (slot == dom * CAPD + position).astype(F32).astype(BF16)


def own_kernel(ad, slots, dom_total, at, dom, x, dy, hot_ref, *outs):
    hot = one_hot(dom[...], at[0], slots, ad, dom_total)
    hot_ref[...] = hot
    width = x.shape[1]
    moved = dot(hot, x[...], ((1,), (0,))).astype(BF16)
    moved_dy = dot(hot, dy[...], ((1,), (0,))).astype(BF16)
    for ka in range(ad):
        outs[ka][:, :width] = moved[ka * slots : (ka + 1) * slots]
        outs[ka][:, width:] = moved_dy[ka * slots : (ka + 1) * slots]


def others_kernel(fsdp, ad, slots, dom_total, at, *refs):
    x_refs, outs, plain = refs[: fsdp - 1], refs[fsdp - 1 : -1], refs[-1]
    for kf in range(fsdp - 1):
        rows = x_refs[kf].shape[0] - 16
        plain[kf] = x_refs[kf][:rows, :]
        dom = x_refs[kf][rows:, :rows].astype(F32).astype(jnp.int32)[:1]
        hot = one_hot(dom, at[0], slots, ad, dom_total)
        moved = dot(hot, x_refs[kf][:rows, :], ((1,), (0,))).astype(BF16)
        for c in range(CHUNKS):
            for ka in range(ad):
                cw = outs[c * ad + ka].shape[2]
                part = moved[ka * slots : (ka + 1) * slots, c * cw : (c + 1) * cw]
                outs[c * ad + ka][kf] = part


def back_kernel(ad, gslots, *refs):
    dy_refs, up, out = refs[:ad], refs[ad], refs[ad + 1]
    for g in range(up.shape[0] // GROUP):
        rows = pl.ds(g * gslots, gslots)
        dy = jnp.concatenate([r[rows, :] for r in dy_refs], axis=0)
        weights = up[g * GROUP : (g + 1) * GROUP].reshape(-1, up.shape[2])
        part = narrow(dot(dy, weights, ((1,), (1,))), gslots)
        for ka in range(ad):
            out[ka, rows, :] = part[ka * gslots : (ka + 1) * gslots]


def both_kernel(ad, mine, got, *refs):
    dy_refs, out = refs[:ad], refs[ad]
    width = dy_refs[0].shape[1]
    for ka in range(ad):
        out[ka, :, :width] = dy_refs[ka][...]
        out[ka, :, width:] = (adapter_scale * (mine[ka] + got[ka])).astype(BF16)


def hidden_kernel(fsdp, ad, gslots, first, last, at, *refs):
    own_refs, x_refs, outs, held = refs[:ad], refs[ad : 2 * ad], refs[2 * ad : -1], refs[-1]
    earlier = None
    if not first:
        earlier, outs = outs[0], outs[1:]
    cw = held.shape[2]
    for g in range(held.shape[0] // GROUP):
        weights = held[g * GROUP : (g + 1) * GROUP].reshape(-1, cw)
        rows = pl.ds(g * gslots, gslots)
        for ka in range(ad):
            x = group_rows((own_refs[ka], x_refs[ka]), g, gslots)
            part = narrow(dot(x, weights, ((1,), (1,))), gslots)
            for kf in range(fsdp):
                new = part[kf * gslots : (kf + 1) * gslots]
                if earlier is not None:
                    new = new + earlier[kf, ka, rows, :]
                if not last:
                    outs[0][kf, ka, rows, :] = new
                else:
                    n = new.shape[1] // 2
                    second = at[2] == 1
                    outs[0][kf, ka, rows, :] = jnp.where(second, new[:, n:], new[:, :n])
                    outs[1][kf, ka, rows, :] = jnp.where(second, new[:, :n], new[:, n:])


def down_grad_kernel(fsdp, ad, gslots, at, *refs):
    own_refs, x_refs, back_refs = refs[:ad], refs[ad : 2 * ad], refs[2 * ad : 2 * ad + fsdp]
    outs, total = refs[2 * ad + fsdp : -1], refs[-1]
    rloc = outs[0].shape[1]
    rank = back_refs[0].shape[2]
    for g in range(outs[0].shape[0] // GROUP):
        rows = pl.ds(g * gslots, gslots)
        x = group_rows([r for pair in zip(own_refs, x_refs) for r in pair], g, gslots)
        back = [back_refs[kf][ka, rows, :] for ka in range(ad) for kf in range(fsdp)]
        back = widen(jnp.concatenate(back, axis=0), gslots)
        total[...] = dot(back, x, ((0,), (0,)))
        for r in range(fsdp):
            for e in range(GROUP):
                first = pl.multiple_of(e * rank + at[r] * rloc, rloc)
                outs[r][g * GROUP + e] = total[pl.ds(first, rloc), :].astype(BF16)


def delta_kernel(fsdp, ad, gslots, at, own, got, up, *outs):
    for g in range(up.shape[0] // GROUP):
        rows = pl.ds(g * gslots, gslots)
        mine = jnp.concatenate([own[ka, rows, :] for ka in range(ad)], axis=0)
        other = jnp.concatenate([got[ka, rows, :] for ka in range(ad)], axis=0)
        second = at[0] == 1
        low = jnp.where(second, other.astype(F32), mine.astype(F32))
        high = jnp.where(second, mine.astype(F32), other.astype(F32))
        hidden = jnp.concatenate([low, high], axis=1)
        weights = up[g * GROUP : (g + 1) * GROUP].reshape(-1, up.shape[2])
        delta = dot(widen(hidden.astype(BF16), gslots), weights, ((1,), (0,)))
        delta = (adapter_scale * delta).astype(BF16)
        rloc = hidden.shape[1] // fsdp
        for ka in range(ad):
            outs[ka][rows, :] = delta[ka * gslots : (ka + 1) * gslots]
        for kf in range(fsdp):
            part = hidden[:, :rloc]
            for i in range(1, fsdp):
                part = jnp.where(at[1 + kf] == i, hidden[:, i * rloc : (i + 1) * rloc], part)
            part = part.astype(BF16)
            for ka in range(ad):
                outs[ad + kf][ka, rows, :] = part[ka * gslots : (ka + 1) * gslots]


def up_grad_kernel(fsdp, ad, gslots, *refs):
    hid_refs, dy_refs, out = refs[:fsdp], refs[fsdp:-1], refs[-1]
    rloc = hid_refs[0].shape[2]
    for g in range(out.shape[0] // GROUP):
        hid = group_rows(hid_refs, g, gslots)
        dy = group_rows(dy_refs, g, gslots)
        domain = slot_domain(hid.shape[0], rloc, gslots)
        wide = [jnp.where(domain == e, hid.astype(F32), 0.0) for e in range(GROUP)]
        wide = jnp.concatenate(wide, axis=1).astype(BF16)
        total = adapter_scale * dot(wide, dy, ((0,), (0,)))
        for e in range(GROUP):
            out[g * GROUP + e] = total[e * rloc : (e + 1) * rloc]


def output_kernel(fsdp, ad, *refs):
    base, hot, rows, out = refs[:fsdp], refs[fsdp], refs[fsdp + 1 : -1], refs[-1]
    total = base[0][...]
    for k in range(1, fsdp):
        total = total + base[k][...]
    delta = jnp.concatenate([r[...] for r in rows], axis=0)
    out[...] = (total + dot(hot[...], delta, ((0,), (0,)))).astype(BF16)


def base_kernel(fsdp, at, own, mine, got, weight, *outs):
    kt = mine.shape[2]
    outs[0][...] = dot(own[...], weight[...], ((1,), (0,)))
    w_mine = weight[pl.ds(pl.multiple_of(at[0] * kt, kt), kt), :]
    w_got = weight[pl.ds(pl.multiple_of((1 - at[0]) * kt, kt), kt), :]
    for k in range(1, fsdp):
        total = dot(mine[k - 1], w_mine, ((1,), (0,)))
        outs[k][...] = total + dot(got[k - 1], w_got, ((1,), (0,)))


def column_body(
    input_rows,
    value_weight_frozen,
    adapter_down_weight,
    adapter_up_weight,
    layer_output_gradient,
    domain,
):
    fsdp, ad = lax.axis_size("fsdp"), lax.axis_size("ad")
    f, t, a = lax.axis_index("fsdp"), lax.axis_index("tp"), lax.axis_index("ad")
    fy, fx = f // 2, f % 2
    rows, width = input_rows.shape
    dloc, rank, half = adapter_down_weight.shape
    vloc = adapter_up_weight.shape[2]
    rloc = rank // fsdp
    kf_width = width // fsdp
    kt = kf_width // 2
    slots = dloc * CAPD
    gslots = GROUP * CAPD
    cw = kt // CHUNKS

    def over_f(v, k):
        return lax.ppermute(v, "fsdp", [(i, i ^ k) for i in range(fsdp)]) if k else v

    def over_a(v, k):
        return lax.ppermute(v, "ad", [(i, (i + k) % ad) for i in range(ad)]) if k else v

    def swap(v):
        return lax.ppermute(v, "tp", [(0, 1), (1, 0)])

    def numbers(*values):
        return jnp.stack([jnp.asarray(v, jnp.int32) for v in values])

    def after(v, *others):
        return lax.optimization_barrier((v, others))[0]

    x_in = []
    for k in range(fsdp):
        block = lax.dynamic_slice_in_dim(input_rows, (f ^ k) * kf_width + t * kt, kt, 1)
        if k:
            dom_row = jnp.pad(domain.T.astype(BF16), ((0, 15), (0, kt - rows)))
            block = jnp.concatenate([block, dom_row], axis=0)
        x_in.append(block)
    x_in = lax.optimization_barrier(x_in)
    x_in[1], x_in[2] = over_f(x_in[1], 1), over_f(x_in[2], 2)
    x_in[3] = over_f(x_in[3], 3)

    hot, *sends = call(
        functools.partial(own_kernel, ad, slots, ad * dloc),
        [((ad * slots, rows), BF16)] + [((slots, kt + vloc), BF16)] * ad,
        [(v, None) for v in (domain.T, x_in[0], layer_output_gradient)],
        at=numbers(a),
    )
    held = after(adapter_down_weight, *sends)
    sends[-1] = after(sends[-1], x_in[1])
    own = [over_a(v, ka) for ka, v in enumerate(sends)]

    down_other = lax.dynamic_slice_in_dim(held, (fx * 2 + 1 - t) * kt, kt, 2)
    pairs = [(i * 2 + i // 2, i * 2 + 1 - i // 2) for i in range(fsdp)]

    ready, own, down_other = lax.optimization_barrier((x_in[1:], own, down_other))
    *sends, x_plain = call(
        functools.partial(others_kernel, fsdp, ad, slots, ad * dloc),
        [((fsdp - 1, slots, cw), BF16)] * (CHUNKS * ad) + [((fsdp - 1, rows, kt), BF16)],
        [(v, None) for v in ready],
        at=numbers(a),
    )
    x_routed = [[over_a(v, ka) for ka, v in enumerate(sends[:ad])]]

    dy = [(v, (kt, vloc)) for v in after(own, x_plain)]
    (back,) = call(
        functools.partial(back_kernel, ad, gslots),
        [((ad, slots, rank), F32)],
        [*dy, (adapter_up_weight, None)],
    )
    x_other = swap(x_plain)
    back, back_got = after((back, swap(back)), x_other)
    (both,) = call(
        functools.partial(both_kernel, ad),
        [((ad, slots, vloc + rank), BF16)],
        [(back, None), (back_got, None), *dy],
    )
    down_got = lax.ppermute(after(down_other, both), ("fsdp", "tp"), pairs)
    both = [over_f(both, k) for k in range(fsdp)]

    x_chip = lax.dynamic_slice_in_dim(input_rows, f * kf_width, kf_width, 1)
    x_chip = after(x_chip, x_routed[0][2], *both, down_got)
    base = call(
        functools.partial(base_kernel, fsdp),
        [((rows, vloc), F32)] * fsdp,
        [(v, None) for v in (x_chip, x_plain, x_other, value_weight_frozen)],
        at=numbers(t),
    )
    base = [over_f(v, k) for k, v in enumerate(base)]
    x_routed[0] = after(x_routed[0], *base)

    def chunk_of(c, routed):
        return [(v, (c * cw, cw)) for v in own] + [(v, None) for v in routed]

    def hidden(c, earlier, routed):
        last = c == CHUNKS - 1
        return call(
            functools.partial(hidden_kernel, fsdp, ad, gslots, c == 0, last),
            [((fsdp, ad, slots, rank // 2 if last else rank), F32)] * (2 if last else 1),
            [*chunk_of(c, routed), *[(v, None) for v in earlier]],
            at=numbers(t == fy, fx * kf_width + t * kt + c * cw, t),
            either=(adapter_down_weight, down_got, (c * cw, cw)),
        )

    hid = hidden(0, [], x_routed[0])
    hid, both = lax.optimization_barrier((hid, both))
    hid = hid[0] + swap(hid[1])

    sums = call(
        functools.partial(down_grad_kernel, fsdp, ad, gslots),
        [((dloc, rloc, kt), BF16)] * fsdp,
        [*chunk_of(0, x_routed[0]), *[(v, (vloc, rank)) for v in both]],
        at=numbers(*[(t ^ (r // 2)) * 2 + (fx ^ (r % 2)) for r in range(fsdp)]),
        scratch=[pltpu.VMEM((GROUP * rank, kt), F32)],
        flops=20 * dloc * rank * kt * 192,
    )
    hid, sums = lax.optimization_barrier((hid, sums))
    hid = [over_f(hid[k], k) for k in range(fsdp)]
    grad_a = jnp.zeros((dloc, rloc, half), F32)
    for r in range(fsdp):
        p, q = r % 2, r // 2
        perm = [
            ((y * 2 + x) * 2 + s, ((s ^ q) * 2 + (x ^ p)) * 2 + y)
            for y in range(2)
            for x in range(2)
            for s in range(2)
        ]
        got = lax.ppermute(sums[r], ("fsdp", "tp"), perm)
        at = (fx ^ p) * kf_width + (fy ^ q) * kt
        grad_a = lax.dynamic_update_slice_in_dim(grad_a, got.astype(F32), at, 2)

    hid_own = (hid[0] + hid[1] + hid[2] + hid[3]).astype(BF16)
    outs = call(
        functools.partial(delta_kernel, fsdp, ad, gslots),
        [((slots, vloc), BF16)] * ad + [((ad, slots, rloc), BF16)] * fsdp,
        [(v, None) for v in (hid_own, swap(hid_own), adapter_up_weight)],
        at=numbers(t, *[f ^ k for k in range(fsdp)]),
    )
    returned = [over_a(v, (ad - ka) % ad) for ka, v in enumerate(outs[:ad])]
    hid_cols = [over_f(v, k) for k, v in enumerate(outs[ad:])]

    (y_out,) = call(
        functools.partial(output_kernel, fsdp, ad),
        [((rows, vloc), BF16)],
        [(v, None) for v in (*base, hot, *returned)],
    )
    (grad_b,) = call(
        functools.partial(up_grad_kernel, fsdp, ad, gslots),
        [((dloc, rloc, vloc), F32)],
        [(v, None) for v in hid_cols] + [(v, (0, vloc)) for v in both],
    )
    return y_out, grad_a, grad_b


def solution(mesh):
    placed = (
        P(("fsdp", "ad"), None),
        P("fsdp", "tp"),
        P("ad", None, "tp"),
        P("ad", None, "tp"),
        P(("fsdp", "ad"), "tp"),
        P(("fsdp", "ad"), None),
    )
    square = mesh.shape["fsdp"] == 4 and mesh.shape["tp"] == 2
    return jax.shard_map(
        column_body if square else general_body,
        mesh=mesh,
        in_specs=placed,
        out_specs=(P(("fsdp", "ad"), "tp"), P("ad", "fsdp", "tp"), P("ad", "fsdp", "tp")),
        check_vma=False,
    )
```

```python
import functools

import jax
import jax.numpy as jnp
from jax import lax
from jax.experimental import pallas as pl
from jax.experimental.pallas import tpu as pltpu
from jax.sharding import PartitionSpec as P

CAPD = 12
GROUP = 4
CHUNKS = 1

adapter_scale = 0.5


def slot_places(dom_ids, dom_total):
    row_count = dom_ids.shape[0]
    onehot = (dom_ids[:, None] == jnp.arange(dom_total, dtype=jnp.int32)[None, :]).astype(
        jnp.float32
    )
    row_iota = jnp.arange(row_count, dtype=jnp.int32)
    earlier = (row_iota[:, None] > row_iota[None, :]).astype(jnp.float32)
    prior = jnp.dot(earlier, onehot, preferred_element_type=jnp.float32)
    position = jnp.sum(prior * onehot, axis=1).astype(jnp.int32)
    return dom_ids * CAPD + position


def general_body(
    input_rows,
    value_weight_frozen,
    adapter_down_weight,
    adapter_up_weight,
    layer_output_gradient,
    domain,
):
    row_count = input_rows.shape[0]
    domain_local = adapter_down_weight.shape[0]
    width_local = adapter_down_weight.shape[2]
    value_width_local = adapter_up_weight.shape[2]
    ad_count = lax.axis_size("ad")
    slot_total = ad_count * domain_local * CAPD
    place = slot_places(domain[:, 0], ad_count * domain_local)
    row_iota = jnp.arange(row_count, dtype=jnp.int32)
    matches = place[None, :] == jnp.arange(slot_total, dtype=jnp.int32)[:, None]
    filled = jnp.any(matches, axis=1)
    source_row = jnp.sum(jnp.where(matches, row_iota[None, :], 0), axis=1)
    base = jnp.dot(
        input_rows,
        lax.all_gather(value_weight_frozen, "fsdp", axis=0, tiled=True),
        preferred_element_type=jnp.float32,
    )
    feature_cols = lax.dynamic_slice_in_dim(
        input_rows, lax.axis_index("tp") * width_local, width_local, 1
    )
    zero_value = jnp.zeros((), jnp.bfloat16)
    send_x = jnp.where(filled[:, None], feature_cols[source_row], zero_value)
    send_dy = jnp.where(filled[:, None], layer_output_gradient[source_row], zero_value)
    send_x = send_x.reshape(ad_count, domain_local * CAPD, width_local)
    send_dy = send_dy.reshape(ad_count, domain_local * CAPD, value_width_local)
    got_x = lax.all_to_all(send_x, "ad", split_axis=0, concat_axis=0, tiled=True)
    got_dy = lax.all_to_all(send_dy, "ad", split_axis=0, concat_axis=0, tiled=True)
    rows = got_x.reshape(ad_count, domain_local, CAPD, width_local)
    grads = got_dy.reshape(ad_count, domain_local, CAPD, value_width_local)
    f32 = dict(preferred_element_type=jnp.float32)
    hidden, back = lax.psum(
        (
            jnp.einsum("vqfj,qwj->vqfw", rows, adapter_down_weight, **f32),
            jnp.einsum("amgy,mzy->amgz", grads, adapter_up_weight, **f32),
        ),
        "tp",
    )
    hidden = hidden.astype(jnp.bfloat16)
    back = (adapter_scale * back).astype(jnp.bfloat16)
    delta = adapter_scale * jnp.einsum("lokh,ohi->loki", hidden, adapter_up_weight, **f32)
    delta = delta.astype(jnp.bfloat16).reshape(ad_count, domain_local * CAPD, value_width_local)
    part_a = jnp.einsum("sdcr,sdcx->drx", back, rows, **f32)
    part_b = adapter_scale * jnp.einsum("sdcr,sdce->dre", hidden, grads, **f32)
    returned = lax.all_to_all(delta, "ad", split_axis=0, concat_axis=0, tiled=True)
    returned = returned.reshape(slot_total, value_width_local)
    y_out = (base + returned[place].astype(jnp.float32)).astype(jnp.bfloat16)
    return (
        y_out,
        lax.psum_scatter(part_a, "fsdp", scatter_dimension=1, tiled=True),
        lax.psum_scatter(part_b, "fsdp", scatter_dimension=1, tiled=True),
    )


BF16, F32 = jnp.bfloat16, jnp.float32
VMEM_BYTES = 58 << 20
VMEM = pl.BlockSpec(memory_space=pltpu.VMEM)
SMEM = pl.BlockSpec(memory_space=pltpu.SMEM)
ANY = pl.BlockSpec(memory_space=pl.ANY)


def dot(lhs, rhs, dims):
    return lax.dot_general(lhs, rhs, (dims, ((), ())), preferred_element_type=F32)


def call(kernel, out_shape, fetched, at=None, scratch=(), either=None, flops=1):
    nf, n_out = len(fetched), len(out_shape)
    shapes = [v.shape[:-1] + (v.shape[-1] if w is None else w[1],) for v, w in fetched]
    sources = [v for v, _ in fetched] + ([] if either is None else list(either[:2]))
    buffers = [pltpu.VMEM(shape, v.dtype) for shape, (v, _) in zip(shapes, fetched)]
    if either is not None:
        lead, width = either[0].shape[:-1], either[2][1]
        buffers.append(pltpu.VMEM(lead + (width,), either[0].dtype))
        buffers.append(pltpu.SemaphoreType.DMA((lead[0],)))

    def body(*refs):
        refs = list(refs)
        head = [refs.pop(0)] if at is not None else []
        froms, refs = refs[: len(sources)], refs[len(sources) :]
        outs, refs = refs[:n_out], refs[n_out:]
        sems, held, extra = refs[0], refs[1 : 1 + len(buffers)], refs[1 + len(buffers) :]
        copies = []
        for i, (source, (_, columns)) in enumerate(zip(froms, fetched)):
            if columns is not None:
                first = (slice(None),) * (len(source.shape) - 1)
                source = source.at[first + (pl.ds(*columns),)]
            copies.append(pltpu.make_async_copy(source, held[i], sems.at[i]))
        for c in copies:
            c.start()
        if either is not None:
            one, other = froms[nf:]
            buffer, more = held[nf], held.pop()
            start = pl.multiple_of(head[0][1], 128)
            parts = [
                pltpu.make_async_copy(one.at[d, :, pl.ds(start, width)], buffer.at[d], more.at[d])
                for d in range(lead[0])
            ]
            others = [
                pltpu.make_async_copy(
                    other.at[d, :, pl.ds(*either[2])], buffer.at[d], more.at[d]
                )
                for d in range(lead[0])
            ]

            @pl.when(head[0][0] == 1)
            def _():
                for c in parts:
                    c.start()

            @pl.when(head[0][0] != 1)
            def _():
                for c in others:
                    c.start()

            copies.extend(others)
        for c in copies:
            c.wait()
        kernel(*head, *held[:nf], *outs, *held[nf:], *extra)

    return pl.pallas_call(
        body,
        out_shape=[jax.ShapeDtypeStruct(shape, dtype) for shape, dtype in out_shape],
        in_specs=[SMEM] * (at is not None) + [ANY] * len(sources),
        out_specs=[VMEM] * n_out,
        scratch_shapes=[pltpu.SemaphoreType.DMA((nf,)), *buffers, *scratch],
        compiler_params=pltpu.CompilerParams(vmem_limit_bytes=VMEM_BYTES),
        cost_estimate=pl.CostEstimate(flops=flops, bytes_accessed=1, transcendentals=0),
    )(*([at] if at is not None else []), *sources)


def slot_domain(count, lanes, gslots):
    slot = lax.broadcasted_iota(jnp.int32, (count, lanes), 0)
    return lax.rem(slot, gslots) // CAPD


def widen(v, gslots):
    domain = slot_domain(*v.shape, gslots)
    parts = [jnp.where(domain == e, v.astype(F32), 0.0).astype(v.dtype) for e in range(GROUP)]
    return jnp.concatenate(parts, axis=1)


def narrow(v, gslots):
    n = v.shape[1] // GROUP
    domain = slot_domain(v.shape[0], n, gslots)
    total = v[:, :n]
    for e in range(1, GROUP):
        total = jnp.where(domain == e, v[:, e * n : (e + 1) * n], total)
    return total


def group_rows(refs, g, gslots):
    rows = pl.ds(g * gslots, gslots)
    parts = []
    for r in refs:
        if len(r.shape) == 2:
            parts.append(r[rows, :])
        else:
            parts.extend(r[i, rows, :] for i in range(r.shape[0]))
    return jnp.concatenate(parts, axis=0)


def one_hot(dom, first, slots, ad, dom_total):
    rows = dom.shape[1]
    names = lax.broadcasted_iota(jnp.int32, (dom_total, rows), 0)
    is_dom = (names == dom).astype(F32)
    before = lax.broadcasted_iota(jnp.int32, (rows, rows), 0) < lax.broadcasted_iota(
        jnp.int32, (rows, rows), 1
    )
    prior = dot(is_dom.astype(BF16), before.astype(F32).astype(BF16), ((1,), (0,)))
    position = jnp.sum(prior * is_dom, axis=0, keepdims=True).astype(jnp.int32)
    slot = lax.broadcasted_iota(jnp.int32, (ad * slots, rows), 0)
    slot = lax.rem(slot + first * slots, ad * slots)
    return (slot == dom * CAPD + position).astype(F32).astype(BF16)


def own_kernel(ad, slots, dom_total, at, dom, x, dy, hot_ref, *outs):
    hot = one_hot(dom[...], at[0], slots, ad, dom_total)
    hot_ref[...] = hot
    width = x.shape[1]
    moved = dot(hot, x[...], ((1,), (0,))).astype(BF16)
    moved_dy = dot(hot, dy[...], ((1,), (0,))).astype(BF16)
    for ka in range(ad):
        outs[ka][:, :width] = moved[ka * slots : (ka + 1) * slots]
        outs[ka][:, width:] = moved_dy[ka * slots : (ka + 1) * slots]


def others_kernel(fsdp, ad, slots, dom_total, at, *refs):
    x_refs, outs = refs[: fsdp - 1], refs[fsdp - 1 :]
    for kf in range(fsdp - 1):
        rows = x_refs[kf].shape[0] - 16
        dom = x_refs[kf][rows:, :rows].astype(F32).astype(jnp.int32)[:1]
        hot = one_hot(dom, at[0], slots, ad, dom_total)
        moved = dot(hot, x_refs[kf][:rows, :], ((1,), (0,))).astype(BF16)
        for c in range(CHUNKS):
            for ka in range(ad):
                cw = outs[c * ad + ka].shape[2]
                part = moved[ka * slots : (ka + 1) * slots, c * cw : (c + 1) * cw]
                outs[c * ad + ka][kf] = part


def back_kernel(ad, gslots, *refs):
    dy_refs, up, out = refs[:ad], refs[ad], refs[ad + 1]
    for g in range(up.shape[0] // GROUP):
        rows = pl.ds(g * gslots, gslots)
        dy = jnp.concatenate([r[rows, :] for r in dy_refs], axis=0)
        weights = up[g * GROUP : (g + 1) * GROUP].reshape(-1, up.shape[2])
        part = narrow(dot(dy, weights, ((1,), (1,))), gslots)
        for ka in range(ad):
            out[ka, rows, :] = part[ka * gslots : (ka + 1) * gslots]


def both_kernel(ad, mine, got, *refs):
    dy_refs, out = refs[:ad], refs[ad]
    width = dy_refs[0].shape[1]
    for ka in range(ad):
        out[ka, :, :width] = dy_refs[ka][...]
        out[ka, :, width:] = (adapter_scale * (mine[ka] + got[ka])).astype(BF16)


def hidden_kernel(fsdp, gslots, at, *refs):
    count = (len(refs) - 3) // 2
    own_refs, x_refs, outs, held = refs[:count], refs[count:-3], refs[-3:-1], refs[-1]
    cw = held.shape[2]
    second = at[2] == 1
    for g in range(held.shape[0] // GROUP):
        weights = held[g * GROUP : (g + 1) * GROUP].reshape(-1, cw)
        rows = pl.ds(g * gslots, gslots)
        for i in range(count):
            x = group_rows((own_refs[i], x_refs[i]), g, gslots)
            part = narrow(dot(x, weights, ((1,), (1,))), gslots)
            n = part.shape[1] // 2
            halves = jnp.where(second, part[:, n:], part[:, :n])
            others = jnp.where(second, part[:, :n], part[:, n:])
            for kf in range(fsdp):
                outs[0][kf, i, rows, :] = halves[kf * gslots : (kf + 1) * gslots]
                outs[1][kf, i, rows, :] = others[kf * gslots : (kf + 1) * gslots]


def down_grad_kernel(fsdp, ad, gslots, at, *refs):
    own_refs, x_refs, back_refs = refs[:ad], refs[ad : 2 * ad], refs[2 * ad : 2 * ad + fsdp]
    outs, total = refs[2 * ad + fsdp : -1], refs[-1]
    rloc = outs[0].shape[1]
    rank = back_refs[0].shape[2]
    for g in range(outs[0].shape[0] // GROUP):
        rows = pl.ds(g * gslots, gslots)
        x = group_rows([r for pair in zip(own_refs, x_refs) for r in pair], g, gslots)
        back = [back_refs[kf][ka, rows, :] for ka in range(ad) for kf in range(fsdp)]
        back = widen(jnp.concatenate(back, axis=0), gslots)
        total[...] = dot(back, x, ((0,), (0,)))
        for r in range(fsdp):
            for e in range(GROUP):
                first = pl.multiple_of(e * rank + at[r] * rloc, rloc)
                outs[r][g * GROUP + e] = total[pl.ds(first, rloc), :].astype(BF16)


def delta_kernel(fsdp, ad, gslots, at, own, got, up, *outs):
    for g in range(up.shape[0] // GROUP):
        rows = pl.ds(g * gslots, gslots)
        mine = jnp.concatenate([own[ka, rows, :] for ka in range(ad)], axis=0)
        other = jnp.concatenate([got[ka, rows, :] for ka in range(ad)], axis=0)
        second = at[0] == 1
        low = jnp.where(second, other.astype(F32), mine.astype(F32))
        high = jnp.where(second, mine.astype(F32), other.astype(F32))
        hidden = jnp.concatenate([low, high], axis=1)
        weights = up[g * GROUP : (g + 1) * GROUP].reshape(-1, up.shape[2])
        delta = dot(widen(hidden.astype(BF16), gslots), weights, ((1,), (0,)))
        delta = (adapter_scale * delta).astype(BF16)
        rloc = hidden.shape[1] // fsdp
        for ka in range(ad):
            outs[ka][rows, :] = delta[ka * gslots : (ka + 1) * gslots]
        for kf in range(fsdp):
            part = hidden[:, :rloc]
            for i in range(1, fsdp):
                part = jnp.where(at[1 + kf] == i, hidden[:, i * rloc : (i + 1) * rloc], part)
            part = part.astype(BF16)
            for ka in range(ad):
                outs[ad + kf][ka, rows, :] = part[ka * gslots : (ka + 1) * gslots]


def up_grad_kernel(fsdp, ad, gslots, *refs):
    hid_refs, dy_refs, out = refs[:fsdp], refs[fsdp:-1], refs[-1]
    rloc = hid_refs[0].shape[2]
    for g in range(out.shape[0] // GROUP):
        hid = group_rows(hid_refs, g, gslots)
        dy = group_rows(dy_refs, g, gslots)
        domain = slot_domain(hid.shape[0], rloc, gslots)
        wide = [jnp.where(domain == e, hid.astype(F32), 0.0) for e in range(GROUP)]
        wide = jnp.concatenate(wide, axis=1).astype(BF16)
        total = adapter_scale * dot(wide, dy, ((0,), (0,)))
        for e in range(GROUP):
            out[g * GROUP + e] = total[e * rloc : (e + 1) * rloc]


def output_kernel(fsdp, ad, *refs):
    base, hot, rows, out = refs[:fsdp], refs[fsdp], refs[fsdp + 1 : -1], refs[-1]
    total = base[0][...]
    for k in range(1, fsdp):
        total = total + base[k][...]
    delta = jnp.concatenate([r[...] for r in rows], axis=0)
    out[...] = (total + dot(hot[...], delta, ((0,), (0,)))).astype(BF16)


def base_kernel(fsdp, at, own, *refs):
    mine, got = refs[: fsdp - 1], refs[fsdp - 1 : 2 * fsdp - 2]
    weight, outs = refs[2 * fsdp - 2], refs[2 * fsdp - 1 :]
    rows, kt = own.shape[0], mine[0].shape[1]
    outs[0][...] = dot(own[...], weight[...], ((1,), (0,)))
    w_mine = weight[pl.ds(pl.multiple_of(at[0] * kt, kt), kt), :]
    w_got = weight[pl.ds(pl.multiple_of((1 - at[0]) * kt, kt), kt), :]
    for k in range(1, fsdp):
        total = dot(mine[k - 1][:rows, :], w_mine, ((1,), (0,)))
        outs[k][...] = total + dot(got[k - 1][:rows, :], w_got, ((1,), (0,)))


def column_body(
    input_rows,
    value_weight_frozen,
    adapter_down_weight,
    adapter_up_weight,
    layer_output_gradient,
    domain,
):
    fsdp, ad = lax.axis_size("fsdp"), lax.axis_size("ad")
    f, t, a = lax.axis_index("fsdp"), lax.axis_index("tp"), lax.axis_index("ad")
    fy, fx = f // 2, f % 2
    rows, width = input_rows.shape
    dloc, rank, half = adapter_down_weight.shape
    vloc = adapter_up_weight.shape[2]
    rloc = rank // fsdp
    kf_width = width // fsdp
    kt = kf_width // 2
    slots = dloc * CAPD
    gslots = GROUP * CAPD
    cw = kt // CHUNKS

    def over_f(v, k):
        return lax.ppermute(v, "fsdp", [(i, i ^ k) for i in range(fsdp)]) if k else v

    def over_a(v, k):
        return lax.ppermute(v, "ad", [(i, (i + k) % ad) for i in range(ad)]) if k else v

    def swap(v):
        return lax.ppermute(v, "tp", [(0, 1), (1, 0)])

    def numbers(*values):
        return jnp.stack([jnp.asarray(v, jnp.int32) for v in values])

    def after(v, *others):
        return lax.optimization_barrier((v, others))[0]

    x_in = []
    for k in range(fsdp):
        block = lax.dynamic_slice_in_dim(input_rows, (f ^ k) * kf_width + t * kt, kt, 1)
        if k:
            dom_row = jnp.pad(domain.T.astype(BF16), ((0, 15), (0, kt - rows)))
            block = jnp.concatenate([block, dom_row], axis=0)
        x_in.append(block)
    x_in = lax.optimization_barrier(x_in)
    x_in[1], x_in[2] = over_f(x_in[1], 1), over_f(x_in[2], 2)
    x_in[3] = over_f(x_in[3], 3)

    hot, *sends = call(
        functools.partial(own_kernel, ad, slots, ad * dloc),
        [((ad * slots, rows), BF16)] + [((slots, kt + vloc), BF16)] * ad,
        [(v, None) for v in (domain.T, x_in[0], layer_output_gradient)],
        at=numbers(a),
    )
    held = after((adapter_down_weight, input_rows), *sends)
    sends[-1] = after(sends[-1], x_in[1])
    own = [over_a(v, ka) for ka, v in enumerate(sends)]

    down_other = lax.dynamic_slice_in_dim(held[0], (fx * 2 + 1 - t) * kt, kt, 2)
    pairs = [(i * 2 + i // 2, i * 2 + 1 - i // 2) for i in range(fsdp)]

    x_chip = lax.dynamic_slice_in_dim(held[1], f * kf_width, kf_width, 1)
    x_in, own, down_other, x_chip = lax.optimization_barrier((x_in, own, down_other, x_chip))
    x_other = [swap(v) for v in x_in[1:]]
    down_got = lax.ppermute(down_other, ("fsdp", "tp"), pairs)
    sends = call(
        functools.partial(others_kernel, fsdp, ad, slots, ad * dloc),
        [((fsdp - 1, slots, cw), BF16)] * (CHUNKS * ad),
        [(v, None) for v in x_in[1:]],
        at=numbers(a),
    )
    x_routed = [[over_a(v, ka) for ka, v in enumerate(sends[:ad])]]

    base = call(
        functools.partial(base_kernel, fsdp),
        [((rows, vloc), F32)] * fsdp,
        [(v, None) for v in (x_chip, *x_in[1:], *after(x_other, *sends), value_weight_frozen)],
        at=numbers(t),
    )
    dy = [(v, (kt, vloc)) for v in after(own, base[0], down_got)]
    base = [over_f(v, k) for k, v in enumerate(base)]

    (back,) = call(
        functools.partial(back_kernel, ad, gslots),
        [((ad, slots, rank), F32)],
        [*dy, (adapter_up_weight, None)],
        flops=10**10,
    )
    (both,) = call(
        functools.partial(both_kernel, ad),
        [((ad, slots, vloc + rank), BF16)],
        [(back, None), (swap(back), None), *dy],
    )
    both = after(both, *base, x_routed[0][2])
    both = [over_f(both, k) for k in range(fsdp)]

    def hidden(shifts, routed):
        return call(
            functools.partial(hidden_kernel, fsdp, gslots),
            [((fsdp, len(shifts), slots, rank // 2), F32)] * 2,
            [(own[ka], (0, kt)) for ka in shifts] + [(v, None) for v in routed],
            at=numbers(t == fy, fx * kf_width + t * kt, t),
            either=(adapter_down_weight, down_got, (0, kt)),
            flops=10**10,
        )

    early, late = [ka for ka in range(ad) if ka % 2 == 0], [ka for ka in range(ad) if ka % 2]
    hid_early = hidden(early, after([x_routed[0][ka] for ka in early], both[0]))
    x_last = after(x_routed[0], *base, *hid_early)
    hid_late = hidden(late, [x_last[ka] for ka in late])
    x_last, both = after((x_last, both), *hid_late)
    hid = jnp.concatenate(
        [hid_early[0] + swap(hid_early[1]), hid_late[0] + swap(hid_late[1])], axis=1
    )

    sums = call(
        functools.partial(down_grad_kernel, fsdp, ad, gslots),
        [((dloc, rloc, kt), BF16)] * fsdp,
        [(v, (0, kt)) for v in own]
        + [(v, None) for v in x_last]
        + [(v, (vloc, rank)) for v in both],
        at=numbers(*[(t ^ (r // 2)) * 2 + (fx ^ (r % 2)) for r in range(fsdp)]),
        scratch=[pltpu.VMEM((GROUP * rank, kt), F32)],
        flops=10**10,
    )
    hid = [over_f(hid[k], k) for k in range(fsdp)]
    sums = [sums[0], sums[1], *after(sums[2:], *hid[1:])]
    grad_a = jnp.zeros((dloc, rloc, half), F32)
    got = []
    for r in range(fsdp):
        p, q = r % 2, r // 2
        perm = [
            ((y * 2 + x) * 2 + s, ((s ^ q) * 2 + (x ^ p)) * 2 + y)
            for y in range(2)
            for x in range(2)
            for s in range(2)
        ]
        got.append(lax.ppermute(sums[r], ("fsdp", "tp"), perm))
        at = (fx ^ p) * kf_width + (fy ^ q) * kt
        grad_a = lax.dynamic_update_slice_in_dim(grad_a, got[r].astype(F32), at, 2)

    hid_own = (hid[0] + hid[1] + hid[2] + hid[3]).astype(BF16)
    shift_order = [(early + late).index(ka) for ka in range(ad)]
    hid_own = jnp.concatenate([hid_own[i : i + 1] for i in shift_order], axis=0)
    outs = call(
        functools.partial(delta_kernel, fsdp, ad, gslots),
        [((slots, vloc), BF16)] * ad + [((ad, slots, rloc), BF16)] * fsdp,
        [(v, None) for v in (hid_own, swap(hid_own), adapter_up_weight)],
        at=numbers(t, *[f ^ k for k in range(fsdp)]),
    )
    returned = [over_a(v, (ad - ka) % ad) for ka, v in enumerate(outs[:ad])]
    hid_cols = [over_f(after(v, got[2], *returned[1:]), k) for k, v in enumerate(outs[ad:])]

    (y_out,) = call(
        functools.partial(output_kernel, fsdp, ad),
        [((rows, vloc), BF16)],
        [(v, None) for v in (*base, hot, *returned)],
    )
    (grad_b,) = call(
        functools.partial(up_grad_kernel, fsdp, ad, gslots),
        [((dloc, rloc, vloc), F32)],
        [(v, None) for v in hid_cols] + [(v, (0, vloc)) for v in both],
    )
    return y_out, grad_a, grad_b


def solution(mesh):
    placed = (
        P(("fsdp", "ad"), None),
        P("fsdp", "tp"),
        P("ad", None, "tp"),
        P("ad", None, "tp"),
        P(("fsdp", "ad"), "tp"),
        P(("fsdp", "ad"), None),
    )
    square = mesh.shape["fsdp"] == 4 and mesh.shape["tp"] == 2 and mesh.shape["ad"] == 4
    return jax.shard_map(
        column_body if square else general_body,
        mesh=mesh,
        in_specs=placed,
        out_specs=(P(("fsdp", "ad"), "tp"), P("ad", "fsdp", "tp"), P("ad", "fsdp", "tp")),
        check_vma=False,
    )
```

```python
import functools

import jax
import jax.numpy as jnp
from jax import lax
from jax.experimental import pallas as pl
from jax.experimental.pallas import tpu as pltpu
from jax.sharding import PartitionSpec as P

CAPD = 12
GROUP = 4
CHUNKS = 1

adapter_scale = 0.5


def slot_places(dom_ids, dom_total):
    row_count = dom_ids.shape[0]
    onehot = (dom_ids[:, None] == jnp.arange(dom_total, dtype=jnp.int32)[None, :]).astype(
        jnp.float32
    )
    row_iota = jnp.arange(row_count, dtype=jnp.int32)
    earlier = (row_iota[:, None] > row_iota[None, :]).astype(jnp.float32)
    prior = jnp.dot(earlier, onehot, preferred_element_type=jnp.float32)
    position = jnp.sum(prior * onehot, axis=1).astype(jnp.int32)
    return dom_ids * CAPD + position


def general_body(
    input_rows,
    value_weight_frozen,
    adapter_down_weight,
    adapter_up_weight,
    layer_output_gradient,
    domain,
):
    row_count = input_rows.shape[0]
    domain_local = adapter_down_weight.shape[0]
    width_local = adapter_down_weight.shape[2]
    value_width_local = adapter_up_weight.shape[2]
    ad_count = lax.axis_size("ad")
    slot_total = ad_count * domain_local * CAPD
    place = slot_places(domain[:, 0], ad_count * domain_local)
    row_iota = jnp.arange(row_count, dtype=jnp.int32)
    matches = place[None, :] == jnp.arange(slot_total, dtype=jnp.int32)[:, None]
    filled = jnp.any(matches, axis=1)
    source_row = jnp.sum(jnp.where(matches, row_iota[None, :], 0), axis=1)
    base = jnp.dot(
        input_rows,
        lax.all_gather(value_weight_frozen, "fsdp", axis=0, tiled=True),
        preferred_element_type=jnp.float32,
    )
    feature_cols = lax.dynamic_slice_in_dim(
        input_rows, lax.axis_index("tp") * width_local, width_local, 1
    )
    zero_value = jnp.zeros((), jnp.bfloat16)
    send_x = jnp.where(filled[:, None], feature_cols[source_row], zero_value)
    send_dy = jnp.where(filled[:, None], layer_output_gradient[source_row], zero_value)
    send_x = send_x.reshape(ad_count, domain_local * CAPD, width_local)
    send_dy = send_dy.reshape(ad_count, domain_local * CAPD, value_width_local)
    got_x = lax.all_to_all(send_x, "ad", split_axis=0, concat_axis=0, tiled=True)
    got_dy = lax.all_to_all(send_dy, "ad", split_axis=0, concat_axis=0, tiled=True)
    rows = got_x.reshape(ad_count, domain_local, CAPD, width_local)
    grads = got_dy.reshape(ad_count, domain_local, CAPD, value_width_local)
    f32 = dict(preferred_element_type=jnp.float32)
    hidden, back = lax.psum(
        (
            jnp.einsum("vqfj,qwj->vqfw", rows, adapter_down_weight, **f32),
            jnp.einsum("amgy,mzy->amgz", grads, adapter_up_weight, **f32),
        ),
        "tp",
    )
    hidden = hidden.astype(jnp.bfloat16)
    back = (adapter_scale * back).astype(jnp.bfloat16)
    delta = adapter_scale * jnp.einsum("lokh,ohi->loki", hidden, adapter_up_weight, **f32)
    delta = delta.astype(jnp.bfloat16).reshape(ad_count, domain_local * CAPD, value_width_local)
    part_a = jnp.einsum("sdcr,sdcx->drx", back, rows, **f32)
    part_b = adapter_scale * jnp.einsum("sdcr,sdce->dre", hidden, grads, **f32)
    returned = lax.all_to_all(delta, "ad", split_axis=0, concat_axis=0, tiled=True)
    returned = returned.reshape(slot_total, value_width_local)
    y_out = (base + returned[place].astype(jnp.float32)).astype(jnp.bfloat16)
    return (
        y_out,
        lax.psum_scatter(part_a, "fsdp", scatter_dimension=1, tiled=True),
        lax.psum_scatter(part_b, "fsdp", scatter_dimension=1, tiled=True),
    )


BF16, F32 = jnp.bfloat16, jnp.float32
VMEM_BYTES = 58 << 20
VMEM = pl.BlockSpec(memory_space=pltpu.VMEM)
SMEM = pl.BlockSpec(memory_space=pltpu.SMEM)
ANY = pl.BlockSpec(memory_space=pl.ANY)


def dot(lhs, rhs, dims):
    return lax.dot_general(lhs, rhs, (dims, ((), ())), preferred_element_type=F32)


def call(kernel, out_shape, fetched, at=None, scratch=(), either=None, flops=1):
    nf, n_out = len(fetched), len(out_shape)
    shapes = [v.shape[:-1] + (v.shape[-1] if w is None else w[1],) for v, w in fetched]
    sources = [v for v, _ in fetched] + ([] if either is None else list(either[:2]))
    buffers = [pltpu.VMEM(shape, v.dtype) for shape, (v, _) in zip(shapes, fetched)]
    if either is not None:
        lead, width = either[0].shape[:-1], either[2][1]
        buffers.append(pltpu.VMEM(lead + (width,), either[0].dtype))
        buffers.append(pltpu.SemaphoreType.DMA((lead[0],)))

    def body(*refs):
        refs = list(refs)
        head = [refs.pop(0)] if at is not None else []
        froms, refs = refs[: len(sources)], refs[len(sources) :]
        outs, refs = refs[:n_out], refs[n_out:]
        sems, held, extra = refs[0], refs[1 : 1 + len(buffers)], refs[1 + len(buffers) :]
        copies = []
        for i, (source, (_, columns)) in enumerate(zip(froms, fetched)):
            if columns is not None:
                first = (slice(None),) * (len(source.shape) - 1)
                source = source.at[first + (pl.ds(*columns),)]
            copies.append(pltpu.make_async_copy(source, held[i], sems.at[i]))
        for c in copies:
            c.start()
        if either is not None:
            one, other = froms[nf:]
            buffer, more = held[nf], held.pop()
            start = pl.multiple_of(head[0][1], 128)
            parts = [
                pltpu.make_async_copy(one.at[d, :, pl.ds(start, width)], buffer.at[d], more.at[d])
                for d in range(lead[0])
            ]
            others = [
                pltpu.make_async_copy(
                    other.at[d, :, pl.ds(*either[2])], buffer.at[d], more.at[d]
                )
                for d in range(lead[0])
            ]

            @pl.when(head[0][0] == 1)
            def _():
                for c in parts:
                    c.start()

            @pl.when(head[0][0] != 1)
            def _():
                for c in others:
                    c.start()

            copies.extend(others)
        for c in copies:
            c.wait()
        kernel(*head, *held[:nf], *outs, *held[nf:], *extra)

    return pl.pallas_call(
        body,
        out_shape=[jax.ShapeDtypeStruct(shape, dtype) for shape, dtype in out_shape],
        in_specs=[SMEM] * (at is not None) + [ANY] * len(sources),
        out_specs=[VMEM] * n_out,
        scratch_shapes=[pltpu.SemaphoreType.DMA((nf,)), *buffers, *scratch],
        compiler_params=pltpu.CompilerParams(vmem_limit_bytes=VMEM_BYTES),
        cost_estimate=pl.CostEstimate(flops=flops, bytes_accessed=1, transcendentals=0),
    )(*([at] if at is not None else []), *sources)


def slot_domain(count, lanes, gslots):
    slot = lax.broadcasted_iota(jnp.int32, (count, lanes), 0)
    return lax.rem(slot, gslots) // CAPD


def widen(v, gslots):
    domain = slot_domain(*v.shape, gslots)
    parts = [jnp.where(domain == e, v.astype(F32), 0.0).astype(v.dtype) for e in range(GROUP)]
    return jnp.concatenate(parts, axis=1)


def narrow(v, gslots):
    n = v.shape[1] // GROUP
    domain = slot_domain(v.shape[0], n, gslots)
    total = v[:, :n]
    for e in range(1, GROUP):
        total = jnp.where(domain == e, v[:, e * n : (e + 1) * n], total)
    return total


def group_rows(refs, g, gslots):
    rows = pl.ds(g * gslots, gslots)
    parts = []
    for r in refs:
        if len(r.shape) == 2:
            parts.append(r[rows, :])
        else:
            parts.extend(r[i, rows, :] for i in range(r.shape[0]))
    return jnp.concatenate(parts, axis=0)


def one_hot(dom, first, slots, ad, dom_total):
    rows = dom.shape[1]
    names = lax.broadcasted_iota(jnp.int32, (dom_total, rows), 0)
    is_dom = (names == dom).astype(F32)
    before = lax.broadcasted_iota(jnp.int32, (rows, rows), 0) < lax.broadcasted_iota(
        jnp.int32, (rows, rows), 1
    )
    prior = dot(is_dom.astype(BF16), before.astype(F32).astype(BF16), ((1,), (0,)))
    position = jnp.sum(prior * is_dom, axis=0, keepdims=True).astype(jnp.int32)
    slot = lax.broadcasted_iota(jnp.int32, (ad * slots, rows), 0)
    slot = lax.rem(slot + first * slots, ad * slots)
    return (slot == dom * CAPD + position).astype(F32).astype(BF16)


def own_kernel(ad, slots, dom_total, at, dom, x, dy, hot_ref, *outs):
    hot = one_hot(dom[...], at[0], slots, ad, dom_total)
    hot_ref[...] = hot
    width = x.shape[1]
    moved = dot(hot, x[...], ((1,), (0,))).astype(BF16)
    moved_dy = dot(hot, dy[...], ((1,), (0,))).astype(BF16)
    for ka in range(ad):
        outs[ka][:, :width] = moved[ka * slots : (ka + 1) * slots]
        outs[ka][:, width:] = moved_dy[ka * slots : (ka + 1) * slots]


def others_kernel(fsdp, ad, slots, dom_total, at, *refs):
    x_refs, outs = refs[: fsdp - 1], refs[fsdp - 1 :]
    for kf in range(fsdp - 1):
        rows = x_refs[kf].shape[0] - 16
        dom = x_refs[kf][rows:, :rows].astype(F32).astype(jnp.int32)[:1]
        hot = one_hot(dom, at[0], slots, ad, dom_total)
        moved = dot(hot, x_refs[kf][:rows, :], ((1,), (0,))).astype(BF16)
        for c in range(CHUNKS):
            for ka in range(ad):
                cw = outs[c * ad + ka].shape[2]
                part = moved[ka * slots : (ka + 1) * slots, c * cw : (c + 1) * cw]
                outs[c * ad + ka][kf] = part


def back_kernel(gslots, dy_ref, up, out):
    ad = dy_ref.shape[0]
    for g in range(up.shape[0] // GROUP):
        rows = pl.ds(g * gslots, gslots)
        dy = jnp.concatenate([dy_ref[ka, rows, :] for ka in range(ad)], axis=0)
        weights = up[g * GROUP : (g + 1) * GROUP].reshape(-1, up.shape[2])
        part = narrow(dot(dy, weights, ((1,), (1,))), gslots)
        for ka in range(ad):
            out[ka, rows, :] = part[ka * gslots : (ka + 1) * gslots]


def sum_kernel(mine, got, out):
    out[...] = (adapter_scale * (mine[...] + got[...])).astype(BF16)


def hidden_kernel(fsdp, gslots, at, *refs):
    count = (len(refs) - 3) // 2
    own_refs, x_refs, outs, held = refs[:count], refs[count:-3], refs[-3:-1], refs[-1]
    cw = held.shape[2]
    second = at[2] == 1
    for g in range(held.shape[0] // GROUP):
        weights = held[g * GROUP : (g + 1) * GROUP].reshape(-1, cw)
        rows = pl.ds(g * gslots, gslots)
        for i in range(count):
            x = group_rows((own_refs[i], x_refs[i]), g, gslots)
            part = narrow(dot(x, weights, ((1,), (1,))), gslots)
            n = part.shape[1] // 2
            halves = jnp.where(second, part[:, n:], part[:, :n])
            others = jnp.where(second, part[:, :n], part[:, n:])
            for kf in range(fsdp):
                outs[0][kf, i, rows, :] = halves[kf * gslots : (kf + 1) * gslots]
                outs[1][kf, i, rows, :] = others[kf * gslots : (kf + 1) * gslots]


def down_grad_kernel(fsdp, ad, gslots, at, *refs):
    own_refs, x_refs, back_refs = refs[:ad], refs[ad : 2 * ad], refs[2 * ad : 2 * ad + fsdp]
    outs, total = refs[2 * ad + fsdp : -1], refs[-1]
    rloc = outs[0].shape[1]
    rank = back_refs[0].shape[2]
    for g in range(outs[0].shape[0] // GROUP):
        rows = pl.ds(g * gslots, gslots)
        x = group_rows([r for pair in zip(own_refs, x_refs) for r in pair], g, gslots)
        back = [back_refs[kf][ka, rows, :] for ka in range(ad) for kf in range(fsdp)]
        back = widen(jnp.concatenate(back, axis=0), gslots)
        total[...] = dot(back, x, ((0,), (0,)))
        for r in range(fsdp):
            for e in range(GROUP):
                first = pl.multiple_of(e * rank + at[r] * rloc, rloc)
                outs[r][g * GROUP + e] = total[pl.ds(first, rloc), :].astype(BF16)


def delta_kernel(fsdp, ad, gslots, at, own, got, up, *outs):
    for g in range(up.shape[0] // GROUP):
        rows = pl.ds(g * gslots, gslots)
        mine = jnp.concatenate([own[ka, rows, :] for ka in range(ad)], axis=0)
        other = jnp.concatenate([got[ka, rows, :] for ka in range(ad)], axis=0)
        second = at[0] == 1
        low = jnp.where(second, other.astype(F32), mine.astype(F32))
        high = jnp.where(second, mine.astype(F32), other.astype(F32))
        hidden = jnp.concatenate([low, high], axis=1)
        weights = up[g * GROUP : (g + 1) * GROUP].reshape(-1, up.shape[2])
        delta = dot(widen(hidden.astype(BF16), gslots), weights, ((1,), (0,)))
        delta = (adapter_scale * delta).astype(BF16)
        rloc = hidden.shape[1] // fsdp
        for ka in range(ad):
            outs[ka][rows, :] = delta[ka * gslots : (ka + 1) * gslots]
        for kf in range(fsdp):
            part = hidden[:, :rloc]
            for i in range(1, fsdp):
                part = jnp.where(at[1 + kf] == i, hidden[:, i * rloc : (i + 1) * rloc], part)
            part = part.astype(BF16)
            for ka in range(ad):
                outs[ad + kf][ka, rows, :] = part[ka * gslots : (ka + 1) * gslots]


def up_grad_kernel(fsdp, ad, gslots, *refs):
    hid_refs, dy_refs, out = refs[:fsdp], refs[fsdp:-1], refs[-1]
    rloc = hid_refs[0].shape[2]
    for g in range(out.shape[0] // GROUP):
        hid = group_rows(hid_refs, g, gslots)
        dy = group_rows(dy_refs, g, gslots)
        domain = slot_domain(hid.shape[0], rloc, gslots)
        wide = [jnp.where(domain == e, hid.astype(F32), 0.0) for e in range(GROUP)]
        wide = jnp.concatenate(wide, axis=1).astype(BF16)
        total = adapter_scale * dot(wide, dy, ((0,), (0,)))
        for e in range(GROUP):
            out[g * GROUP + e] = total[e * rloc : (e + 1) * rloc]


def output_kernel(fsdp, ad, *refs):
    base, hot, rows, out = refs[:fsdp], refs[fsdp], refs[fsdp + 1 : -1], refs[-1]
    total = base[0][...]
    for k in range(1, fsdp):
        total = total + base[k][...]
    delta = jnp.concatenate([r[...] for r in rows], axis=0)
    out[...] = (total + dot(hot[...], delta, ((0,), (0,)))).astype(BF16)


def base_kernel(fsdp, at, own, *refs):
    mine, got = refs[: fsdp - 1], refs[fsdp - 1 : 2 * fsdp - 2]
    weight, outs = refs[2 * fsdp - 2], refs[2 * fsdp - 1 :]
    rows, kt = own.shape[0], mine[0].shape[1]
    outs[0][...] = dot(own[...], weight[...], ((1,), (0,)))
    w_mine = weight[pl.ds(pl.multiple_of(at[0] * kt, kt), kt), :]
    w_got = weight[pl.ds(pl.multiple_of((1 - at[0]) * kt, kt), kt), :]
    for k in range(1, fsdp):
        total = dot(mine[k - 1][:rows, :], w_mine, ((1,), (0,)))
        outs[k][...] = total + dot(got[k - 1][:rows, :], w_got, ((1,), (0,)))


def column_body(
    input_rows,
    value_weight_frozen,
    adapter_down_weight,
    adapter_up_weight,
    layer_output_gradient,
    domain,
):
    fsdp, ad = lax.axis_size("fsdp"), lax.axis_size("ad")
    f, t, a = lax.axis_index("fsdp"), lax.axis_index("tp"), lax.axis_index("ad")
    fy, fx = f // 2, f % 2
    rows, width = input_rows.shape
    dloc, rank, half = adapter_down_weight.shape
    vloc = adapter_up_weight.shape[2]
    rloc = rank // fsdp
    kf_width = width // fsdp
    kt = kf_width // 2
    slots = dloc * CAPD
    gslots = GROUP * CAPD
    cw = kt // CHUNKS

    def over_f(v, k):
        return lax.ppermute(v, "fsdp", [(i, i ^ k) for i in range(fsdp)]) if k else v

    def over_a(v, k):
        return lax.ppermute(v, "ad", [(i, (i + k) % ad) for i in range(ad)]) if k else v

    def swap(v):
        return lax.ppermute(v, "tp", [(0, 1), (1, 0)])

    def numbers(*values):
        return jnp.stack([jnp.asarray(v, jnp.int32) for v in values])

    def after(v, *others):
        return lax.optimization_barrier((v, others))[0]

    x_in = []
    for k in range(fsdp):
        block = lax.dynamic_slice_in_dim(input_rows, (f ^ k) * kf_width + t * kt, kt, 1)
        if k:
            dom_row = jnp.pad(domain.T.astype(BF16), ((0, 15), (0, kt - rows)))
            block = jnp.concatenate([block, dom_row], axis=0)
        x_in.append(block)
    x_in = lax.optimization_barrier(x_in)
    x_in[1], x_in[2] = over_f(x_in[1], 1), over_f(x_in[2], 2)
    x_in[3] = over_f(x_in[3], 3)

    hot, *sends = call(
        functools.partial(own_kernel, ad, slots, ad * dloc),
        [((ad * slots, rows), BF16)] + [((slots, kt + vloc), BF16)] * ad,
        [(v, None) for v in (domain.T, x_in[0], layer_output_gradient)],
        at=numbers(a),
    )
    held = after((adapter_down_weight, input_rows), *sends)
    sends[-1] = after(sends[-1], x_in[1])
    own = [over_a(v, ka) for ka, v in enumerate(sends)]

    down_other = lax.dynamic_slice_in_dim(held[0], (fx * 2 + 1 - t) * kt, kt, 2)
    pairs = [(i * 2 + i // 2, i * 2 + 1 - i // 2) for i in range(fsdp)]

    x_chip = lax.dynamic_slice_in_dim(held[1], f * kf_width, kf_width, 1)
    x_in, own, down_other, x_chip = lax.optimization_barrier((x_in, own, down_other, x_chip))
    x_other = [swap(v) for v in x_in[1:]]
    down_got = lax.ppermute(after(down_other, x_other), ("fsdp", "tp"), pairs)
    dy = jnp.stack([v[:, kt:] for v in own])
    dy_all = [over_f(dy, k) for k in range(fsdp)]
    sends = call(
        functools.partial(others_kernel, fsdp, ad, slots, ad * dloc),
        [((fsdp - 1, slots, cw), BF16)] * (CHUNKS * ad),
        [(v, None) for v in x_in[1:]],
        at=numbers(a),
    )
    x_routed = [[over_a(v, ka) for ka, v in enumerate(sends[:ad])]]

    base = call(
        functools.partial(base_kernel, fsdp),
        [((rows, vloc), F32)] * fsdp,
        [(v, None) for v in (x_chip, *x_in[1:], *after(x_other, *sends, *dy_all), value_weight_frozen)],
        at=numbers(t),
    )
    dy = after(dy, base[0], down_got)
    base = [over_f(v, k) for k, v in enumerate(base)]

    (back,) = call(
        functools.partial(back_kernel, gslots),
        [((ad, slots, rank), F32)],
        [(dy, None), (adapter_up_weight, None)],
        flops=10**10,
    )
    (back,) = call(
        sum_kernel, [((ad, slots, rank), BF16)], [(back, None), (swap(back), None)]
    )
    back = after(back, *base, x_routed[0][2])
    back = [over_f(back, k) for k in range(fsdp)]

    def hidden(shifts, routed):
        return call(
            functools.partial(hidden_kernel, fsdp, gslots),
            [((fsdp, len(shifts), slots, rank // 2), F32)] * 2,
            [(own[ka], (0, kt)) for ka in shifts] + [(v, None) for v in routed],
            at=numbers(t == fy, fx * kf_width + t * kt, t),
            either=(adapter_down_weight, down_got, (0, kt)),
            flops=10**10,
        )

    early, late = [ka for ka in range(ad) if ka % 2 == 0], [ka for ka in range(ad) if ka % 2]
    hid_early = hidden(early, after([x_routed[0][ka] for ka in early], back[0]))
    x_last = after(x_routed[0], *base, *hid_early, *back)
    hid_late = hidden(late, [x_last[ka] for ka in late])
    x_last, back = after((x_last, back), *hid_late)
    hid = jnp.concatenate(
        [hid_early[0] + swap(hid_early[1]), hid_late[0] + swap(hid_late[1])], axis=1
    )

    sums = call(
        functools.partial(down_grad_kernel, fsdp, ad, gslots),
        [((dloc, rloc, kt), BF16)] * fsdp,
        [(v, (0, kt)) for v in own]
        + [(v, None) for v in x_last]
        + [(v, None) for v in back],
        at=numbers(*[(t ^ (r // 2)) * 2 + (fx ^ (r % 2)) for r in range(fsdp)]),
        scratch=[pltpu.VMEM((GROUP * rank, kt), F32)],
        flops=10**10,
    )
    hid = [over_f(hid[k], k) for k in range(fsdp)]
    hid_own = (hid[0] + hid[1] + hid[2] + hid[3]).astype(BF16)
    shift_order = [(early + late).index(ka) for ka in range(ad)]
    hid_own = jnp.concatenate([hid_own[i : i + 1] for i in shift_order], axis=0)
    outs = call(
        functools.partial(delta_kernel, fsdp, ad, gslots),
        [((slots, vloc), BF16)] * ad + [((ad, slots, rloc), BF16)] * fsdp,
        [(v, None) for v in (hid_own, swap(hid_own), adapter_up_weight)],
        at=numbers(t, *[f ^ k for k in range(fsdp)]),
    )
    returned = [over_a(v, (ad - ka) % ad) for ka, v in enumerate(outs[:ad])]
    grad_a = jnp.zeros((dloc, rloc, half), F32)
    hid_cols, grad_a = after((outs[ad:], grad_a), *returned[1:])
    hid_cols = [over_f(v, k) for k, v in enumerate(hid_cols)]
    got = []
    for r in range(fsdp):
        p, q = r % 2, r // 2
        perm = [
            ((y * 2 + x) * 2 + s, ((s ^ q) * 2 + (x ^ p)) * 2 + y)
            for y in range(2)
            for x in range(2)
            for s in range(2)
        ]
        block = after(sums[r], *(hid[1:] if r < 2 else [*got[:2], *hid_cols[1:]]))
        got.append(lax.ppermute(block, ("fsdp", "tp"), perm))
        at = (fx ^ p) * kf_width + (fy ^ q) * kt
        grad_a = lax.dynamic_update_slice_in_dim(grad_a, got[r].astype(F32), at, 2)

    (y_out,) = call(
        functools.partial(output_kernel, fsdp, ad),
        [((rows, vloc), BF16)],
        [(v, None) for v in (*base, hot, *returned)],
    )
    (grad_b,) = call(
        functools.partial(up_grad_kernel, fsdp, ad, gslots),
        [((dloc, rloc, vloc), F32)],
        [(v, None) for v in [*hid_cols, *dy_all]],
    )
    return y_out, grad_a, grad_b


def solution(mesh):
    placed = (
        P(("fsdp", "ad"), None),
        P("fsdp", "tp"),
        P("ad", None, "tp"),
        P("ad", None, "tp"),
        P(("fsdp", "ad"), "tp"),
        P(("fsdp", "ad"), None),
    )
    square = mesh.shape["fsdp"] == 4 and mesh.shape["tp"] == 2 and mesh.shape["ad"] == 4
    return jax.shard_map(
        column_body if square else general_body,
        mesh=mesh,
        in_specs=placed,
        out_specs=(P(("fsdp", "ad"), "tp"), P("ad", "fsdp", "tp"), P("ad", "fsdp", "tp")),
        check_vma=False,
    )
```

```python
import functools

import jax
import jax.numpy as jnp
from jax import lax
from jax.experimental import pallas as pl
from jax.experimental.pallas import tpu as pltpu
from jax.sharding import PartitionSpec as P

CAPD = 12
GROUP = 4
CHUNKS = 1

adapter_scale = 0.5


def slot_places(dom_ids, dom_total):
    row_count = dom_ids.shape[0]
    onehot = (dom_ids[:, None] == jnp.arange(dom_total, dtype=jnp.int32)[None, :]).astype(
        jnp.float32
    )
    row_iota = jnp.arange(row_count, dtype=jnp.int32)
    earlier = (row_iota[:, None] > row_iota[None, :]).astype(jnp.float32)
    prior = jnp.dot(earlier, onehot, preferred_element_type=jnp.float32)
    position = jnp.sum(prior * onehot, axis=1).astype(jnp.int32)
    return dom_ids * CAPD + position


def general_body(
    input_rows,
    value_weight_frozen,
    adapter_down_weight,
    adapter_up_weight,
    layer_output_gradient,
    domain,
):
    row_count = input_rows.shape[0]
    domain_local = adapter_down_weight.shape[0]
    width_local = adapter_down_weight.shape[2]
    value_width_local = adapter_up_weight.shape[2]
    ad_count = lax.axis_size("ad")
    slot_total = ad_count * domain_local * CAPD
    place = slot_places(domain[:, 0], ad_count * domain_local)
    row_iota = jnp.arange(row_count, dtype=jnp.int32)
    matches = place[None, :] == jnp.arange(slot_total, dtype=jnp.int32)[:, None]
    filled = jnp.any(matches, axis=1)
    source_row = jnp.sum(jnp.where(matches, row_iota[None, :], 0), axis=1)
    base = jnp.dot(
        input_rows,
        lax.all_gather(value_weight_frozen, "fsdp", axis=0, tiled=True),
        preferred_element_type=jnp.float32,
    )
    feature_cols = lax.dynamic_slice_in_dim(
        input_rows, lax.axis_index("tp") * width_local, width_local, 1
    )
    zero_value = jnp.zeros((), jnp.bfloat16)
    send_x = jnp.where(filled[:, None], feature_cols[source_row], zero_value)
    send_dy = jnp.where(filled[:, None], layer_output_gradient[source_row], zero_value)
    send_x = send_x.reshape(ad_count, domain_local * CAPD, width_local)
    send_dy = send_dy.reshape(ad_count, domain_local * CAPD, value_width_local)
    got_x = lax.all_to_all(send_x, "ad", split_axis=0, concat_axis=0, tiled=True)
    got_dy = lax.all_to_all(send_dy, "ad", split_axis=0, concat_axis=0, tiled=True)
    rows = got_x.reshape(ad_count, domain_local, CAPD, width_local)
    grads = got_dy.reshape(ad_count, domain_local, CAPD, value_width_local)
    f32 = dict(preferred_element_type=jnp.float32)
    hidden, back = lax.psum(
        (
            jnp.einsum("vqfj,qwj->vqfw", rows, adapter_down_weight, **f32),
            jnp.einsum("amgy,mzy->amgz", grads, adapter_up_weight, **f32),
        ),
        "tp",
    )
    hidden = hidden.astype(jnp.bfloat16)
    back = (adapter_scale * back).astype(jnp.bfloat16)
    delta = adapter_scale * jnp.einsum("lokh,ohi->loki", hidden, adapter_up_weight, **f32)
    delta = delta.astype(jnp.bfloat16).reshape(ad_count, domain_local * CAPD, value_width_local)
    part_a = jnp.einsum("sdcr,sdcx->drx", back, rows, **f32)
    part_b = adapter_scale * jnp.einsum("sdcr,sdce->dre", hidden, grads, **f32)
    returned = lax.all_to_all(delta, "ad", split_axis=0, concat_axis=0, tiled=True)
    returned = returned.reshape(slot_total, value_width_local)
    y_out = (base + returned[place].astype(jnp.float32)).astype(jnp.bfloat16)
    return (
        y_out,
        lax.psum_scatter(part_a, "fsdp", scatter_dimension=1, tiled=True),
        lax.psum_scatter(part_b, "fsdp", scatter_dimension=1, tiled=True),
    )


BF16, F32 = jnp.bfloat16, jnp.float32
VMEM_BYTES = 58 << 20
VMEM = pl.BlockSpec(memory_space=pltpu.VMEM)
SMEM = pl.BlockSpec(memory_space=pltpu.SMEM)
ANY = pl.BlockSpec(memory_space=pl.ANY)


def dot(lhs, rhs, dims):
    return lax.dot_general(lhs, rhs, (dims, ((), ())), preferred_element_type=F32)


def call(kernel, out_shape, fetched, at=None, scratch=(), either=None, flops=1):
    nf, n_out = len(fetched), len(out_shape)
    shapes = [v.shape[:-1] + (v.shape[-1] if w is None else w[1],) for v, w in fetched]
    sources = [v for v, _ in fetched] + ([] if either is None else list(either[:2]))
    buffers = [pltpu.VMEM(shape, v.dtype) for shape, (v, _) in zip(shapes, fetched)]
    if either is not None:
        lead, width = either[0].shape[:-1], either[2][1]
        buffers.append(pltpu.VMEM(lead + (width,), either[0].dtype))
        buffers.append(pltpu.SemaphoreType.DMA((lead[0],)))

    def body(*refs):
        refs = list(refs)
        head = [refs.pop(0)] if at is not None else []
        froms, refs = refs[: len(sources)], refs[len(sources) :]
        outs, refs = refs[:n_out], refs[n_out:]
        sems, held, extra = refs[0], refs[1 : 1 + len(buffers)], refs[1 + len(buffers) :]
        copies = []
        for i, (source, (_, columns)) in enumerate(zip(froms, fetched)):
            if columns is not None:
                first = (slice(None),) * (len(source.shape) - 1)
                source = source.at[first + (pl.ds(*columns),)]
            copies.append(pltpu.make_async_copy(source, held[i], sems.at[i]))
        for c in copies:
            c.start()
        if either is not None:
            one, other = froms[nf:]
            buffer, more = held[nf], held.pop()
            start = pl.multiple_of(head[0][1], 128)
            parts = [
                pltpu.make_async_copy(one.at[d, :, pl.ds(start, width)], buffer.at[d], more.at[d])
                for d in range(lead[0])
            ]
            others = [
                pltpu.make_async_copy(
                    other.at[d, :, pl.ds(*either[2])], buffer.at[d], more.at[d]
                )
                for d in range(lead[0])
            ]

            @pl.when(head[0][0] == 1)
            def _():
                for c in parts:
                    c.start()

            @pl.when(head[0][0] != 1)
            def _():
                for c in others:
                    c.start()

            copies.extend(others)
        for c in copies:
            c.wait()
        kernel(*head, *held[:nf], *outs, *held[nf:], *extra)

    return pl.pallas_call(
        body,
        out_shape=[jax.ShapeDtypeStruct(shape, dtype) for shape, dtype in out_shape],
        in_specs=[SMEM] * (at is not None) + [ANY] * len(sources),
        out_specs=[VMEM] * n_out,
        scratch_shapes=[pltpu.SemaphoreType.DMA((nf,)), *buffers, *scratch],
        compiler_params=pltpu.CompilerParams(vmem_limit_bytes=VMEM_BYTES),
        cost_estimate=pl.CostEstimate(flops=flops, bytes_accessed=1, transcendentals=0),
    )(*([at] if at is not None else []), *sources)


def slot_domain(count, lanes, gslots):
    slot = lax.broadcasted_iota(jnp.int32, (count, lanes), 0)
    return lax.rem(slot, gslots) // CAPD


def widen(v, gslots):
    domain = slot_domain(*v.shape, gslots)
    parts = [jnp.where(domain == e, v.astype(F32), 0.0).astype(v.dtype) for e in range(GROUP)]
    return jnp.concatenate(parts, axis=1)


def narrow(v, gslots):
    n = v.shape[1] // GROUP
    domain = slot_domain(v.shape[0], n, gslots)
    total = v[:, :n]
    for e in range(1, GROUP):
        total = jnp.where(domain == e, v[:, e * n : (e + 1) * n], total)
    return total


def group_rows(refs, g, gslots):
    rows = pl.ds(g * gslots, gslots)
    parts = []
    for r in refs:
        if len(r.shape) == 2:
            parts.append(r[rows, :])
        else:
            parts.extend(r[i, rows, :] for i in range(r.shape[0]))
    return jnp.concatenate(parts, axis=0)


def one_hot(dom, first, slots, ad, dom_total):
    rows = dom.shape[1]
    names = lax.broadcasted_iota(jnp.int32, (dom_total, rows), 0)
    is_dom = (names == dom).astype(F32)
    before = lax.broadcasted_iota(jnp.int32, (rows, rows), 0) < lax.broadcasted_iota(
        jnp.int32, (rows, rows), 1
    )
    prior = dot(is_dom.astype(BF16), before.astype(F32).astype(BF16), ((1,), (0,)))
    position = jnp.sum(prior * is_dom, axis=0, keepdims=True).astype(jnp.int32)
    slot = lax.broadcasted_iota(jnp.int32, (ad * slots, rows), 0)
    slot = lax.rem(slot + first * slots, ad * slots)
    return (slot == dom * CAPD + position).astype(F32).astype(BF16)


def own_kernel(ad, slots, dom_total, at, dom, x, dy, hot_ref, *outs):
    hot = one_hot(dom[...], at[0], slots, ad, dom_total)
    hot_ref[...] = hot
    width = x.shape[1]
    moved = dot(hot, x[...], ((1,), (0,))).astype(BF16)
    moved_dy = dot(hot, dy[...], ((1,), (0,))).astype(BF16)
    for ka in range(ad):
        outs[ka][:, :width] = moved[ka * slots : (ka + 1) * slots]
        outs[ka][:, width:] = moved_dy[ka * slots : (ka + 1) * slots]


def others_kernel(fsdp, ad, slots, dom_total, at, *refs):
    x_refs, outs = refs[: fsdp - 1], refs[fsdp - 1 :]
    for kf in range(fsdp - 1):
        rows = x_refs[kf].shape[0] - 16
        dom = x_refs[kf][rows:, :rows].astype(F32).astype(jnp.int32)[:1]
        hot = one_hot(dom, at[0], slots, ad, dom_total)
        moved = dot(hot, x_refs[kf][:rows, :], ((1,), (0,))).astype(BF16)
        for c in range(CHUNKS):
            for ka in range(ad):
                cw = outs[c * ad + ka].shape[2]
                part = moved[ka * slots : (ka + 1) * slots, c * cw : (c + 1) * cw]
                outs[c * ad + ka][kf] = part


def back_kernel(ad, gslots, *refs):
    dy_refs, up, out = refs[:ad], refs[ad], refs[ad + 1]
    for g in range(up.shape[0] // GROUP):
        rows = pl.ds(g * gslots, gslots)
        dy = jnp.concatenate([r[rows, :] for r in dy_refs], axis=0)
        weights = up[g * GROUP : (g + 1) * GROUP].reshape(-1, up.shape[2])
        part = narrow(dot(dy, weights, ((1,), (1,))), gslots)
        for ka in range(ad):
            out[ka, rows, :] = part[ka * gslots : (ka + 1) * gslots]


def both_kernel(ad, mine, got, *refs):
    dy_refs, out = refs[:ad], refs[ad]
    width = dy_refs[0].shape[1]
    for ka in range(ad):
        out[ka, :, :width] = dy_refs[ka][...]
        out[ka, :, width:] = (adapter_scale * (mine[ka] + got[ka])).astype(BF16)


def hidden_kernel(fsdp, gslots, at, *refs):
    count = (len(refs) - 3) // 2
    own_refs, x_refs, outs, held = refs[:count], refs[count:-3], refs[-3:-1], refs[-1]
    cw = held.shape[2]
    second = at[2] == 1
    for g in range(held.shape[0] // GROUP):
        weights = held[g * GROUP : (g + 1) * GROUP].reshape(-1, cw)
        rows = pl.ds(g * gslots, gslots)
        for i in range(count):
            x = group_rows((own_refs[i], x_refs[i]), g, gslots)
            part = narrow(dot(x, weights, ((1,), (1,))), gslots)
            n = part.shape[1] // 2
            halves = jnp.where(second, part[:, n:], part[:, :n])
            others = jnp.where(second, part[:, :n], part[:, n:])
            for kf in range(fsdp):
                outs[0][kf, i, rows, :] = halves[kf * gslots : (kf + 1) * gslots]
                outs[1][kf, i, rows, :] = others[kf * gslots : (kf + 1) * gslots]


def down_grad_kernel(fsdp, ad, gslots, at, *refs):
    own_refs, x_refs, back_refs = refs[:ad], refs[ad : 2 * ad], refs[2 * ad : 2 * ad + fsdp]
    outs, total = refs[2 * ad + fsdp : -1], refs[-1]
    rloc = outs[0].shape[1]
    rank = back_refs[0].shape[2]
    for g in range(outs[0].shape[0] // GROUP):
        rows = pl.ds(g * gslots, gslots)
        x = group_rows([r for pair in zip(own_refs, x_refs) for r in pair], g, gslots)
        back = [back_refs[kf][ka, rows, :] for ka in range(ad) for kf in range(fsdp)]
        back = widen(jnp.concatenate(back, axis=0), gslots)
        total[...] = dot(back, x, ((0,), (0,)))
        for r in range(fsdp):
            for e in range(GROUP):
                first = pl.multiple_of(e * rank + at[r] * rloc, rloc)
                outs[r][g * GROUP + e] = total[pl.ds(first, rloc), :].astype(BF16)


def delta_kernel(fsdp, ad, gslots, at, own, got, up, *outs):
    for g in range(up.shape[0] // GROUP):
        rows = pl.ds(g * gslots, gslots)
        mine = jnp.concatenate([own[ka, rows, :] for ka in range(ad)], axis=0)
        other = jnp.concatenate([got[ka, rows, :] for ka in range(ad)], axis=0)
        second = at[0] == 1
        low = jnp.where(second, other.astype(F32), mine.astype(F32))
        high = jnp.where(second, mine.astype(F32), other.astype(F32))
        hidden = jnp.concatenate([low, high], axis=1)
        weights = up[g * GROUP : (g + 1) * GROUP].reshape(-1, up.shape[2])
        delta = dot(widen(hidden.astype(BF16), gslots), weights, ((1,), (0,)))
        delta = (adapter_scale * delta).astype(BF16)
        rloc = hidden.shape[1] // fsdp
        for ka in range(ad):
            outs[ka][rows, :] = delta[ka * gslots : (ka + 1) * gslots]
        for kf in range(fsdp):
            part = hidden[:, :rloc]
            for i in range(1, fsdp):
                part = jnp.where(at[1 + kf] == i, hidden[:, i * rloc : (i + 1) * rloc], part)
            part = part.astype(BF16)
            for ka in range(ad):
                outs[ad + kf][ka, rows, :] = part[ka * gslots : (ka + 1) * gslots]


def up_grad_kernel(fsdp, ad, gslots, *refs):
    hid_refs, dy_refs, out = refs[:fsdp], refs[fsdp:-1], refs[-1]
    rloc = hid_refs[0].shape[2]
    for g in range(out.shape[0] // GROUP):
        hid = group_rows(hid_refs, g, gslots)
        dy = group_rows(dy_refs, g, gslots)
        domain = slot_domain(hid.shape[0], rloc, gslots)
        wide = [jnp.where(domain == e, hid.astype(F32), 0.0) for e in range(GROUP)]
        wide = jnp.concatenate(wide, axis=1).astype(BF16)
        total = adapter_scale * dot(wide, dy, ((0,), (0,)))
        for e in range(GROUP):
            out[g * GROUP + e] = total[e * rloc : (e + 1) * rloc]


def output_kernel(fsdp, ad, *refs):
    base, hot, rows, out = refs[:fsdp], refs[fsdp], refs[fsdp + 1 : -1], refs[-1]
    total = base[0][...]
    for k in range(1, fsdp):
        total = total + base[k][...]
    delta = jnp.concatenate([r[...] for r in rows], axis=0)
    out[...] = (total + dot(hot[...], delta, ((0,), (0,)))).astype(BF16)


def base_kernel(fsdp, at, own, *refs):
    mine, got = refs[: fsdp - 1], refs[fsdp - 1 : 2 * fsdp - 2]
    weight, outs = refs[2 * fsdp - 2], refs[2 * fsdp - 1 :]
    rows, kt = own.shape[0], mine[0].shape[1]
    outs[0][...] = dot(own[...], weight[...], ((1,), (0,)))
    w_mine = weight[pl.ds(pl.multiple_of(at[0] * kt, kt), kt), :]
    w_got = weight[pl.ds(pl.multiple_of((1 - at[0]) * kt, kt), kt), :]
    for k in range(1, fsdp):
        total = dot(mine[k - 1][:rows, :], w_mine, ((1,), (0,)))
        outs[k][...] = total + dot(got[k - 1][:rows, :], w_got, ((1,), (0,)))


def column_body(
    input_rows,
    value_weight_frozen,
    adapter_down_weight,
    adapter_up_weight,
    layer_output_gradient,
    domain,
):
    fsdp, ad = lax.axis_size("fsdp"), lax.axis_size("ad")
    f, t, a = lax.axis_index("fsdp"), lax.axis_index("tp"), lax.axis_index("ad")
    fy, fx = f // 2, f % 2
    rows, width = input_rows.shape
    dloc, rank, half = adapter_down_weight.shape
    vloc = adapter_up_weight.shape[2]
    rloc = rank // fsdp
    kf_width = width // fsdp
    kt = kf_width // 2
    slots = dloc * CAPD
    gslots = GROUP * CAPD
    cw = kt // CHUNKS

    def over_f(v, k):
        return lax.ppermute(v, "fsdp", [(i, i ^ k) for i in range(fsdp)]) if k else v

    def over_a(v, k):
        return lax.ppermute(v, "ad", [(i, (i + k) % ad) for i in range(ad)]) if k else v

    def swap(v):
        return lax.ppermute(v, "tp", [(0, 1), (1, 0)])

    def numbers(*values):
        return jnp.stack([jnp.asarray(v, jnp.int32) for v in values])

    def after(v, *others):
        return lax.optimization_barrier((v, others))[0]

    x_in = []
    for k in range(fsdp):
        block = lax.dynamic_slice_in_dim(input_rows, (f ^ k) * kf_width + t * kt, kt, 1)
        if k:
            dom_row = jnp.pad(domain.T.astype(BF16), ((0, 15), (0, kt - rows)))
            block = jnp.concatenate([block, dom_row], axis=0)
        x_in.append(block)
    x_in = lax.optimization_barrier(x_in)
    x_in[1], x_in[2] = over_f(x_in[1], 1), over_f(x_in[2], 2)
    x_in[3] = over_f(x_in[3], 3)

    hot, *sends = call(
        functools.partial(own_kernel, ad, slots, ad * dloc),
        [((ad * slots, rows), BF16)] + [((slots, kt + vloc), BF16)] * ad,
        [(v, None) for v in (domain.T, x_in[0], layer_output_gradient)],
        at=numbers(a),
    )
    held = after((adapter_down_weight, input_rows), *sends)
    sends[-1] = after(sends[-1], x_in[1])
    own = [over_a(v, ka) for ka, v in enumerate(sends)]

    down_other = lax.dynamic_slice_in_dim(held[0], (fx * 2 + 1 - t) * kt, kt, 2)
    pairs = [(i * 2 + i // 2, i * 2 + 1 - i // 2) for i in range(fsdp)]

    x_chip = lax.dynamic_slice_in_dim(held[1], f * kf_width, kf_width, 1)
    x_in, own, down_other, x_chip = lax.optimization_barrier((x_in, own, down_other, x_chip))
    x_other = [swap(v) for v in x_in[1:]]
    down_got = lax.ppermute(down_other, ("fsdp", "tp"), pairs)
    sends = call(
        functools.partial(others_kernel, fsdp, ad, slots, ad * dloc),
        [((fsdp - 1, slots, cw), BF16)] * (CHUNKS * ad),
        [(v, None) for v in x_in[1:]],
        at=numbers(a),
    )
    x_routed = [[over_a(v, ka) for ka, v in enumerate(sends[:ad])]]

    base = call(
        functools.partial(base_kernel, fsdp),
        [((rows, vloc), F32)] * fsdp,
        [(v, None) for v in (x_chip, *x_in[1:], *after(x_other, *sends), value_weight_frozen)],
        at=numbers(t),
    )
    dy = [(v, (kt, vloc)) for v in after(own, base[0], down_got)]
    base = [over_f(v, k) for k, v in enumerate(base)]

    (back,) = call(
        functools.partial(back_kernel, ad, gslots),
        [((ad, slots, rank), F32)],
        [*dy, (adapter_up_weight, None)],
        flops=10**10,
    )
    (both,) = call(
        functools.partial(both_kernel, ad),
        [((ad, slots, vloc + rank), BF16)],
        [(back, None), (swap(back), None), *dy],
    )
    both = after(both, *base, x_routed[0][2])
    both = [over_f(both, k) for k in range(fsdp)]

    def hidden(shifts, routed):
        return call(
            functools.partial(hidden_kernel, fsdp, gslots),
            [((fsdp, len(shifts), slots, rank // 2), F32)] * 2,
            [(own[ka], (0, kt)) for ka in shifts] + [(v, None) for v in routed],
            at=numbers(t == fy, fx * kf_width + t * kt, t),
            either=(adapter_down_weight, down_got, (0, kt)),
            flops=10**10,
        )

    early, late = [ka for ka in range(ad) if ka % 2 == 0], [ka for ka in range(ad) if ka % 2]
    hid_early = hidden(early, after([x_routed[0][ka] for ka in early], both[0]))
    x_last = after(x_routed[0], *base, *hid_early)
    hid_late = hidden(late, [x_last[ka] for ka in late])
    x_last, both = after((x_last, both), *hid_late)
    hid = jnp.concatenate(
        [hid_early[0] + swap(hid_early[1]), hid_late[0] + swap(hid_late[1])], axis=1
    )

    sums = call(
        functools.partial(down_grad_kernel, fsdp, ad, gslots),
        [((dloc, rloc, kt), BF16)] * fsdp,
        [(v, (0, kt)) for v in own]
        + [(v, None) for v in x_last]
        + [(v, (vloc, rank)) for v in both],
        at=numbers(*[(t ^ (r // 2)) * 2 + (fx ^ (r % 2)) for r in range(fsdp)]),
        scratch=[pltpu.VMEM((GROUP * rank, kt), F32)],
        flops=10**10,
    )
    hid = [over_f(hid[k], k) for k in range(fsdp)]
    hid_own = (hid[0] + hid[1] + hid[2] + hid[3]).astype(BF16)
    shift_order = [(early + late).index(ka) for ka in range(ad)]
    hid_own = jnp.concatenate([hid_own[i : i + 1] for i in shift_order], axis=0)
    outs = call(
        functools.partial(delta_kernel, fsdp, ad, gslots),
        [((slots, vloc), BF16)] * ad + [((ad, slots, rloc), BF16)] * fsdp,
        [(v, None) for v in (hid_own, swap(hid_own), adapter_up_weight)],
        at=numbers(t, *[f ^ k for k in range(fsdp)]),
    )
    returned = [over_a(v, (ad - ka) % ad) for ka, v in enumerate(outs[:ad])]
    grad_a = jnp.zeros((dloc, rloc, half), F32)
    hid_cols, grad_a = after((outs[ad:], grad_a), *returned[1:])
    hid_cols = [over_f(v, k) for k, v in enumerate(hid_cols)]
    got = []
    for r in range(fsdp):
        p, q = r % 2, r // 2
        perm = [
            ((y * 2 + x) * 2 + s, ((s ^ q) * 2 + (x ^ p)) * 2 + y)
            for y in range(2)
            for x in range(2)
            for s in range(2)
        ]
        block = after(sums[r], *(hid[1:] if r < 2 else [*got[:2], *returned[1:]]))
        got.append(lax.ppermute(block, ("fsdp", "tp"), perm))
        at = (fx ^ p) * kf_width + (fy ^ q) * kt
        grad_a = lax.dynamic_update_slice_in_dim(grad_a, got[r].astype(F32), at, 2)

    (y_out,) = call(
        functools.partial(output_kernel, fsdp, ad),
        [((rows, vloc), BF16)],
        [(v, None) for v in (*base, hot, *returned)],
    )
    (grad_b,) = call(
        functools.partial(up_grad_kernel, fsdp, ad, gslots),
        [((dloc, rloc, vloc), F32)],
        [(v, None) for v in hid_cols] + [(v, (0, vloc)) for v in both],
    )
    return y_out, grad_a, grad_b


def solution(mesh):
    placed = (
        P(("fsdp", "ad"), None),
        P("fsdp", "tp"),
        P("ad", None, "tp"),
        P("ad", None, "tp"),
        P(("fsdp", "ad"), "tp"),
        P(("fsdp", "ad"), None),
    )
    square = mesh.shape["fsdp"] == 4 and mesh.shape["tp"] == 2 and mesh.shape["ad"] == 4
    return jax.shard_map(
        column_body if square else general_body,
        mesh=mesh,
        in_specs=placed,
        out_specs=(P(("fsdp", "ad"), "tp"), P("ad", "fsdp", "tp"), P("ad", "fsdp", "tp")),
        check_vma=False,
    )
```

```python
import functools

import jax
import jax.numpy as jnp
from jax import lax
from jax.experimental import pallas as pl
from jax.experimental.pallas import tpu as pltpu
from jax.sharding import PartitionSpec as P

CAPD = 12
GROUP = 4
CHUNKS = 1

adapter_scale = 0.5


def slot_places(dom_ids, dom_total):
    row_count = dom_ids.shape[0]
    onehot = (dom_ids[:, None] == jnp.arange(dom_total, dtype=jnp.int32)[None, :]).astype(
        jnp.float32
    )
    row_iota = jnp.arange(row_count, dtype=jnp.int32)
    earlier = (row_iota[:, None] > row_iota[None, :]).astype(jnp.float32)
    prior = jnp.dot(earlier, onehot, preferred_element_type=jnp.float32)
    position = jnp.sum(prior * onehot, axis=1).astype(jnp.int32)
    return dom_ids * CAPD + position


def general_body(
    input_rows,
    value_weight_frozen,
    adapter_down_weight,
    adapter_up_weight,
    layer_output_gradient,
    domain,
):
    row_count = input_rows.shape[0]
    domain_local = adapter_down_weight.shape[0]
    width_local = adapter_down_weight.shape[2]
    value_width_local = adapter_up_weight.shape[2]
    ad_count = lax.axis_size("ad")
    slot_total = ad_count * domain_local * CAPD
    place = slot_places(domain[:, 0], ad_count * domain_local)
    row_iota = jnp.arange(row_count, dtype=jnp.int32)
    matches = place[None, :] == jnp.arange(slot_total, dtype=jnp.int32)[:, None]
    filled = jnp.any(matches, axis=1)
    source_row = jnp.sum(jnp.where(matches, row_iota[None, :], 0), axis=1)
    base = jnp.dot(
        input_rows,
        lax.all_gather(value_weight_frozen, "fsdp", axis=0, tiled=True),
        preferred_element_type=jnp.float32,
    )
    feature_cols = lax.dynamic_slice_in_dim(
        input_rows, lax.axis_index("tp") * width_local, width_local, 1
    )
    zero_value = jnp.zeros((), jnp.bfloat16)
    send_x = jnp.where(filled[:, None], feature_cols[source_row], zero_value)
    send_dy = jnp.where(filled[:, None], layer_output_gradient[source_row], zero_value)
    send_x = send_x.reshape(ad_count, domain_local * CAPD, width_local)
    send_dy = send_dy.reshape(ad_count, domain_local * CAPD, value_width_local)
    got_x = lax.all_to_all(send_x, "ad", split_axis=0, concat_axis=0, tiled=True)
    got_dy = lax.all_to_all(send_dy, "ad", split_axis=0, concat_axis=0, tiled=True)
    rows = got_x.reshape(ad_count, domain_local, CAPD, width_local)
    grads = got_dy.reshape(ad_count, domain_local, CAPD, value_width_local)
    f32 = dict(preferred_element_type=jnp.float32)
    hidden, back = lax.psum(
        (
            jnp.einsum("vqfj,qwj->vqfw", rows, adapter_down_weight, **f32),
            jnp.einsum("amgy,mzy->amgz", grads, adapter_up_weight, **f32),
        ),
        "tp",
    )
    hidden = hidden.astype(jnp.bfloat16)
    back = (adapter_scale * back).astype(jnp.bfloat16)
    delta = adapter_scale * jnp.einsum("lokh,ohi->loki", hidden, adapter_up_weight, **f32)
    delta = delta.astype(jnp.bfloat16).reshape(ad_count, domain_local * CAPD, value_width_local)
    part_a = jnp.einsum("sdcr,sdcx->drx", back, rows, **f32)
    part_b = adapter_scale * jnp.einsum("sdcr,sdce->dre", hidden, grads, **f32)
    returned = lax.all_to_all(delta, "ad", split_axis=0, concat_axis=0, tiled=True)
    returned = returned.reshape(slot_total, value_width_local)
    y_out = (base + returned[place].astype(jnp.float32)).astype(jnp.bfloat16)
    return (
        y_out,
        lax.psum_scatter(part_a, "fsdp", scatter_dimension=1, tiled=True),
        lax.psum_scatter(part_b, "fsdp", scatter_dimension=1, tiled=True),
    )


BF16, F32 = jnp.bfloat16, jnp.float32
VMEM_BYTES = 58 << 20
VMEM = pl.BlockSpec(memory_space=pltpu.VMEM)
SMEM = pl.BlockSpec(memory_space=pltpu.SMEM)
ANY = pl.BlockSpec(memory_space=pl.ANY)


def dot(lhs, rhs, dims):
    return lax.dot_general(lhs, rhs, (dims, ((), ())), preferred_element_type=F32)


def call(kernel, out_shape, fetched, at=None, scratch=(), either=None, flops=1):
    nf, n_out = len(fetched), len(out_shape)
    shapes = [v.shape[:-1] + (v.shape[-1] if w is None else w[1],) for v, w in fetched]
    sources = [v for v, _ in fetched] + ([] if either is None else list(either[:2]))
    buffers = [pltpu.VMEM(shape, v.dtype) for shape, (v, _) in zip(shapes, fetched)]
    if either is not None:
        lead, width = either[0].shape[:-1], either[2][1]
        buffers.append(pltpu.VMEM(lead + (width,), either[0].dtype))
        buffers.append(pltpu.SemaphoreType.DMA((lead[0],)))

    def body(*refs):
        refs = list(refs)
        head = [refs.pop(0)] if at is not None else []
        froms, refs = refs[: len(sources)], refs[len(sources) :]
        outs, refs = refs[:n_out], refs[n_out:]
        sems, held, extra = refs[0], refs[1 : 1 + len(buffers)], refs[1 + len(buffers) :]
        copies = []
        for i, (source, (_, columns)) in enumerate(zip(froms, fetched)):
            if columns is not None:
                first = (slice(None),) * (len(source.shape) - 1)
                source = source.at[first + (pl.ds(*columns),)]
            copies.append(pltpu.make_async_copy(source, held[i], sems.at[i]))
        for c in copies:
            c.start()
        if either is not None:
            one, other = froms[nf:]
            buffer, more = held[nf], held.pop()
            start = pl.multiple_of(head[0][1], 128)
            parts = [
                pltpu.make_async_copy(one.at[d, :, pl.ds(start, width)], buffer.at[d], more.at[d])
                for d in range(lead[0])
            ]
            others = [
                pltpu.make_async_copy(
                    other.at[d, :, pl.ds(*either[2])], buffer.at[d], more.at[d]
                )
                for d in range(lead[0])
            ]

            @pl.when(head[0][0] == 1)
            def _():
                for c in parts:
                    c.start()

            @pl.when(head[0][0] != 1)
            def _():
                for c in others:
                    c.start()

            copies.extend(others)
        for c in copies:
            c.wait()
        kernel(*head, *held[:nf], *outs, *held[nf:], *extra)

    return pl.pallas_call(
        body,
        out_shape=[jax.ShapeDtypeStruct(shape, dtype) for shape, dtype in out_shape],
        in_specs=[SMEM] * (at is not None) + [ANY] * len(sources),
        out_specs=[VMEM] * n_out,
        scratch_shapes=[pltpu.SemaphoreType.DMA((nf,)), *buffers, *scratch],
        compiler_params=pltpu.CompilerParams(vmem_limit_bytes=VMEM_BYTES),
        cost_estimate=pl.CostEstimate(flops=flops, bytes_accessed=1, transcendentals=0),
    )(*([at] if at is not None else []), *sources)


def slot_domain(count, lanes, gslots):
    slot = lax.broadcasted_iota(jnp.int32, (count, lanes), 0)
    return lax.rem(slot, gslots) // CAPD


def widen(v, gslots):
    domain = slot_domain(*v.shape, gslots)
    parts = [jnp.where(domain == e, v.astype(F32), 0.0).astype(v.dtype) for e in range(GROUP)]
    return jnp.concatenate(parts, axis=1)


def narrow(v, gslots):
    n = v.shape[1] // GROUP
    domain = slot_domain(v.shape[0], n, gslots)
    total = v[:, :n]
    for e in range(1, GROUP):
        total = jnp.where(domain == e, v[:, e * n : (e + 1) * n], total)
    return total


def group_rows(refs, g, gslots):
    rows = pl.ds(g * gslots, gslots)
    parts = []
    for r in refs:
        if len(r.shape) == 2:
            parts.append(r[rows, :])
        else:
            parts.extend(r[i, rows, :] for i in range(r.shape[0]))
    return jnp.concatenate(parts, axis=0)


def one_hot(dom, first, slots, ad, dom_total):
    rows = dom.shape[1]
    names = lax.broadcasted_iota(jnp.int32, (dom_total, rows), 0)
    is_dom = (names == dom).astype(F32)
    before = lax.broadcasted_iota(jnp.int32, (rows, rows), 0) < lax.broadcasted_iota(
        jnp.int32, (rows, rows), 1
    )
    prior = dot(is_dom.astype(BF16), before.astype(F32).astype(BF16), ((1,), (0,)))
    position = jnp.sum(prior * is_dom, axis=0, keepdims=True).astype(jnp.int32)
    slot = lax.broadcasted_iota(jnp.int32, (ad * slots, rows), 0)
    slot = lax.rem(slot + first * slots, ad * slots)
    return (slot == dom * CAPD + position).astype(F32).astype(BF16)


def own_kernel(ad, slots, dom_total, at, dom, x, dy, hot_ref, *outs):
    hot = one_hot(dom[...], at[0], slots, ad, dom_total)
    hot_ref[...] = hot
    width = x.shape[1]
    moved = dot(hot, x[...], ((1,), (0,))).astype(BF16)
    moved_dy = dot(hot, dy[...], ((1,), (0,))).astype(BF16)
    for ka in range(ad):
        outs[ka][:, :width] = moved[ka * slots : (ka + 1) * slots]
        outs[ka][:, width:] = moved_dy[ka * slots : (ka + 1) * slots]


def others_kernel(fsdp, ad, slots, dom_total, at, *refs):
    x_refs, outs = refs[: fsdp - 1], refs[fsdp - 1 :]
    for kf in range(fsdp - 1):
        rows = x_refs[kf].shape[0] - 16
        dom = x_refs[kf][rows:, :rows].astype(F32).astype(jnp.int32)[:1]
        hot = one_hot(dom, at[0], slots, ad, dom_total)
        moved = dot(hot, x_refs[kf][:rows, :], ((1,), (0,))).astype(BF16)
        for c in range(CHUNKS):
            for ka in range(ad):
                cw = outs[c * ad + ka].shape[2]
                part = moved[ka * slots : (ka + 1) * slots, c * cw : (c + 1) * cw]
                outs[c * ad + ka][kf] = part


def back_kernel(ad, gslots, *refs):
    dy_refs, up, out = refs[:ad], refs[ad], refs[ad + 1]
    for g in range(up.shape[0] // GROUP):
        rows = pl.ds(g * gslots, gslots)
        dy = jnp.concatenate([r[rows, :] for r in dy_refs], axis=0)
        weights = up[g * GROUP : (g + 1) * GROUP].reshape(-1, up.shape[2])
        part = narrow(dot(dy, weights, ((1,), (1,))), gslots)
        for ka in range(ad):
            out[ka, rows, :] = part[ka * gslots : (ka + 1) * gslots]


def both_kernel(ad, mine, got, *refs):
    dy_refs, out = refs[:ad], refs[ad]
    width = dy_refs[0].shape[1]
    for ka in range(ad):
        out[ka, :, :width] = dy_refs[ka][...]
        out[ka, :, width:] = (adapter_scale * (mine[ka] + got[ka])).astype(BF16)


def hidden_kernel(fsdp, gslots, at, *refs):
    count = (len(refs) - 3) // 2
    own_refs, x_refs, outs, held = refs[:count], refs[count:-3], refs[-3:-1], refs[-1]
    cw = held.shape[2]
    second = at[2] == 1
    for g in range(held.shape[0] // GROUP):
        weights = held[g * GROUP : (g + 1) * GROUP].reshape(-1, cw)
        rows = pl.ds(g * gslots, gslots)
        for i in range(count):
            x = group_rows((own_refs[i], x_refs[i]), g, gslots)
            part = narrow(dot(x, weights, ((1,), (1,))), gslots)
            n = part.shape[1] // 2
            halves = jnp.where(second, part[:, n:], part[:, :n])
            others = jnp.where(second, part[:, :n], part[:, n:])
            for kf in range(fsdp):
                outs[0][kf, i, rows, :] = halves[kf * gslots : (kf + 1) * gslots]
                outs[1][kf, i, rows, :] = others[kf * gslots : (kf + 1) * gslots]


def down_grad_kernel(fsdp, ad, gslots, at, *refs):
    own_refs, x_refs, back_refs = refs[:ad], refs[ad : 2 * ad], refs[2 * ad : 2 * ad + fsdp]
    outs, total = refs[2 * ad + fsdp : -1], refs[-1]
    rloc = outs[0].shape[1]
    rank = back_refs[0].shape[2]
    for g in range(outs[0].shape[0] // GROUP):
        rows = pl.ds(g * gslots, gslots)
        x = group_rows([r for pair in zip(own_refs, x_refs) for r in pair], g, gslots)
        back = [back_refs[kf][ka, rows, :] for ka in range(ad) for kf in range(fsdp)]
        back = widen(jnp.concatenate(back, axis=0), gslots)
        total[...] = dot(back, x, ((0,), (0,)))
        for r in range(fsdp):
            for e in range(GROUP):
                first = pl.multiple_of(e * rank + at[r] * rloc, rloc)
                outs[r][g * GROUP + e] = total[pl.ds(first, rloc), :].astype(BF16)


def delta_kernel(fsdp, ad, gslots, at, own, got, up, *outs):
    for g in range(up.shape[0] // GROUP):
        rows = pl.ds(g * gslots, gslots)
        mine = jnp.concatenate([own[ka, rows, :] for ka in range(ad)], axis=0)
        other = jnp.concatenate([got[ka, rows, :] for ka in range(ad)], axis=0)
        second = at[0] == 1
        low = jnp.where(second, other.astype(F32), mine.astype(F32))
        high = jnp.where(second, mine.astype(F32), other.astype(F32))
        hidden = jnp.concatenate([low, high], axis=1)
        weights = up[g * GROUP : (g + 1) * GROUP].reshape(-1, up.shape[2])
        delta = dot(widen(hidden.astype(BF16), gslots), weights, ((1,), (0,)))
        delta = (adapter_scale * delta).astype(BF16)
        rloc = hidden.shape[1] // fsdp
        for ka in range(ad):
            outs[ka][rows, :] = delta[ka * gslots : (ka + 1) * gslots]
        for kf in range(fsdp):
            part = hidden[:, :rloc]
            for i in range(1, fsdp):
                part = jnp.where(at[1 + kf] == i, hidden[:, i * rloc : (i + 1) * rloc], part)
            part = part.astype(BF16)
            for ka in range(ad):
                outs[ad + kf][ka, rows, :] = part[ka * gslots : (ka + 1) * gslots]


def up_grad_kernel(fsdp, ad, gslots, *refs):
    hid_refs, dy_refs, out = refs[:fsdp], refs[fsdp:-1], refs[-1]
    rloc = hid_refs[0].shape[2]
    for g in range(out.shape[0] // GROUP):
        hid = group_rows(hid_refs, g, gslots)
        dy = group_rows(dy_refs, g, gslots)
        domain = slot_domain(hid.shape[0], rloc, gslots)
        wide = [jnp.where(domain == e, hid.astype(F32), 0.0) for e in range(GROUP)]
        wide = jnp.concatenate(wide, axis=1).astype(BF16)
        total = adapter_scale * dot(wide, dy, ((0,), (0,)))
        for e in range(GROUP):
            out[g * GROUP + e] = total[e * rloc : (e + 1) * rloc]


def output_kernel(fsdp, ad, *refs):
    base, hot, rows, out = refs[:fsdp], refs[fsdp], refs[fsdp + 1 : -1], refs[-1]
    total = base[0][...]
    for k in range(1, fsdp):
        total = total + base[k][...]
    delta = jnp.concatenate([r[...] for r in rows], axis=0)
    out[...] = (total + dot(hot[...], delta, ((0,), (0,)))).astype(BF16)


def base_kernel(fsdp, at, own, *refs):
    mine, got = refs[: fsdp - 1], refs[fsdp - 1 : 2 * fsdp - 2]
    weight, outs = refs[2 * fsdp - 2], refs[2 * fsdp - 1 :]
    rows, kt = own.shape[0], mine[0].shape[1]
    outs[0][...] = dot(own[...], weight[...], ((1,), (0,)))
    w_mine = weight[pl.ds(pl.multiple_of(at[0] * kt, kt), kt), :]
    w_got = weight[pl.ds(pl.multiple_of((1 - at[0]) * kt, kt), kt), :]
    for k in range(1, fsdp):
        total = dot(mine[k - 1][:rows, :], w_mine, ((1,), (0,)))
        outs[k][...] = total + dot(got[k - 1][:rows, :], w_got, ((1,), (0,)))


def column_body(
    input_rows,
    value_weight_frozen,
    adapter_down_weight,
    adapter_up_weight,
    layer_output_gradient,
    domain,
):
    fsdp, ad = lax.axis_size("fsdp"), lax.axis_size("ad")
    f, t, a = lax.axis_index("fsdp"), lax.axis_index("tp"), lax.axis_index("ad")
    fy, fx = f // 2, f % 2
    rows, width = input_rows.shape
    dloc, rank, half = adapter_down_weight.shape
    vloc = adapter_up_weight.shape[2]
    rloc = rank // fsdp
    kf_width = width // fsdp
    kt = kf_width // 2
    slots = dloc * CAPD
    gslots = GROUP * CAPD
    cw = kt // CHUNKS

    def over_f(v, k):
        return lax.ppermute(v, "fsdp", [(i, i ^ k) for i in range(fsdp)]) if k else v

    def over_a(v, k):
        return lax.ppermute(v, "ad", [(i, (i + k) % ad) for i in range(ad)]) if k else v

    def swap(v):
        return lax.ppermute(v, "tp", [(0, 1), (1, 0)])

    def numbers(*values):
        return jnp.stack([jnp.asarray(v, jnp.int32) for v in values])

    def after(v, *others):
        return lax.optimization_barrier((v, others))[0]

    x_in = []
    for k in range(fsdp):
        block = lax.dynamic_slice_in_dim(input_rows, (f ^ k) * kf_width + t * kt, kt, 1)
        if k:
            dom_row = jnp.pad(domain.T.astype(BF16), ((0, 15), (0, kt - rows)))
            block = jnp.concatenate([block, dom_row], axis=0)
        x_in.append(block)
    x_in = lax.optimization_barrier(x_in)
    x_in[1], x_in[2] = over_f(x_in[1], 1), over_f(x_in[2], 2)
    x_in[3] = over_f(x_in[3], 3)

    hot, *sends = call(
        functools.partial(own_kernel, ad, slots, ad * dloc),
        [((ad * slots, rows), BF16)] + [((slots, kt + vloc), BF16)] * ad,
        [(v, None) for v in (domain.T, x_in[0], layer_output_gradient)],
        at=numbers(a),
    )
    held = after((adapter_down_weight, input_rows), *sends)
    sends[-1] = after(sends[-1], x_in[1])
    own = [over_a(v, ka) for ka, v in enumerate(sends)]

    down_other = lax.dynamic_slice_in_dim(held[0], (fx * 2 + 1 - t) * kt, kt, 2)
    pairs = [(i * 2 + i // 2, i * 2 + 1 - i // 2) for i in range(fsdp)]

    x_chip = lax.dynamic_slice_in_dim(held[1], f * kf_width, kf_width, 1)
    x_in, own, down_other, x_chip = lax.optimization_barrier((x_in, own, down_other, x_chip))
    x_other = [swap(v) for v in x_in[1:]]
    down_got = lax.ppermute(down_other, ("fsdp", "tp"), pairs)
    sends = call(
        functools.partial(others_kernel, fsdp, ad, slots, ad * dloc),
        [((fsdp - 1, slots, cw), BF16)] * (CHUNKS * ad),
        [(v, None) for v in x_in[1:]],
        at=numbers(a),
    )
    x_routed = [[over_a(v, ka) for ka, v in enumerate(sends[:ad])]]

    base = call(
        functools.partial(base_kernel, fsdp),
        [((rows, vloc), F32)] * fsdp,
        [(v, None) for v in (x_chip, *x_in[1:], *after(x_other, *sends), value_weight_frozen)],
        at=numbers(t),
    )
    dy = [(v, (kt, vloc)) for v in after(own, base[0], down_got)]
    base = [over_f(v, k) for k, v in enumerate(base)]

    (back,) = call(
        functools.partial(back_kernel, ad, gslots),
        [((ad, slots, rank), F32)],
        [*dy, (adapter_up_weight, None)],
        flops=10**10,
    )
    (both,) = call(
        functools.partial(both_kernel, ad),
        [((ad, slots, vloc + rank), BF16)],
        [(back, None), (swap(back), None), *dy],
    )
    both = after(both, *base, x_routed[0][2])
    both = [over_f(both, k) for k in range(fsdp)]

    def hidden(shifts, routed):
        return call(
            functools.partial(hidden_kernel, fsdp, gslots),
            [((fsdp, len(shifts), slots, rank // 2), F32)] * 2,
            [(own[ka], (0, kt)) for ka in shifts] + [(v, None) for v in routed],
            at=numbers(t == fy, fx * kf_width + t * kt, t),
            either=(adapter_down_weight, down_got, (0, kt)),
            flops=10**10,
        )

    early, late = [ka for ka in range(ad) if ka % 2 == 0], [ka for ka in range(ad) if ka % 2]
    hid_early = hidden(early, after([x_routed[0][ka] for ka in early], both[0]))
    x_last = after(x_routed[0], *base, *hid_early)
    hid_late = hidden(late, [x_last[ka] for ka in late])
    x_last, both = after((x_last, both), *hid_late)
    hid = jnp.concatenate(
        [hid_early[0] + swap(hid_early[1]), hid_late[0] + swap(hid_late[1])], axis=1
    )

    sums = call(
        functools.partial(down_grad_kernel, fsdp, ad, gslots),
        [((dloc, rloc, kt), BF16)] * fsdp,
        [(v, (0, kt)) for v in own]
        + [(v, None) for v in x_last]
        + [(v, (vloc, rank)) for v in both],
        at=numbers(*[(t ^ (r // 2)) * 2 + (fx ^ (r % 2)) for r in range(fsdp)]),
        scratch=[pltpu.VMEM((GROUP * rank, kt), F32)],
        flops=10**10,
    )
    hid = [over_f(hid[k], k) for k in range(fsdp)]
    hid_own = (hid[0] + hid[1] + hid[2] + hid[3]).astype(BF16)
    shift_order = [(early + late).index(ka) for ka in range(ad)]
    hid_own = jnp.concatenate([hid_own[i : i + 1] for i in shift_order], axis=0)
    outs = call(
        functools.partial(delta_kernel, fsdp, ad, gslots),
        [((slots, vloc), BF16)] * ad + [((ad, slots, rloc), BF16)] * fsdp,
        [(v, None) for v in (hid_own, swap(hid_own), adapter_up_weight)],
        at=numbers(t, *[f ^ k for k in range(fsdp)]),
    )
    hid_cols = [over_f(v, k) for k, v in enumerate(outs[ad:])]
    returned = after(outs[:ad], *hid_cols[1:])
    returned = [over_a(v, (ad - ka) % ad) for ka, v in enumerate(returned)]
    grad_a = jnp.zeros((dloc, rloc, half), F32)
    got = []
    for r in range(fsdp):
        p, q = r % 2, r // 2
        perm = [
            ((y * 2 + x) * 2 + s, ((s ^ q) * 2 + (x ^ p)) * 2 + y)
            for y in range(2)
            for x in range(2)
            for s in range(2)
        ]
        block = after(sums[r], *(hid[1:] if r < 2 else [*got[:2], *hid_cols[1:]]))
        got.append(lax.ppermute(block, ("fsdp", "tp"), perm))
        at = (fx ^ p) * kf_width + (fy ^ q) * kt
        grad_a = lax.dynamic_update_slice_in_dim(grad_a, got[r].astype(F32), at, 2)

    (y_out,) = call(
        functools.partial(output_kernel, fsdp, ad),
        [((rows, vloc), BF16)],
        [(v, None) for v in (*base, hot, *returned)],
    )
    (grad_b,) = call(
        functools.partial(up_grad_kernel, fsdp, ad, gslots),
        [((dloc, rloc, vloc), F32)],
        [(v, None) for v in hid_cols] + [(v, (0, vloc)) for v in both],
    )
    return y_out, grad_a, grad_b


def solution(mesh):
    placed = (
        P(("fsdp", "ad"), None),
        P("fsdp", "tp"),
        P("ad", None, "tp"),
        P("ad", None, "tp"),
        P(("fsdp", "ad"), "tp"),
        P(("fsdp", "ad"), None),
    )
    square = mesh.shape["fsdp"] == 4 and mesh.shape["tp"] == 2 and mesh.shape["ad"] == 4
    return jax.shard_map(
        column_body if square else general_body,
        mesh=mesh,
        in_specs=placed,
        out_specs=(P(("fsdp", "ad"), "tp"), P("ad", "fsdp", "tp"), P("ad", "fsdp", "tp")),
        check_vma=False,
    )
```
